32 devices in a mesh: dp: 4 (over z), seq: 8 (over y, x, core).
Axes of the slice: x: 2, y: 2, z: 4, core: 2. Of those that a mesh axis runs over, the one named last changes fastest.
Arguments:
- tokens: bfloat16 [4096, 2048], P(('dp', 'seq')), may hold values from -6 to 6
- cotangent: bfloat16 [4096, 2048], P(('dp', 'seq')), may hold values from -6 to 6
- lengths: int32 [8], P('dp'), may hold values from 16 to 1008, as said below
- lower_bound: float32 [2048], replicated, may hold values from 0.5 to 1
- mixer_w: float32 [2048, 4, 2048], P(('dp', 'seq')), may hold values from -0.125 to 0.125
- mlp_in: float32 [2048, 2, 5632], P(('dp', 'seq')), may hold values from -0.125 to 0.125
- mlp_down: float32 [5632, 2048], P(('dp', 'seq')), may hold values from -0.078125 to 0.078125
- gains: float32 [3, 2048], P(None, ('dp', 'seq')), may hold values from 0.3 to 2.5
- mixer_m: float32 [2048, 4, 2048], P(('dp', 'seq')), may hold values from -9.1552734e-05 to 9.1552734e-05
- mixer_v: float32 [2048, 4, 2048], P(('dp', 'seq')), may hold values from 1.9460414e-11 to 7.784166e-11
- in_m: float32 [2048, 2, 5632], P(('dp', 'seq')), may hold values from -9.1552734e-05 to 9.1552734e-05
- in_v: float32 [2048, 2, 5632], P(('dp', 'seq')), may hold values from 1.9460414e-11 to 7.784166e-11
- down_m: float32 [5632, 2048], P(('dp', 'seq')), may hold values from -9.1552734e-05 to 9.1552734e-05
- down_v: float32 [5632, 2048], P(('dp', 'seq')), may hold values from 1.9460414e-11 to 7.784166e-11
- gain_m: float32 [3, 2048], P(None, ('dp', 'seq')), may hold values from -0.00036621094 to 0.00036621094
- gain_v: float32 [3, 2048], P(None, ('dp', 'seq')), may hold values from 3.1136663e-10 to 1.2454665e-09
Outputs:
- block_out: bfloat16 [4096, 2048], P(('dp', 'seq'))
- input_grad: float32 [4096, 2048], P(('dp', 'seq'))
- grad_norm: float32 [], replicated
- new_mixer: float32 [2048, 4, 2048], P(('dp', 'seq'))
- new_mixer_m: float32 [2048, 4, 2048], P(('dp', 'seq'))
- new_mixer_v: float32 [2048, 4, 2048], P(('dp', 'seq'))
- new_in: float32 [2048, 2, 5632], P(('dp', 'seq'))
- new_in_m: float32 [2048, 2, 5632], P(('dp', 'seq'))
- new_in_v: float32 [2048, 2, 5632], P(('dp', 'seq'))
- new_down: float32 [5632, 2048], P(('dp', 'seq'))
- new_down_m: float32 [5632, 2048], P(('dp', 'seq'))
- new_down_v: float32 [5632, 2048], P(('dp', 'seq'))
- new_gains: float32 [3, 2048], P(None, ('dp', 'seq'))
- new_gain_m: float32 [3, 2048], P(None, ('dp', 'seq'))
- new_gain_v: float32 [3, 2048], P(None, ('dp', 'seq'))
The draws below stay inside these ranges and needn't reach their ends.
Inputs may be any that keep to these rules, and one draw needn't show every extreme that they name: Positions beyond the sum of a group's lengths are padding at the group's end, fewer than 128 of them; one sequence of each group starts on the group's first device and ends on its last.
All inputs are finite; a program needn't handle non-finite values.
Results may differ from the reference program's by a relative error of at most 0.0098.
Values may be sent and summed in bfloat16 or wider, within the bound.
No kernel may reach another device: no remote copies, remote signals or barrier semaphores. Data moves between devices by JAX's collectives and lax.ppermute only.
A program may use at most 640 MiB of HBM per device.

```python
import math
import jax
import jax.numpy as jnp
from jax import lax

D = 2048
FF = 5632
TOK_DEV = 128
SEQS = 2
STEP = 10
TOKENS = 4096
PARAMS = 51386368
N_DP = 4
N_SEQ = 8


def draw_lengths(key, part):
    key = jax.random.fold_in(key, 1)
    key_short, key_pad, key_order = jax.random.split(key, 3)
    group_len = TOK_DEV * N_SEQ
    short = jax.random.randint(key_short, (N_DP,), TOK_DEV // 8, TOK_DEV // 2 + 1)
    padding = jax.random.randint(key_pad, (N_DP,), 0, TOK_DEV // 2)
    short = short.at[0].set(TOK_DEV // 8)
    padding = padding.at[0].set(0)
    longest = group_len - short - padding
    order = jax.random.randint(key_order, (N_DP,), 0, 2)
    first = jnp.where(order == 1, longest, short)
    second = jnp.where(order == 1, short, longest)
    return jnp.stack([first, second], axis=1).reshape(-1).astype(jnp.int32)


def draw_lower_bound(key, part):
    key = jax.random.fold_in(key, 2)
    key_level, key_kind = jax.random.split(key, 2)
    group_len = TOK_DEV * N_SEQ
    level = jax.random.uniform(key_level, (D,), jnp.float32)
    slow_share = 0.5
    slow = jax.random.uniform(key_kind, (D,), jnp.float32) < slow_share
    slow_gap = jnp.exp(jnp.log(0.1 / group_len) + level * jnp.log(4.0))
    fast_gap = jnp.exp(jnp.log(0.02) + level * jnp.log(4.0))
    return (1.0 - jnp.where(slow, slow_gap, fast_gap)).astype(jnp.float32)


def draw_gains(key, part):
    key = jax.random.fold_in(key, 3)
    along = jnp.arange(D, dtype=jnp.float32) / (D - 1)
    base = 0.6 * (1.0 + 2.0 * along)
    noise = jax.random.uniform(key, (3, D), jnp.float32, 0.8, 1.2)
    return (base[None, :] * noise).astype(jnp.float32)


def block_levels(rng, extent, cuts, least, largest):
    loudness, own = 1.0, jax.random.fold_in(rng, 6)
    for dim, blocks in cuts:
        draws = jnp.exp(jax.random.uniform(jax.random.fold_in(own, dim), (blocks,), jnp.float32, least / len(cuts), largest / len(cuts)))
        loudness = loudness * jnp.repeat(draws, extent[dim] // blocks).reshape([-1 if axis == dim else 1 for axis in range(len(extent))])
    return loudness


def bell_draw(own_key, shape, width, limit, cuts=(), held_as=jnp.bfloat16):
    entries = jax.random.normal(own_key, shape, jnp.float32) * width
    if len(cuts) > 0:
        entries = block_levels(own_key, shape, cuts, -0.22, 0.18) * entries
    return jnp.clip(entries, min=-limit, max=limit).astype(held_as)


def setup_inputs(seed: int = 0) -> dict:
    arg_keys = jax.random.split(jax.random.key(seed), 17)
    return {
        "tokens": bell_draw(arg_keys[0], (TOKENS, D), 1.0, 6.0, ((0, 32),)),
        "cotangent": bell_draw(arg_keys[1], (TOKENS, D), 1.0, 6.0, ((0, 32),)),
        "lengths": draw_lengths(jax.random.fold_in(arg_keys[16], 71), 0),
        "lower_bound": draw_lower_bound(jax.random.fold_in(arg_keys[16], 71), 0),
        "mixer_w": bell_draw(arg_keys[4], (D, 4, D), D ** -0.5, 0.125, ((0, 32),), jnp.float32),
        "mlp_in": bell_draw(arg_keys[5], (D, 2, FF), D ** -0.5, 0.125, ((0, 32),), jnp.float32),
        "mlp_down": bell_draw(arg_keys[6], (FF, D), FF ** -0.5, 0.078125, ((0, 32),), jnp.float32),
        "gains": draw_gains(jax.random.fold_in(arg_keys[16], 71), 0),
        "mixer_m": bell_draw(arg_keys[8], (D, 4, D), (0.11 * PARAMS ** -0.5), 9.1552734375e-05, ((0, 32),), jnp.float32),
        "mixer_v": jnp.clip(jnp.exp(math.log(7.784165673152543e-11) - 1.3862944 * jax.random.uniform(arg_keys[9], (D, 4, D), jnp.float32) ** block_levels(arg_keys[9], (D, 4, D), ((0, 32),), -0.2, 0.2)), 1.9460414182881358e-11, 7.784165673152543e-11),
        "in_m": bell_draw(arg_keys[10], (D, 2, FF), (0.11 * PARAMS ** -0.5), 9.1552734375e-05, ((0, 32),), jnp.float32),
        "in_v": jnp.clip(jnp.exp(math.log(7.784165673152543e-11) - 1.3862944 * jax.random.uniform(arg_keys[11], (D, 2, FF), jnp.float32) ** block_levels(arg_keys[11], (D, 2, FF), ((0, 32),), -0.2, 0.2)), 1.9460414182881358e-11, 7.784165673152543e-11),
        "down_m": bell_draw(arg_keys[12], (FF, D), (0.11 * PARAMS ** -0.5), 9.1552734375e-05, ((0, 32),), jnp.float32),
        "down_v": jnp.clip(jnp.exp(math.log(7.784165673152543e-11) - 1.3862944 * jax.random.uniform(arg_keys[13], (FF, D), jnp.float32) ** block_levels(arg_keys[13], (FF, D), ((0, 32),), -0.2, 0.2)), 1.9460414182881358e-11, 7.784165673152543e-11),
        "gain_m": bell_draw(arg_keys[14], (3, D), (0.44 * PARAMS ** -0.5), 0.00036621094, ((1, 32),), jnp.float32),
        "gain_v": jnp.clip(jnp.exp(math.log(1.245466507704407e-09) - 1.3862944 * jax.random.uniform(arg_keys[15], (3, D), jnp.float32) ** block_levels(arg_keys[15], (3, D), ((1, 32),), -0.2, 0.2)), 3.1136662692610173e-10, 1.245466507704407e-09),
    }


EPS_NORM = 1e-06
BETA_ONE = 0.9
BETA_TWO = 0.999
ADAM_EPS = 1e-08
RATE_MATRIX = 0.03
RATE_GAIN = 0.5
DECAY_WEIGHT = 0.1
CLIP_NORM = 1.0

@jax.custom_vjp
def low(v):
    return lax.optimization_barrier(v.astype(jnp.bfloat16)).astype(jnp.float32)

@jax.custom_vjp
def low_back(v):
    return v

def low_keep(v):
    return (low(v), None)

def low_pass(kept, grad):
    return (grad,)

def back_keep(v):
    return (v, None)

def back_low(kept, grad):
    return (low(grad),)
low.defvjp(low_keep, low_pass)
low_back.defvjp(back_keep, back_low)

def combine_pairs(earlier, later):
    return (earlier[0] * later[0], later[0] * earlier[1] + later[1])

def normalize(v):
    return v * lax.rsqrt(lax.optimization_barrier(jnp.mean(v * v, axis=-1, keepdims=True)) + EPS_NORM)

def silu(v):
    return v * jax.nn.sigmoid(v)

def layout(lengths):
    places = jnp.arange(TOK_DEV * N_SEQ, dtype=jnp.int32)
    per_group = lengths.reshape(N_DP, SEQS).astype(jnp.int32)
    ends = jnp.cumsum(per_group, axis=1).astype(jnp.int32)
    starts = ends - per_group
    is_start = jnp.any(places[None, :, None] == starts[:, None, :], axis=-1).reshape(-1)
    valid = (places[None, :] < ends[:, -1:]).reshape(-1)
    return (is_start, valid)

def forward(x, mixer_w, mlp_in, mlp_down, gains, lower_bound, is_start):
    highest = lax.Precision.HIGHEST
    w_mix = low(mixer_w)
    w_in = low(mlp_in)
    w_down = low(mlp_down)
    n1 = low(normalize(x) * gains[0])
    proj = low_back(jnp.einsum('td,dkc->tkc', n1, w_mix[:, :3, :], precision=highest))
    in_proj = proj[:, 0, :]
    forget_proj = proj[:, 1, :]
    gate_proj = proj[:, 2, :]
    keep = (1.0 - lower_bound) * jax.nn.sigmoid(-forget_proj)
    decay = jnp.where(is_start[:, None], jnp.zeros_like(keep), 1.0 - keep)
    inputs = silu(in_proj) * keep
    shaped = (decay.reshape(N_DP, -1, D), inputs.reshape(N_DP, -1, D))
    state = lax.associative_scan(combine_pairs, shaped, axis=1)[1].reshape(-1, D)
    mixed_in = low(normalize(state) * gains[1] * silu(gate_proj))
    mix = low_back(jnp.dot(mixed_in, w_mix[:, 3, :], precision=highest))
    after_mix = x + mix
    n2 = low(normalize(after_mix) * gains[2])
    gate_up = low_back(jnp.einsum('td,dkf->tkf', n2, w_in, precision=highest))
    hidden = low(silu(gate_up[:, 0, :]) * gate_up[:, 1, :])
    down = low_back(jnp.dot(hidden, w_down, precision=highest))
    return after_mix + down

def adam_step(weight, first, second, grad, rate, decay_w):
    first_new = BETA_ONE * first + (1.0 - BETA_ONE) * grad
    second_new = BETA_TWO * second + (1.0 - BETA_TWO) * grad * grad
    step_size = first_new / (1.0 - BETA_ONE ** STEP) / (jnp.sqrt(second_new / (1.0 - BETA_TWO ** STEP)) + ADAM_EPS)
    return (weight - rate * (step_size + decay_w * weight), first_new, second_new)

def reference(tokens, cotangent, lengths, lower_bound, mixer_w, mlp_in, mlp_down, gains, mixer_m, mixer_v, in_m, in_v, down_m, down_v, gain_m, gain_v):
    is_start, valid = layout(lengths)

    def run(x, w_mix, w_in, w_down, gain_rows):
        return forward(x, w_mix, w_in, w_down, gain_rows, lower_bound, is_start)
    primal, pull = jax.vjp(run, tokens.astype(jnp.float32), mixer_w, mlp_in, mlp_down, gains)
    cot = cotangent.astype(jnp.float32) * valid[:, None].astype(jnp.float32)
    input_grad, grad_mixer, grad_in, grad_down, grad_gains = pull(cot)
    total = jnp.sum(grad_mixer * grad_mixer) + jnp.sum(grad_in * grad_in) + jnp.sum(grad_down * grad_down) + jnp.sum(grad_gains * grad_gains)
    grad_norm = jnp.sqrt(total)
    clip = jnp.minimum(1.0, CLIP_NORM / (grad_norm + 1e-06))
    new_mixer, new_mixer_m, new_mixer_v = adam_step(mixer_w, mixer_m, mixer_v, clip * grad_mixer, RATE_MATRIX, DECAY_WEIGHT)
    new_in, new_in_m, new_in_v = adam_step(mlp_in, in_m, in_v, clip * grad_in, RATE_MATRIX, DECAY_WEIGHT)
    new_down, new_down_m, new_down_v = adam_step(mlp_down, down_m, down_v, clip * grad_down, RATE_MATRIX, DECAY_WEIGHT)
    new_gains, new_gain_m, new_gain_v = adam_step(gains, gain_m, gain_v, clip * grad_gains, RATE_GAIN, 0.0)
    return (primal.astype(jnp.bfloat16), input_grad, grad_norm, new_mixer, new_mixer_m, new_mixer_v, new_in, new_in_m, new_in_v, new_down, new_down_m, new_down_v, new_gains, new_gain_m, new_gain_v)
```

```python
import functools
import math

import jax
import jax.numpy as jnp
from jax import lax
from jax.experimental import pallas as pl
from jax.experimental.pallas import tpu as pltpu
from jax.sharding import Mesh, PartitionSpec as P

STEP = 10


EPS_NORM = 1e-06
BETA_ONE = 0.9
BETA_TWO = 0.999
ADAM_EPS = 1e-08
RATE_MATRIX = 0.03
RATE_GAIN = 0.5
DECAY_WEIGHT = 0.1
CLIP_NORM = 1.0

ALL = ("z", "y", "x", "c")
PLANE = ("y", "x", "c")
LINE = ("z", "c")
QUAD = ("y", "x")
TILE = 8
BF = jnp.bfloat16
F32 = jnp.float32


def gather(value, axes):
    return lax.all_gather(value, axes, axis=0, tiled=True)


def scatter(value, axes):
    return lax.psum_scatter(value, axes, scatter_dimension=0, tiled=True)


def exchange(value, axes):
    return lax.all_to_all(value, axes, 0, 0, tiled=True)


def total_of(value):
    for axis in ("c", "x", "y", "z"):
        count = lax.axis_size(axis)
        hop = 1
        while hop < count:
            value = value + lax.ppermute(value, axis, [(i, i ^ hop) for i in range(count)])
            hop *= 2
    return value


def normalize(value):
    factor = lax.rsqrt(jnp.mean(value * value, axis=-1, keepdims=True) + EPS_NORM)
    return (value * factor, factor)


def norm_back(grad_normed, normed, factor):
    return factor * (grad_normed - normed * jnp.mean(grad_normed * normed, axis=-1, keepdims=True))


def silu(value):
    return value * jax.nn.sigmoid(value)


def silu_grad(value):
    sig = jax.nn.sigmoid(value)
    return sig * (1.0 + value * (1.0 - sig))


def adam_step(weight, first, second, grad, rate, decay_w):
    first_new = BETA_ONE * first + (1.0 - BETA_ONE) * grad
    second_new = BETA_TWO * second + (1.0 - BETA_TWO) * grad * grad
    step_size = (
        first_new
        / (1.0 - BETA_ONE**STEP)
        / (jnp.sqrt(second_new / (1.0 - BETA_TWO**STEP)) + ADAM_EPS)
    )
    return (weight - rate * (step_size + decay_w * weight), first_new, second_new)


def shifted(value, hop, fill, row, later):
    size = value.shape[0]
    moved = pltpu.roll(value, size - hop if later else hop, 0)
    inside = row < size - hop if later else row >= hop
    return jnp.where(inside, moved, fill)


def tile_scan(coeff, value, row, later):
    hop = 1
    while hop < value.shape[0]:
        value = coeff * shifted(value, hop, 0.0, row, later) + value
        coeff = coeff * shifted(coeff, hop, 1.0, row, later)
        hop *= 2
    return coeff, value


def gates(forget_proj, gap, started):
    sig_neg = jax.nn.sigmoid(-forget_proj)
    keep = gap * sig_neg
    return sig_neg, keep, jnp.where(started > 0.0, 0.0, 1.0 - keep)


def scan_forward(proj_ref, started_ref, gap_ref, state_ref):
    rows, width = state_ref.shape
    row = lax.broadcasted_iota(jnp.int32, (TILE, width), 0)
    gap = gap_ref[...]

    def step(index, carry):
        place = pl.ds(pl.multiple_of(index * TILE, TILE), TILE)
        in_proj = proj_ref[place, pl.ds(0, width)]
        forget_proj = proj_ref[place, pl.ds(width, width)]
        _, keep, decay = gates(forget_proj, gap, started_ref[place, :])
        coeff, value = tile_scan(decay, silu(in_proj) * keep, row, False)
        state = value + coeff * carry
        state_ref[place, :] = state
        return state[TILE - 1 :, :]

    lax.fori_loop(0, rows // TILE, step, jnp.zeros((1, width), F32), unroll=4)


def scan_backward(proj_ref, state_ref, d_state_ref, started_ref, gap_ref, d_in_ref, d_forget_ref):
    rows, width = state_ref.shape
    row = lax.broadcasted_iota(jnp.int32, (TILE, width), 0)
    gap = gap_ref[...]
    tiles = rows // TILE

    def step(count, carry):
        index = tiles - 1 - count
        place = pl.ds(pl.multiple_of(index * TILE, TILE), TILE)
        before = pl.ds(pl.multiple_of(jnp.maximum(index - 1, 0) * TILE, TILE), TILE)
        in_proj = proj_ref[place, pl.ds(0, width)]
        forget_proj = proj_ref[place, pl.ds(width, width)]
        started = started_ref[place, :]
        sig_neg, keep, decay = gates(forget_proj, gap, started)
        d_state = d_state_ref[place, :]
        coeff, value = tile_scan(decay, decay * d_state, row, True)
        passed = value + coeff * carry
        moved = jnp.where(row < TILE - 1, pltpu.roll(passed, TILE - 1, 0), carry)
        d_total = d_state + moved
        last = state_ref[before, :][TILE - 1 :, :]
        previous = jnp.where(row >= 1, pltpu.roll(state_ref[place, :], 1, 0), last)
        previous = jnp.where(started > 0.0, 0.0, previous)
        sig = jax.nn.sigmoid(in_proj)
        d_in_ref[place, :] = d_total * keep * (sig * (1.0 + in_proj * (1.0 - sig)))
        d_keep = d_total * (in_proj * sig) - d_total * previous
        d_forget_ref[place, :] = -d_keep * gap * sig_neg * (1.0 - sig_neg)
        return passed[:1, :]

    lax.fori_loop(0, tiles, step, jnp.zeros((1, width), F32), unroll=4)


def run_forward(proj, started, gap):
    rows, width = proj.shape[0], gap.shape[1]
    return pl.pallas_call(
        scan_forward,
        out_shape=jax.ShapeDtypeStruct((rows, width), F32),
        compiler_params=pltpu.CompilerParams(vmem_limit_bytes=48 * 2**20),
    )(proj, started, gap)


def run_backward(proj, state, d_state, started, gap):
    rows, width = state.shape
    return pl.pallas_call(
        scan_backward,
        out_shape=[jax.ShapeDtypeStruct((rows, width), F32)] * 2,
        compiler_params=pltpu.CompilerParams(vmem_limit_bytes=48 * 2**20),
    )(proj, state, d_state, started, gap)


def shards(
    tokens,
    cotangent,
    lengths,
    lower_bound,
    mixer_w,
    mlp_in,
    mlp_down,
    gains,
    mixer_m,
    mixer_v,
    in_m,
    in_v,
    down_m,
    down_v,
    gain_m,
    gain_v,
):
    rows, width = tokens.shape
    own, _, hidden_width = mlp_in.shape
    down_rows = mlp_down.shape[0]
    planes = lax.axis_size("z")
    spots = lax.axis_size(PLANE)
    quads = lax.axis_size(QUAD)
    pairs = lax.axis_size("c")
    group = spots * rows
    spot = lax.axis_index(PLANE)
    chans = planes * own

    low_mixer = mixer_w.astype(BF)
    sent = low_mixer[:, :3, :].reshape(own, 3, planes, spots, own).transpose(3, 0, 1, 2, 4)
    part = exchange(sent.reshape(spots, own, 3 * chans), PLANE)
    w_proj = gather(part.reshape(spots * own, 3 * chans), "z")
    w_out = gather(low_mixer[:, 3, :], "z")
    low_in = mlp_in.astype(BF)
    sent = low_in.reshape(own, 2, planes, quads, pairs, down_rows).transpose(2, 4, 0, 1, 3, 5)
    inner = quads * down_rows
    part = exchange(sent.reshape(planes * pairs, own, 2 * inner), LINE)
    w_in = gather(part.reshape(planes * pairs * own, 2 * inner), QUAD)
    w_down = gather(mlp_down.astype(BF), QUAD)

    full_gains = gather(gather(gains.T, PLANE), "z").T
    bound = lower_bound.reshape(planes, spots, own)
    gap = (1.0 - lax.dynamic_index_in_dim(bound, spot, 1, False)).reshape(1, chans)
    gain_mid = full_gains[1].reshape(planes, spots, own)
    gain_mid = lax.dynamic_index_in_dim(gain_mid, spot, 1, False).reshape(1, chans)

    ends = jnp.cumsum(lengths)
    starts = ends - lengths
    places = jnp.arange(group, dtype=jnp.int32)
    started = jnp.any(places[:, None] == starts[None, :], axis=-1, keepdims=True).astype(F32)
    home = spot * rows + jnp.arange(rows, dtype=jnp.int32)
    valid = (home < ends[-1]).astype(F32)

    def swapped(value, first, second):
        return value.reshape(rows, first, second, -1).swapaxes(1, 2).reshape(rows, width)

    x = tokens.astype(F32)
    x_normed, x_factor = normalize(x)
    n1 = gather((x_normed * full_gains[0]).astype(BF), PLANE)
    cot = cotangent.astype(F32) * valid[:, None]
    cot_all = gather(cot.astype(BF), LINE)
    proj = jnp.dot(n1, w_proj, preferred_element_type=F32)
    state = run_forward(proj[:, : 2 * chans], started, gap)
    gate_proj = proj[:, 2 * chans :]
    gate_act = silu(gate_proj)
    raw = (state * gain_mid * gate_act).astype(BF)
    squares = lax.psum(jnp.sum(state * state, axis=-1), PLANE)
    state_factor = lax.rsqrt(squares / width + EPS_NORM)
    mix_raw = scatter(jnp.dot(raw, w_out, preferred_element_type=F32).astype(BF), PLANE)
    home_factor = lax.dynamic_slice_in_dim(state_factor, spot * rows, rows)
    mix = mix_raw.astype(F32) * home_factor[:, None]
    after_mix = x + mix

    mid_normed, mid_factor = normalize(after_mix)
    n2 = gather(swapped((mid_normed * full_gains[2]).astype(BF), planes, quads), LINE)
    gate_up = jnp.dot(n2, w_in, preferred_element_type=F32)
    gate, up_value = gate_up[:, :inner], gate_up[:, inner:]
    silu_gate = silu(gate)
    hidden = (silu_gate * up_value).astype(BF)
    down = scatter(jnp.dot(hidden, w_down, preferred_element_type=F32).astype(BF), LINE)
    block_out = (after_mix + down.astype(F32)).astype(BF)

    grad_down = lax.dot_general(hidden, cot_all, (((0,), (0,)), ((), ())), preferred_element_type=F32)
    shard_down = scatter(grad_down.astype(BF), QUAD).astype(F32)
    d_hidden = lax.dot_general(cot_all, w_down, (((1,), (1,)), ((), ())), preferred_element_type=F32)
    d_gate = d_hidden * up_value * silu_grad(gate)
    d_up = d_hidden * silu_gate
    d_gate_up = jnp.concatenate([d_gate.astype(BF), d_up.astype(BF)], axis=1)
    d_n2 = lax.dot_general(d_gate_up, w_in, (((1,), (1,)), ((), ())), preferred_element_type=F32)
    d_n2 = swapped(scatter(d_n2.astype(BF), LINE), quads, planes).astype(F32)
    grad_in = lax.dot_general(n2, d_gate_up, (((0,), (0,)), ((), ())), preferred_element_type=F32)
    shard_in = scatter(grad_in.astype(BF), QUAD)
    shard_in = exchange(shard_in.reshape(planes * pairs, own, 2 * inner), LINE)
    shard_in = shard_in.reshape(planes, pairs, own, 2, quads, down_rows).transpose(2, 3, 0, 4, 1, 5)
    shard_in = shard_in.reshape(own, 2, hidden_width).astype(F32)
    d_mid = cot + norm_back(d_n2 * full_gains[2], mid_normed, mid_factor)

    d_mix_home = d_mid.astype(BF)
    d_mix = gather(d_mix_home, PLANE)
    mean = gather(jnp.sum(d_mix_home.astype(F32) * mix, axis=-1) / width, PLANE)
    d_mixed = lax.dot_general(d_mix, w_out, (((1,), (1,)), ((), ())), preferred_element_type=F32)
    factor = state_factor[:, None]
    state_normed = state * factor
    mixed_in = (state_normed * gain_mid * gate_act).astype(BF)
    grad_out = lax.dot_general(mixed_in, d_mix, (((0,), (0,)), ((), ())), preferred_element_type=F32)
    shard_out = scatter(grad_out.astype(BF), "z").astype(F32)
    d_gate_proj = d_mixed * state_normed * gain_mid * silu_grad(gate_proj)
    d_state = factor * (d_mixed * gain_mid * gate_act - state_normed * mean[:, None])
    d_in_proj, d_forget_proj = run_backward(proj[:, : 2 * chans], state, d_state, started, gap)
    d_proj = jnp.concatenate(
        [d_in_proj.astype(BF), d_forget_proj.astype(BF), d_gate_proj.astype(BF)], axis=1
    )
    grad_proj = lax.dot_general(n1, d_proj, (((0,), (0,)), ((), ())), preferred_element_type=F32)
    shard_proj = scatter(grad_proj.astype(BF), "z")
    shard_proj = exchange(shard_proj.reshape(spots, own, 3 * chans), PLANE)
    shard_proj = shard_proj.reshape(spots, own, 3, planes, own).transpose(1, 2, 3, 0, 4)
    shard_proj = shard_proj.reshape(own, 3, width).astype(F32)
    d_n1 = lax.dot_general(d_proj, w_proj, (((1,), (1,)), ((), ())), preferred_element_type=F32)
    d_n1 = scatter(d_n1.astype(BF), PLANE).astype(F32)
    input_grad = d_mid + norm_back(d_n1 * full_gains[0], x_normed, x_factor)

    low_rows = low_mixer.astype(F32)
    shard_gains = jnp.stack(
        [
            jnp.sum(shard_proj * low_rows[:, :3, :], axis=(1, 2)),
            jnp.sum(shard_out * low_rows[:, 3, :], axis=1),
            jnp.sum(shard_in * low_in.astype(F32), axis=(1, 2)),
        ],
        axis=0,
    ) / gains
    shard_mixer = jnp.concatenate([shard_proj, shard_out[:, None, :]], axis=1)

    local_total = (
        jnp.sum(shard_mixer * shard_mixer)
        + jnp.sum(shard_in * shard_in)
        + jnp.sum(shard_down * shard_down)
        + jnp.sum(shard_gains * shard_gains)
    )
    grad_norm = jnp.sqrt(total_of(local_total.reshape(1, 1))[0, 0])
    clip = jnp.minimum(1.0, CLIP_NORM / (grad_norm + 1e-06))
    new_mixer, new_mixer_m, new_mixer_v = adam_step(
        mixer_w, mixer_m, mixer_v, clip * shard_mixer, RATE_MATRIX, DECAY_WEIGHT
    )
    new_in, new_in_m, new_in_v = adam_step(
        mlp_in, in_m, in_v, clip * shard_in, RATE_MATRIX, DECAY_WEIGHT
    )
    new_down, new_down_m, new_down_v = adam_step(
        mlp_down, down_m, down_v, clip * shard_down, RATE_MATRIX, DECAY_WEIGHT
    )
    new_gains, new_gain_m, new_gain_v = adam_step(
        gains, gain_m, gain_v, clip * shard_gains, RATE_GAIN, 0.0
    )
    return (
        block_out,
        input_grad,
        grad_norm,
        new_mixer,
        new_mixer_m,
        new_mixer_v,
        new_in,
        new_in_m,
        new_in_v,
        new_down,
        new_down_m,
        new_down_v,
        new_gains,
        new_gain_m,
        new_gain_v,
    )


def solution(mesh):
    planes, spots = mesh.shape["dp"], mesh.shape["seq"]
    side = math.isqrt(spots // 2)
    split = Mesh(mesh.devices.reshape(planes, spots // (2 * side), side, 2), ALL)
    rows2, rows3, cols = P(ALL, None), P(ALL, None, None), P(None, ALL)
    return jax.shard_map(
        shards,
        mesh=split,
        in_specs=(rows2, rows2, P("z"), P(), rows3, rows3, rows2, cols)
        + (rows3,) * 4
        + (rows2,) * 2
        + (cols,) * 2,
        out_specs=(rows2, rows2, P()) + (rows3,) * 6 + (rows2,) * 3 + (cols,) * 3,
        check_vma=False,
    )
```

```python
import functools
import math

import jax
import jax.numpy as jnp
from jax import lax
from jax.experimental import pallas as pl
from jax.experimental.layout import Layout, with_layout_constraint
from jax.experimental.pallas import tpu as pltpu
from jax.sharding import Mesh, PartitionSpec as P

STEP = 10


EPS_NORM = 1e-06
BETA_ONE = 0.9
BETA_TWO = 0.999
ADAM_EPS = 1e-08
RATE_MATRIX = 0.03
RATE_GAIN = 0.5
DECAY_WEIGHT = 0.1
CLIP_NORM = 1.0

ALL = ("z", "y", "x", "c")
PLANE = ("y", "x", "c")
LINE = ("z", "c")
QUAD = ("y", "x")
TILE = 8
BF = jnp.bfloat16
F32 = jnp.float32


def gather(value, axes):
    return lax.all_gather(value, axes, axis=0, tiled=True)


def scatter(value, axes):
    return lax.psum_scatter(value, axes, scatter_dimension=0, tiled=True)


def exchange(value, axes):
    return lax.all_to_all(value, axes, 0, 0, tiled=True)


def ring_gather(value, axis):
    count, mine = lax.axis_size(axis), lax.axis_index(axis)
    if count == 2:
        other = lax.ppermute(value, axis, [(0, 1), (1, 0)])
        return jnp.stack([jnp.where(mine == 0, value, other), jnp.where(mine == 0, other, value)])
    up, down, ups, downs = value, value, [], []
    for hop in range(1, count):
        up = lax.ppermute(up, axis, [(i, i + 1) for i in range(hop - 1, count - 1)])
        down = lax.ppermute(down, axis, [(i, i - 1) for i in range(1, count - hop + 1)])
        ups.append(up)
        downs.append(down)
    places = []
    for place in range(count):
        found = value
        for back in range(1, count):
            if place + back < count:
                found = jnp.where(mine == place + back, ups[back - 1], found)
            if place >= back:
                found = jnp.where(mine == place - back, downs[back - 1], found)
        places.append(found)
    return jnp.stack(places)


def ring_scatter(value, axis):
    count, mine = lax.axis_size(axis), lax.axis_index(axis)

    def block(back):
        return lax.dynamic_index_in_dim(value, (mine - back) % count, 0, False)

    if count == 2:
        return block(0).astype(F32) + lax.ppermute(block(1), axis, [(0, 1), (1, 0)]).astype(F32)
    up = down = None
    for hop in range(1, count):
        up_sum, down_sum = block(hop), block(count - hop)
        if up is not None:
            up_sum = (up_sum.astype(F32) + up.astype(F32)).astype(BF)
            down_sum = (down_sum.astype(F32) + down.astype(F32)).astype(BF)
        up = lax.ppermute(up_sum, axis, [(i, i + 1) for i in range(hop)])
        down = lax.ppermute(down_sum, axis, [(i, i - 1) for i in range(count - hop, count)])
    return block(0).astype(F32) + up.astype(F32) + down.astype(F32)


def double_gather(value):
    value = value[None]
    for axis in ("c", "x", "y", "z"):
        count, mine = lax.axis_size(axis), lax.axis_index(axis)
        hop = 1
        while hop < count:
            other = lax.ppermute(value, axis, [(i, i ^ hop) for i in range(count)])
            low = (mine // hop) % 2 == 0
            value = jnp.concatenate([jnp.where(low, value, other), jnp.where(low, other, value)])
            hop *= 2
    return value


def tied(*values):
    return lax.optimization_barrier(values)


def in_parts_of(value):
    upper = value.astype(BF)
    rest = value - upper.astype(F32)
    middle = rest.astype(BF)
    lower = (rest - middle.astype(F32)).astype(BF)
    return [upper[:, None], middle[:, None], lower[:, None]]


def as_stored(value):
    return with_layout_constraint(value, Layout(tuple(range(value.ndim))))


def direct_scatter(value, axis):
    count, mine = lax.axis_size(axis), lax.axis_index(axis)
    total = lax.dynamic_index_in_dim(value, mine, 0, False).astype(F32)
    for back in range(1, count):
        block = lax.dynamic_index_in_dim(value, (mine - back) % count, 0, False)
        total += lax.ppermute(block, axis, [(i, (i - back) % count) for i in range(count)])
    return total


def quad_parts(value, axis):
    half = value.shape[axis] // 2
    first = ring_gather(ring_gather(lax.slice_in_dim(value, 0, half, axis=axis), "x"), "y")
    second = lax.slice_in_dim(value, half, 2 * half, axis=axis)
    second = ring_gather(ring_gather(second, "y"), "x").swapaxes(0, 1)
    return [first, second]


def quad_whole(parts):
    return jnp.concatenate(parts, axis=2).reshape(-1, parts[0].shape[-1])


def quad_sums(value):
    value = value.reshape(lax.axis_size("y"), lax.axis_size("x"), -1, value.shape[1])
    half = value.shape[2] // 2
    first = ring_scatter(value[:, :, :half], "y").astype(BF)
    return first, ring_scatter(value[:, :, half:].swapaxes(0, 1), "x").astype(BF)


def quad_rest(first, second):
    return jnp.concatenate([ring_scatter(first, "x"), ring_scatter(second, "y")], axis=0)


def core_gather(parts):
    both = ring_gather(jnp.concatenate(parts, axis=3), "c")
    return jnp.moveaxis(both, 0, 2).reshape(-1, both.shape[-1])


def line_gather(value):
    both = ring_gather(ring_gather(value, "z"), "c")
    return both.swapaxes(0, 1).reshape(-1, value.shape[1])


def line_scatter(value):
    value = value.reshape(lax.axis_size("z"), 2, -1, value.shape[1]).swapaxes(0, 1)
    return direct_scatter(ring_scatter(value, "c").astype(BF), "z")


def total_of(value):
    for axis in ("c", "x", "y", "z"):
        count = lax.axis_size(axis)
        hop = 1
        while hop < count:
            value = value + lax.ppermute(value, axis, [(i, i ^ hop) for i in range(count)])
            hop *= 2
    return value


def normalize(value):
    factor = lax.rsqrt(jnp.mean(value * value, axis=-1, keepdims=True) + EPS_NORM)
    return (value * factor, factor)


def norm_back(grad_normed, normed, factor):
    return factor * (grad_normed - normed * jnp.mean(grad_normed * normed, axis=-1, keepdims=True))


def silu(value):
    return value * jax.nn.sigmoid(value)


def silu_grad(value):
    sig = jax.nn.sigmoid(value)
    return sig * (1.0 + value * (1.0 - sig))


def adam_step(weight, first, second, grad, rate, decay_w):
    first_new = BETA_ONE * first + (1.0 - BETA_ONE) * grad
    second_new = BETA_TWO * second + (1.0 - BETA_TWO) * grad * grad
    step_size = (
        first_new
        / (1.0 - BETA_ONE**STEP)
        / (jnp.sqrt(second_new / (1.0 - BETA_TWO**STEP)) + ADAM_EPS)
    )
    return (weight - rate * (step_size + decay_w * weight), first_new, second_new)


def shifted(value, hop, fill, row, later):
    size = value.shape[0]
    moved = pltpu.roll(value, size - hop if later else hop, 0)
    inside = row < size - hop if later else row >= hop
    return jnp.where(inside, moved, fill)


def tile_scan(coeff, value, row, later):
    hop = 1
    while hop < value.shape[0]:
        value = coeff * shifted(value, hop, 0.0, row, later) + value
        coeff = coeff * shifted(coeff, hop, 1.0, row, later)
        hop *= 2
    return coeff, value


def gates(forget_proj, gap, started):
    sig_neg = jax.nn.sigmoid(-forget_proj)
    keep = gap * sig_neg
    return sig_neg, keep, jnp.where(started > 0.0, 0.0, 1.0 - keep)


def scan_forward(proj_ref, started_ref, gap_ref, state_ref, squares_ref):
    rows, width = state_ref.shape
    row = lax.broadcasted_iota(jnp.int32, (TILE, width), 0)
    gap = gap_ref[...]

    def step(index, carry):
        place = pl.ds(pl.multiple_of(index * TILE, TILE), TILE)
        in_proj = proj_ref[place, pl.ds(0, width)]
        forget_proj = proj_ref[place, pl.ds(width, width)]
        _, keep, decay = gates(forget_proj, gap, started_ref[place, :])
        coeff, value = tile_scan(decay, silu(in_proj) * keep, row, False)
        state = value + coeff * carry
        state_ref[place, :] = state
        squares_ref[place, :] = jnp.sum(state * state, axis=-1, keepdims=True)
        return state[TILE - 1 :, :]

    lax.fori_loop(0, rows // TILE, step, jnp.zeros((1, width), F32), unroll=4)


def scan_backward(proj_ref, state_ref, d_state_ref, started_ref, gap_ref, d_in_ref, d_forget_ref):
    rows, width = state_ref.shape
    row = lax.broadcasted_iota(jnp.int32, (TILE, width), 0)
    gap = gap_ref[...]

    def located(index):
        return pl.ds(pl.multiple_of(index * TILE, TILE), TILE)

    def step(count, carry):
        index = rows // TILE - 1 - count
        place = located(index)
        before = located(jnp.maximum(index - 1, 0))
        in_proj = proj_ref[place, pl.ds(0, width)]
        forget_proj = proj_ref[place, pl.ds(width, width)]
        started = started_ref[place, :]
        sig_neg, keep, decay = gates(forget_proj, gap, started)
        d_state = d_state_ref[place, :]
        coeff, value = tile_scan(decay, decay * d_state, row, True)
        passed = value + coeff * carry
        moved = jnp.where(row < TILE - 1, pltpu.roll(passed, TILE - 1, 0), carry)
        d_total = d_state + moved
        last = state_ref[before, :][TILE - 1 :, :]
        previous = jnp.where(row >= 1, pltpu.roll(state_ref[place, :], 1, 0), last)
        previous = jnp.where(started > 0.0, 0.0, previous)
        sig = jax.nn.sigmoid(in_proj)
        d_in_ref[place, :] = d_total * keep * (sig * (1.0 + in_proj * (1.0 - sig)))
        d_keep = d_total * (in_proj * sig) - d_total * previous
        d_forget_ref[place, :] = -d_keep * gap * sig_neg * (1.0 - sig_neg)
        return passed[:1, :]

    lax.fori_loop(0, rows // TILE, step, jnp.zeros((1, width), F32), unroll=4)


def run_forward(proj, started, gap):
    rows, width = proj.shape[0], gap.shape[1]
    return pl.pallas_call(
        scan_forward,
        out_shape=[
            jax.ShapeDtypeStruct((rows, width), F32),
            jax.ShapeDtypeStruct((rows, 1), F32),
        ],
        compiler_params=pltpu.CompilerParams(vmem_limit_bytes=48 * 2**20),
    )(proj, started, gap)


def run_backward(proj, state, d_state, started, gap):
    rows, width = state.shape
    return pl.pallas_call(
        scan_backward,
        out_shape=[jax.ShapeDtypeStruct((rows, width), F32)] * 2,
        compiler_params=pltpu.CompilerParams(vmem_limit_bytes=48 * 2**20),
    )(proj, state, d_state, started, gap)


def shards(
    tokens,
    cotangent,
    lengths,
    lower_bound,
    mixer_w,
    mlp_in,
    mlp_down,
    gains,
    mixer_m,
    mixer_v,
    in_m,
    in_v,
    down_m,
    down_v,
    gain_m,
    gain_v,
):
    rows, width = tokens.shape
    own, _, hidden_width = mlp_in.shape
    down_rows = mlp_down.shape[0]
    planes = lax.axis_size("z")
    spots = lax.axis_size(PLANE)
    quads = lax.axis_size(QUAD)
    pairs = lax.axis_size("c")
    group = spots * rows
    spot = lax.axis_index(PLANE)
    chans = planes * own

    low_mixer = mixer_w.astype(BF)
    sent = low_mixer[:, :3, :].reshape(own, 3, planes, spots, own).transpose(3, 0, 1, 2, 4)
    x_low, sent, low_gains = tied(tokens, sent.reshape(spots, own, 3 * chans), gains)
    part = exchange(sent, PLANE)
    part = jnp.concatenate(
        [part.reshape(spots * own, 3 * chans), low_mixer[:, 3, :].reshape(spots * own, chans)], axis=1
    )
    x_parts = quad_parts(x_low, 1)
    full_gains = double_gather(low_gains).swapaxes(0, 1).reshape(3, width)
    low_in = mlp_in.astype(BF)
    inner = quads * down_rows
    sent_in = low_in.reshape(own, 2, planes, quads, pairs, down_rows).transpose(2, 4, 0, 1, 3, 5)
    sent_in = sent_in.reshape(planes * pairs, own, 2 * inner)
    part, sent_in = tied(part, sent_in)
    w_all = gather(part, "z")
    w_proj = w_all[:, : 3 * chans]
    w_out = w_all[:, 3 * chans :].reshape(chans, width)
    x_all = core_gather(x_parts)

    bound = lower_bound.reshape(planes, spots, own)
    gap = (1.0 - lax.dynamic_index_in_dim(bound, spot, 1, False)).reshape(1, chans)
    gain_mid = full_gains[1].reshape(planes, spots, own)
    gain_mid = lax.dynamic_index_in_dim(gain_mid, spot, 1, False).reshape(1, chans)

    ends = jnp.cumsum(lengths)
    starts = ends - lengths
    places = jnp.arange(group, dtype=jnp.int32)
    started = jnp.any(places[:, None] == starts[None, :], axis=-1, keepdims=True).astype(F32)
    home = spot * rows + jnp.arange(rows, dtype=jnp.int32)
    valid = (home < ends[-1]).astype(F32)

    def swapped(value, first, second):
        return value.reshape(rows, first, second, -1).swapaxes(1, 2).reshape(rows, width)

    x = tokens.astype(F32)
    x_normed, x_factor = normalize(x)
    n1 = (normalize(x_all.astype(F32))[0] * full_gains[0]).astype(BF)
    cot = cotangent.astype(F32) * valid[:, None]
    cot_low = cot.astype(BF)
    proj = jnp.dot(n1, w_proj, preferred_element_type=F32)
    proj, sent_in = tied(proj, sent_in)
    part_in = exchange(sent_in, LINE)
    cot_low, part_in = tied(cot_low, part_in)
    cot_all = gather(cot_low, LINE)
    state, squares = run_forward(proj[:, : 2 * chans], started, gap)
    gate_proj = proj[:, 2 * chans :]
    gate_act = silu(gate_proj)
    raw = (state * gain_mid * gate_act).astype(BF)
    lane = jnp.arange(128, dtype=jnp.int32)[None, :]
    upper = squares.astype(BF).astype(F32)
    riders = jnp.where(lane == spot, upper, jnp.where(lane == spots + spot, squares - upper, 0.0))
    raw = jnp.concatenate([raw, riders.astype(BF)], axis=1)
    ride = jnp.pad(jnp.eye(128, dtype=BF), ((chans, 0), (width, 0)))
    w_ride = ride + jnp.pad(w_out, ((0, 128), (0, 128)))
    mix_part = jnp.dot(raw, w_ride, preferred_element_type=F32).astype(BF)
    in_parts = quad_parts(part_in.reshape(planes * pairs * own, 2 * inner), 0)
    mix_raw = scatter(mix_part, PLANE)
    mix_raw, cot_all, *in_parts = tied(mix_raw, cot_all, *in_parts)
    w_in = quad_whole(in_parts)
    squares = jnp.sum(mix_raw[:, width : width + 2 * spots].astype(F32), axis=1)
    home_factor = lax.rsqrt(squares / width + EPS_NORM)
    mix = mix_raw[:, :width].astype(F32) * home_factor[:, None]
    after_mix = x + mix

    mid_normed, mid_factor = normalize(after_mix)
    n2_home = swapped((mid_normed * full_gains[2]).astype(BF), planes, quads)
    low_down, n2_home = tied(mlp_down.astype(BF), n2_home)
    w_down = quad_whole(quad_parts(low_down, 0))
    n2, w_down = tied(gather(n2_home, LINE), w_down)
    gate_up = jnp.dot(n2, w_in, preferred_element_type=F32)
    gate, up_value = gate_up[:, :inner], gate_up[:, inner:]
    silu_gate = silu(gate)
    hidden = (silu_gate * up_value).astype(BF)

    grad_down = lax.dot_general(hidden, cot_all, (((0,), (0,)), ((), ())), preferred_element_type=F32)
    grad_down = grad_down.astype(BF)
    d_hidden = lax.dot_general(cot_all, w_down, (((1,), (1,)), ((), ())), preferred_element_type=F32)
    d_gate = d_hidden * up_value * silu_grad(gate)
    d_up = d_hidden * silu_gate
    d_gate_up = jnp.concatenate([d_gate.astype(BF), d_up.astype(BF)], axis=1)
    d_n2 = lax.dot_general(d_gate_up, w_in, (((1,), (1,)), ((), ())), preferred_element_type=F32)
    d_n2 = swapped(scatter(d_n2.astype(BF), LINE).astype(F32), quads, planes)
    grad_in = lax.dot_general(n2, d_gate_up, (((0,), (0,)), ((), ())), preferred_element_type=F32)
    grad_in = grad_in.astype(BF)
    down = jnp.dot(hidden, w_down, preferred_element_type=F32).astype(BF)
    sums_in = quad_sums(grad_in)
    d_n2, grad_down, down, *sums_in = tied(d_n2, grad_down, down, *sums_in)
    d_mid = cot + norm_back(d_n2 * full_gains[2], mid_normed, mid_factor)
    d_mix_home = d_mid.astype(BF)
    down, d_mix_home = tied(down, d_mix_home)
    down = line_scatter(down)
    shard_in = quad_rest(*sums_in).astype(BF)
    mean = jnp.sum(d_mix_home.astype(F32) * mix, axis=-1) / width
    riders = jnp.concatenate(in_parts_of(mean) + in_parts_of(home_factor), axis=1)
    riders = jnp.pad(riders, ((0, 0), (0, 128 - riders.shape[1])))
    d_mix = gather(jnp.concatenate([d_mix_home, riders], axis=1), PLANE)
    d_mix, shard_in, grad_down = tied(d_mix, shard_in, grad_down)
    riders = d_mix[:, width : width + 6].astype(F32)
    mean = jnp.sum(riders[:, :3], axis=1, keepdims=True)
    factor = jnp.sum(riders[:, 3:], axis=1, keepdims=True)
    shard_down = scatter(grad_down, QUAD).astype(F32)
    got_in = exchange(shard_in.reshape(planes * pairs, own, 2 * inner), LINE)

    d_mixed = lax.dot_general(
        d_mix, w_ride[:chans], (((1,), (1,)), ((), ())), preferred_element_type=F32
    )
    state_normed = state * factor
    mixed_in = (state_normed * gain_mid * gate_act).astype(BF)
    grad_out = lax.dot_general(mixed_in, d_mix, (((0,), (0,)), ((), ())), preferred_element_type=F32)
    d_gate_proj = d_mixed * state_normed * gain_mid * silu_grad(gate_proj)
    d_state = factor * (d_mixed * gain_mid * gate_act - state_normed * mean)
    d_gate_proj = d_gate_proj.astype(BF)
    d_in_proj, d_forget_proj = run_backward(proj[:, : 2 * chans], state, d_state, started, gap)
    d_proj = jnp.concatenate(
        [d_in_proj.astype(BF), d_forget_proj.astype(BF), d_gate_proj], axis=1
    )
    grad_proj = lax.dot_general(n1, d_proj, (((0,), (0,)), ((), ())), preferred_element_type=F32)
    grad_out = grad_out[:, :width].astype(BF).reshape(planes, spots * own, chans)
    grad_all = jnp.concatenate(
        [grad_proj.astype(BF).reshape(planes, spots * own, 3 * chans), grad_out], axis=2
    )
    grad_all, down, got_in = tied(grad_all, down, got_in)
    block_out = (after_mix + down).astype(BF)
    shard_all = scatter(grad_all.reshape(planes * spots * own, 4 * chans), "z")
    shard_in = got_in.reshape(planes, pairs, own, 2, quads, down_rows).transpose(2, 3, 0, 4, 1, 5)
    shard_in = as_stored(shard_in.reshape(own, 2, hidden_width).astype(F32))
    shard_all, shard_in, shard_down = tied(shard_all, shard_in, shard_down)
    shard_proj = shard_all[:, : 3 * chans]
    shard_out = shard_all[:, 3 * chans :].reshape(own, width).astype(F32)
    shard_proj = exchange(shard_proj.reshape(spots, own, 3 * chans), PLANE)
    shard_proj = shard_proj.reshape(spots, own, 3, planes, own).transpose(1, 2, 3, 0, 4)
    shard_proj = shard_proj.reshape(own, 3, width).astype(F32)
    d_n1 = lax.dot_general(d_proj, w_proj, (((1,), (1,)), ((), ())), preferred_element_type=F32)
    d_n1 = scatter(d_n1.astype(BF), PLANE).astype(F32)
    input_grad = d_mid + norm_back(d_n1 * full_gains[0], x_normed, x_factor)

    low_rows = low_mixer.astype(F32)
    shard_gains = jnp.stack(
        [
            jnp.sum(shard_proj * low_rows[:, :3, :], axis=(1, 2)),
            jnp.sum(shard_out * low_rows[:, 3, :], axis=1),
            jnp.sum(shard_in * low_in.astype(F32), axis=(1, 2)),
        ],
        axis=0,
    ) / gains
    shard_mixer = as_stored(jnp.concatenate([shard_proj, shard_out[:, None, :]], axis=1))

    local_total = (
        jnp.sum(shard_mixer * shard_mixer)
        + jnp.sum(shard_in * shard_in)
        + jnp.sum(shard_down * shard_down)
        + jnp.sum(shard_gains * shard_gains)
    )
    grad_norm = jnp.sqrt(total_of(local_total.reshape(1, 1))[0, 0])
    clip = jnp.minimum(1.0, CLIP_NORM / (grad_norm + 1e-06))
    new_mixer, new_mixer_m, new_mixer_v = adam_step(
        mixer_w, mixer_m, mixer_v, clip * shard_mixer, RATE_MATRIX, DECAY_WEIGHT
    )
    new_in, new_in_m, new_in_v = adam_step(
        mlp_in, in_m, in_v, clip * shard_in, RATE_MATRIX, DECAY_WEIGHT
    )
    new_down, new_down_m, new_down_v = adam_step(
        mlp_down, down_m, down_v, clip * shard_down, RATE_MATRIX, DECAY_WEIGHT
    )
    new_gains, new_gain_m, new_gain_v = adam_step(
        gains, gain_m, gain_v, clip * shard_gains, RATE_GAIN, 0.0
    )
    return (
        block_out,
        input_grad,
        grad_norm,
        new_mixer,
        new_mixer_m,
        new_mixer_v,
        new_in,
        new_in_m,
        new_in_v,
        new_down,
        new_down_m,
        new_down_v,
        new_gains,
        new_gain_m,
        new_gain_v,
    )


def solution(mesh):
    planes, spots = mesh.shape["dp"], mesh.shape["seq"]
    side = math.isqrt(spots // 2)
    split = Mesh(mesh.devices.reshape(planes, spots // (2 * side), side, 2), ALL)
    rows2, rows3, cols = P(ALL, None), P(ALL, None, None), P(None, ALL)
    return jax.shard_map(
        shards,
        mesh=split,
        in_specs=(rows2, rows2, P("z"), P(), rows3, rows3, rows2, cols)
        + (rows3,) * 4
        + (rows2,) * 2
        + (cols,) * 2,
        out_specs=(rows2, rows2, P()) + (rows3,) * 6 + (rows2,) * 3 + (cols,) * 3,
        check_vma=False,
    )
```

```python
import functools
import math

import jax
import jax.numpy as jnp
from jax import lax
from jax.experimental import pallas as pl
from jax.experimental.layout import Layout, with_layout_constraint
from jax.experimental.pallas import tpu as pltpu
from jax.sharding import Mesh, PartitionSpec as P

STEP = 10


EPS_NORM = 1e-06
BETA_ONE = 0.9
BETA_TWO = 0.999
ADAM_EPS = 1e-08
RATE_MATRIX = 0.03
RATE_GAIN = 0.5
DECAY_WEIGHT = 0.1
CLIP_NORM = 1.0

ALL = ("z", "y", "x", "c")
PLANE = ("y", "x", "c")
LINE = ("z", "c")
QUAD = ("y", "x")
TILE = 8
BF = jnp.bfloat16
F32 = jnp.float32


def gather(value, axes):
    return lax.all_gather(value, axes, axis=0, tiled=True)


def scatter(value, axes):
    return lax.psum_scatter(value, axes, scatter_dimension=0, tiled=True)


def exchange(value, axes):
    return lax.all_to_all(value, axes, 0, 0, tiled=True)


def ring_gather(value, axis):
    count, mine = lax.axis_size(axis), lax.axis_index(axis)
    if count == 2:
        other = lax.ppermute(value, axis, [(0, 1), (1, 0)])
        return jnp.stack([jnp.where(mine == 0, value, other), jnp.where(mine == 0, other, value)])
    up, down, ups, downs = value, value, [], []
    for hop in range(1, count):
        up = lax.ppermute(up, axis, [(i, i + 1) for i in range(hop - 1, count - 1)])
        down = lax.ppermute(down, axis, [(i, i - 1) for i in range(1, count - hop + 1)])
        ups.append(up)
        downs.append(down)
    places = []
    for place in range(count):
        found = value
        for back in range(1, count):
            if place + back < count:
                found = jnp.where(mine == place + back, ups[back - 1], found)
            if place >= back:
                found = jnp.where(mine == place - back, downs[back - 1], found)
        places.append(found)
    return jnp.stack(places)


def added(terms):
    return sum(term.astype(F32) for term in terms)


def ring_scatter(value, axis, dim=0):
    return added(ring_terms(value, axis, dim))


def ring_terms(value, axis, dim=0):
    count, mine = lax.axis_size(axis), lax.axis_index(axis)

    def block(back):
        return lax.dynamic_index_in_dim(value, (mine - back) % count, dim, False)

    if count == 2:
        return [block(0), lax.ppermute(block(1), axis, [(0, 1), (1, 0)])]
    up = down = None
    for hop in range(1, count):
        up_sum, down_sum = block(hop), block(count - hop)
        if up is not None:
            up_sum = (up_sum.astype(F32) + up.astype(F32)).astype(BF)
            down_sum = (down_sum.astype(F32) + down.astype(F32)).astype(BF)
        up = lax.ppermute(up_sum, axis, [(i, i + 1) for i in range(hop)])
        down = lax.ppermute(down_sum, axis, [(i, i - 1) for i in range(count - hop, count)])
    return [block(0), up, down]


def double_gather(value):
    value = value[None]
    for axis in ("c", "x", "y", "z"):
        count, mine = lax.axis_size(axis), lax.axis_index(axis)
        hop = 1
        while hop < count:
            other = lax.ppermute(value, axis, [(i, i ^ hop) for i in range(count)])
            low = (mine // hop) % 2 == 0
            value = jnp.concatenate([jnp.where(low, value, other), jnp.where(low, other, value)])
            hop *= 2
    return value


def tied(*values):
    return lax.optimization_barrier(values)


def in_parts_of(value):
    upper = value.astype(BF)
    rest = value - upper.astype(F32)
    middle = rest.astype(BF)
    lower = (rest - middle.astype(F32)).astype(BF)
    return [upper, middle, lower]


def as_stored(value):
    return with_layout_constraint(value, Layout(tuple(range(value.ndim))))


def direct_scatter(value, axis):
    count, mine = lax.axis_size(axis), lax.axis_index(axis)
    total = lax.dynamic_index_in_dim(value, mine, 0, False).astype(F32)
    for back in range(1, count):
        block = lax.dynamic_index_in_dim(value, (mine - back) % count, 0, False)
        total += lax.ppermute(block, axis, [(i, (i - back) % count) for i in range(count)])
    return total


def quad_halves(value, axis):
    half = value.shape[axis] // 2
    first = ring_gather(lax.slice_in_dim(value, 0, half, axis=axis), "x")
    return [first, ring_gather(lax.slice_in_dim(value, half, 2 * half, axis=axis), "y")]


def quad_others(first, second):
    return [ring_gather(first, "y"), ring_gather(second, "x").swapaxes(0, 1)]


def quad_parts(value, axis):
    return quad_others(*quad_halves(value, axis))


def quad_whole(parts):
    return jnp.concatenate(parts, axis=2).reshape(-1, parts[0].shape[-1])


def quad_sums(value):
    value = value.reshape(lax.axis_size("y"), lax.axis_size("x"), -1, value.shape[1])
    half = value.shape[2] // 2
    first = ring_terms(value[:, :, :half], "y")
    return first + ring_terms(value[:, :, half:].swapaxes(0, 1), "x")


def quad_rest(*terms):
    half = len(terms) // 2
    first, second = added(terms[:half]).astype(BF), added(terms[half:]).astype(BF)
    return jnp.concatenate([ring_scatter(first, "x"), ring_scatter(second, "y")], axis=0)


def core_gather(parts):
    both = ring_gather(jnp.concatenate(parts, axis=3), "c")
    return jnp.moveaxis(both, 0, 2).reshape(-1, both.shape[-1])


def line_gather(value):
    both = ring_gather(ring_gather(value, "z"), "c")
    return both.swapaxes(0, 1).reshape(-1, value.shape[1])


def plane_scatter(value):
    value = value.reshape(lax.axis_size("y"), lax.axis_size("x"), 2, -1, value.shape[1])
    value = ring_scatter(value, "c", 2).astype(BF)
    half = value.shape[3] // 2
    first = ring_scatter(ring_scatter(value[..., :half], "y").astype(BF), "x")
    second = ring_scatter(ring_scatter(value[..., half:], "x", 1).astype(BF), "y")
    return jnp.concatenate([first, second], axis=1)


def direct_gather(value, axis):
    count = lax.axis_size(axis)
    hops = [[(i, (i + back) % count) for i in range(count)] for back in range(1, count)]
    return [value] + [lax.ppermute(value, axis, hop) for hop in hops]


def in_order(values, axis):
    count, mine = lax.axis_size(axis), lax.axis_index(axis)
    places = []
    for place in range(count):
        found = values[0]
        for back in range(1, count):
            found = jnp.where((mine - back) % count == place, values[back], found)
        places.append(found)
    return jnp.stack(places)


def core_exchange(value):
    count, core = lax.axis_size("z"), lax.axis_index("c")
    value = value.reshape((count, 2) + value.shape[1:])
    kept = lax.dynamic_index_in_dim(value, core, 1, False)
    other = lax.dynamic_index_in_dim(value, 1 - core, 1, False)
    other = lax.ppermute(other, "c", [(0, 1), (1, 0)])
    first, second = jnp.where(core == 0, kept, other), jnp.where(core == 0, other, kept)
    return jnp.stack([first, second], axis=1)


def line_exchange(value):
    count, mine = lax.axis_size("z"), lax.axis_index("z")
    blocks = [lax.dynamic_index_in_dim(value, (mine - back) % count, 0, False) for back in range(count)]
    got = [blocks[0]]
    for back in range(1, count):
        got.append(lax.ppermute(blocks[back], "z", [(i, (i - back) % count) for i in range(count)]))
    places = []
    for place in range(count):
        found = got[0]
        for back in range(1, count):
            found = jnp.where((mine + back) % count == place, got[back], found)
        places.append(found)
    return jnp.concatenate(places)


def core_terms(value):
    value = value.reshape(lax.axis_size("z"), 2, -1, value.shape[1]).swapaxes(0, 1)
    return ring_terms(value, "c")


def total_of(value):
    for axis in ("c", "x", "y", "z"):
        count = lax.axis_size(axis)
        hop = 1
        while hop < count:
            value = value + lax.ppermute(value, axis, [(i, i ^ hop) for i in range(count)])
            hop *= 2
    return value


def normalize(value):
    factor = lax.rsqrt(jnp.mean(value * value, axis=-1, keepdims=True) + EPS_NORM)
    return (value * factor, factor)


def norm_back(grad_normed, normed, factor):
    return factor * (grad_normed - normed * jnp.mean(grad_normed * normed, axis=-1, keepdims=True))


def silu(value):
    return value * jax.nn.sigmoid(value)


def silu_grad(value):
    sig = jax.nn.sigmoid(value)
    return sig * (1.0 + value * (1.0 - sig))


def adam_step(weight, first, second, grad, rate, decay_w):
    first_new = BETA_ONE * first + (1.0 - BETA_ONE) * grad
    second_new = BETA_TWO * second + (1.0 - BETA_TWO) * grad * grad
    scale_one, scale_two = 1.0 / (1.0 - BETA_ONE**STEP), 1.0 / (1.0 - BETA_TWO**STEP)
    step_size = (first_new * scale_one) / (jnp.sqrt(second_new * scale_two) + ADAM_EPS)
    return (weight - rate * (step_size + decay_w * weight), first_new, second_new)


def shifted(value, hop, fill, row, later):
    size = value.shape[0]
    moved = pltpu.roll(value, size - hop if later else hop, 0)
    inside = row < size - hop if later else row >= hop
    return jnp.where(inside, moved, fill)


def tile_scan(coeff, value, row, later):
    hop = 1
    while hop < value.shape[0]:
        value = coeff * shifted(value, hop, 0.0, row, later) + value
        coeff = coeff * shifted(coeff, hop, 1.0, row, later)
        hop *= 2
    return coeff, value


def gates(forget_proj, gap, started):
    sig_neg = jax.nn.sigmoid(-forget_proj)
    keep = gap * sig_neg
    return sig_neg, keep, jnp.where(started > 0.0, 0.0, 1.0 - keep)


def scan_forward(proj_ref, started_ref, gap_ref, state_ref, squares_ref):
    rows, width = state_ref.shape
    row = lax.broadcasted_iota(jnp.int32, (TILE, width), 0)
    gap = gap_ref[...]

    def step(index, carry):
        place = pl.ds(pl.multiple_of(index * TILE, TILE), TILE)
        in_proj = proj_ref[place, pl.ds(0, width)]
        forget_proj = proj_ref[place, pl.ds(width, width)]
        _, keep, decay = gates(forget_proj, gap, started_ref[place, :])
        coeff, value = tile_scan(decay, silu(in_proj) * keep, row, False)
        state = value + coeff * carry
        state_ref[place, :] = state
        squares_ref[place, :] = jnp.sum(state * state, axis=-1, keepdims=True)
        return state[TILE - 1 :, :]

    lax.fori_loop(0, rows // TILE, step, jnp.zeros((1, width), F32), unroll=4)


def scan_backward(proj_ref, state_ref, d_state_ref, started_ref, gap_ref, d_in_ref, d_forget_ref):
    rows, width = state_ref.shape
    row = lax.broadcasted_iota(jnp.int32, (TILE, width), 0)
    gap = gap_ref[...]

    def located(index):
        return pl.ds(pl.multiple_of(index * TILE, TILE), TILE)

    def step(count, carry):
        index = rows // TILE - 1 - count
        place = located(index)
        before = located(jnp.maximum(index - 1, 0))
        in_proj = proj_ref[place, pl.ds(0, width)]
        forget_proj = proj_ref[place, pl.ds(width, width)]
        started = started_ref[place, :]
        sig_neg, keep, decay = gates(forget_proj, gap, started)
        d_state = d_state_ref[place, :]
        coeff, value = tile_scan(decay, decay * d_state, row, True)
        passed = value + coeff * carry
        moved = jnp.where(row < TILE - 1, pltpu.roll(passed, TILE - 1, 0), carry)
        d_total = d_state + moved
        last = state_ref[before, :][TILE - 1 :, :]
        previous = jnp.where(row >= 1, pltpu.roll(state_ref[place, :], 1, 0), last)
        previous = jnp.where(started > 0.0, 0.0, previous)
        sig = jax.nn.sigmoid(in_proj)
        d_in_ref[place, :] = d_total * keep * (sig * (1.0 + in_proj * (1.0 - sig)))
        d_keep = d_total * (in_proj * sig) - d_total * previous
        d_forget_ref[place, :] = -d_keep * gap * sig_neg * (1.0 - sig_neg)
        return passed[:1, :]

    lax.fori_loop(0, rows // TILE, step, jnp.zeros((1, width), F32), unroll=4)


def settle(got_ref, out_ref, low_ref, grad_ref, first_ref, inner_ref, total_ref):
    spots, own, packed = got_ref.shape
    width = out_ref.shape[1]
    planes = packed // (3 * own)
    low_half = lax.broadcasted_iota(jnp.int32, (own, 2 * own), 1) < own
    total = jnp.zeros((own, 2 * own), F32)
    first, inner = total, total
    for pair in range(0, spots, 2):
        for kind in range(3):
            for plane in range(0, planes, 2):
                at = pl.ds((kind * planes + plane) * own, 2 * own)
                even = got_ref[pair, :, at].astype(F32)
                odd = got_ref[pair + 1, :, at].astype(F32)
                near = jnp.where(low_half, even, pltpu.roll(odd, own, 1))
                far = jnp.where(low_half, pltpu.roll(even, own, 1), odd)
                for step, grad in enumerate((near, far)):
                    place = pl.ds(((plane + step) * spots + pair) * own, 2 * own)
                    grad_ref[kind, :, place] = grad
                    total += grad * grad
                    first += grad * low_ref[kind, :, place].astype(F32)
    for start in range(0, width, 2 * own):
        place = pl.ds(start, 2 * own)
        grad = out_ref[:, place].astype(F32)
        grad_ref[3, :, place] = grad
        total += grad * grad
        inner += grad * low_ref[3, :, place].astype(F32)
    first_ref[...] = jnp.sum(first, axis=1, keepdims=True)
    inner_ref[...] = jnp.sum(inner, axis=1, keepdims=True)
    total_ref[...] = jnp.sum(total, axis=1, keepdims=True)


def run_settle(got, shard_out, low_mixer):
    spots, own, packed = got.shape
    width = shard_out.shape[1]
    planes = packed // (3 * own)
    if 2 * own != 128 or planes % 2 != 0:
        grad = got.reshape(spots, own, 3, planes, own).transpose(1, 2, 3, 0, 4)
        grad = jnp.concatenate([grad.reshape(own, 3, width), shard_out[:, None, :]], axis=1)
        grad = grad.astype(F32)
        product = jnp.sum(grad * low_mixer.astype(F32), axis=2)
        return grad, jnp.sum(product[:, :3], axis=1), product[:, 3], jnp.sum(grad * grad, axis=(1, 2))
    column = jax.ShapeDtypeStruct((own, 1), F32)
    grad, *sums = pl.pallas_call(
        settle,
        out_shape=[jax.ShapeDtypeStruct((4, own, width), F32)] + [column] * 3,
        compiler_params=pltpu.CompilerParams(vmem_limit_bytes=48 * 2**20),
    )(got, shard_out, low_mixer.swapaxes(0, 1))
    return [grad.swapaxes(0, 1)] + [column[:, 0] for column in sums]


def column_blocks(width, first, second):
    size = width // (first * second)
    for i in range(first):
        for j in range(second):
            yield pl.ds((i * second + j) * size, size), pl.ds((j * first + i) * size, size)


def enter_glu(order, mix_ref, x_ref, gain_ref, after_ref, n2_ref, mid_ref, home_ref):
    width = x_ref.shape[1]
    squares = jnp.sum(mix_ref[:, width:].astype(F32), axis=1, keepdims=True)
    home = lax.rsqrt(squares / width + EPS_NORM)
    after = x_ref[...].astype(F32) + mix_ref[:, :width].astype(F32) * home
    mid = lax.rsqrt(jnp.mean(after * after, axis=1, keepdims=True) + EPS_NORM)
    after_ref[...] = after
    mid_ref[...] = mid
    home_ref[...] = home
    n2 = (after * mid * gain_ref[...]).astype(BF)
    for source, target in column_blocks(width, *order):
        n2_ref[:, target] = n2[:, source.start : source.start + source.size]


def leave_glu(
    order, d_n2_ref, cot_ref, after_ref, mid_ref, mix_ref, home_ref, gain_ref, d_mid_ref, out_ref, held_ref
):
    width = cot_ref.shape[1]
    mid, home = mid_ref[...], home_ref[...]
    for target, source in column_blocks(width, *order):
        held_ref[:, target] = d_n2_ref[:, source].astype(F32) * gain_ref[:, target]
    normed = after_ref[...] * mid
    grad = held_ref[...]
    inner = jnp.mean(grad * normed, axis=1, keepdims=True)
    d_mid = cot_ref[...].astype(F32) + mid * (grad - normed * inner)
    d_mid_ref[...] = d_mid
    low = d_mid.astype(BF)
    out_ref[:, :width] = low
    mean = jnp.sum(low.astype(F32) * (mix_ref[:, :width].astype(F32) * home), axis=1, keepdims=True) / width
    lane = lax.broadcasted_iota(jnp.int32, (mid.shape[0], 128), 1)
    riders = jnp.zeros((mid.shape[0], 128), F32)
    for at, value in ((0, mean), (3, home)):
        for part in range(3):
            upper = value.astype(BF).astype(F32)
            riders = jnp.where(lane == at + part, upper, riders)
            value = value - upper
    out_ref[:, width:] = riders.astype(BF)


def run_enter(mix_raw, tokens, gain, order):
    rows, width = tokens.shape
    if width // (order[0] * order[1]) % 128 != 0:
        squares = jnp.sum(mix_raw[:, width:].astype(F32), axis=1, keepdims=True)
        home = lax.rsqrt(squares / width + EPS_NORM)
        after = tokens.astype(F32) + mix_raw[:, :width].astype(F32) * home
        normed, mid = normalize(after)
        n2 = (normed * gain).astype(BF).reshape(rows, *order, -1).swapaxes(1, 2)
        return after, n2.reshape(rows, width), mid, home
    column = jax.ShapeDtypeStruct((rows, 1), F32)
    return pl.pallas_call(
        functools.partial(enter_glu, order),
        out_shape=[
            jax.ShapeDtypeStruct((rows, width), F32),
            jax.ShapeDtypeStruct((rows, width), BF),
            column,
            column,
        ],
        compiler_params=pltpu.CompilerParams(vmem_limit_bytes=48 * 2**20),
    )(mix_raw, tokens, gain)


def run_leave(d_n2, cot, after, mid, mix_raw, home, gain, order):
    rows, width = cot.shape
    if width // (order[0] * order[1]) % 128 != 0:
        grad = d_n2.reshape(rows, order[1], order[0], -1).swapaxes(1, 2).reshape(rows, width)
        d_mid = cot.astype(F32) + norm_back(grad.astype(F32) * gain, after * mid, mid)
        low = d_mid.astype(BF)
        mix = mix_raw[:, :width].astype(F32) * home
        mean = jnp.sum(low.astype(F32) * mix, axis=1, keepdims=True) / width
        riders = jnp.concatenate(in_parts_of(mean) + in_parts_of(home), axis=1)
        riders = jnp.pad(riders, ((0, 0), (0, 128 - riders.shape[1])))
        return d_mid, jnp.concatenate([low, riders], axis=1)
    return pl.pallas_call(
        functools.partial(leave_glu, order),
        out_shape=[
            jax.ShapeDtypeStruct((rows, width), F32),
            jax.ShapeDtypeStruct((rows, width + 128), BF),
        ],
        scratch_shapes=[pltpu.VMEM((rows, width), F32)],
        compiler_params=pltpu.CompilerParams(vmem_limit_bytes=48 * 2**20),
    )(d_n2, cot, after, mid, mix_raw, home, gain)


def run_forward(proj, started, gap):
    rows, width = proj.shape[0], gap.shape[1]
    return pl.pallas_call(
        scan_forward,
        out_shape=[
            jax.ShapeDtypeStruct((rows, width), F32),
            jax.ShapeDtypeStruct((rows, 1), F32),
        ],
        compiler_params=pltpu.CompilerParams(vmem_limit_bytes=48 * 2**20),
    )(proj, started, gap)


def run_backward(proj, state, d_state, started, gap):
    rows, width = state.shape
    return pl.pallas_call(
        scan_backward,
        out_shape=[jax.ShapeDtypeStruct((rows, width), F32)] * 2,
        compiler_params=pltpu.CompilerParams(vmem_limit_bytes=48 * 2**20),
    )(proj, state, d_state, started, gap)


def shards(
    tokens,
    cotangent,
    lengths,
    lower_bound,
    mixer_w,
    mlp_in,
    mlp_down,
    gains,
    mixer_m,
    mixer_v,
    in_m,
    in_v,
    down_m,
    down_v,
    gain_m,
    gain_v,
):
    rows, width = tokens.shape
    own, _, hidden_width = mlp_in.shape
    down_rows = mlp_down.shape[0]
    planes = lax.axis_size("z")
    spots = lax.axis_size(PLANE)
    quads = lax.axis_size(QUAD)
    pairs = lax.axis_size("c")
    group = spots * rows
    spot = lax.axis_index(PLANE)
    chans = planes * own

    ends = jnp.cumsum(lengths)
    starts = ends - lengths
    places = jnp.arange(group, dtype=jnp.int32)
    started = jnp.any(places[:, None] == starts[None, :], axis=-1, keepdims=True).astype(F32)
    home = spot * rows + jnp.arange(rows, dtype=jnp.int32)
    valid = (home < ends[-1]).astype(F32)

    cot_low = (cotangent.astype(F32) * valid[:, None]).astype(BF)

    low_mixer = mixer_w.astype(BF)
    sent = low_mixer[:, :3, :].reshape(own, 3, planes, spots, own).transpose(3, 0, 1, 2, 4)
    part = exchange(sent.reshape(spots, own, 3 * chans), PLANE)
    part = jnp.concatenate(
        [part.reshape(spots * own, 3 * chans), low_mixer[:, 3, :].reshape(spots * own, chans)], axis=1
    )
    x_low, part, low_gains, low_down, low_in = tied(tokens, part, gains, mlp_down, mlp_in)
    x_parts = quad_parts(x_low, 1)
    full_gains = double_gather(low_gains).swapaxes(0, 1).reshape(3, width)
    low_in = low_in.astype(BF)
    inner = quads * down_rows
    sent_in = low_in.reshape(own, 2, planes, quads, pairs, down_rows).transpose(2, 4, 0, 1, 3, 5)
    sent_in = sent_in.reshape(planes * pairs, own, 2 * inner)
    w_down = quad_whole(quad_parts(low_down.astype(BF), 0))
    w_all = gather(part, "z")
    x_all = core_gather(x_parts)

    bound = lower_bound.reshape(planes, spots, own)
    gap = (1.0 - lax.dynamic_index_in_dim(bound, spot, 1, False)).reshape(1, chans)
    gain_mid = full_gains[1].reshape(planes, spots, own)
    gain_mid = lax.dynamic_index_in_dim(gain_mid, spot, 1, False).reshape(1, chans)

    x = tokens.astype(F32)
    x_normed, x_factor = normalize(x)
    n1 = (normalize(x_all.astype(F32))[0] * full_gains[0]).astype(BF)
    blocks_in = core_exchange(sent_in)
    w_all, w_down, n1, blocks_in = tied(w_all, w_down, n1, blocks_in)
    w_proj = w_all[:, : 3 * chans]
    w_out = w_all[:, 3 * chans :].reshape(chans, width)
    proj = jnp.dot(n1, w_proj, preferred_element_type=F32)
    proj, blocks_in = tied(proj, blocks_in)
    part_in = line_exchange(blocks_in)
    state, squares = run_forward(proj[:, : 2 * chans], started, gap)
    state, held_cot = tied(state, cot_low)
    cots = direct_gather(held_cot, "z")
    gate_proj = proj[:, 2 * chans :]
    gate_act = silu(gate_proj)
    raw = (state * gain_mid * gate_act).astype(BF)
    lane = jnp.arange(128, dtype=jnp.int32)[None, :]
    upper = squares.astype(BF).astype(F32)
    riders = jnp.where(lane == spot, upper, jnp.where(lane == spots + spot, squares - upper, 0.0))
    raw = jnp.concatenate([raw, riders.astype(BF)], axis=1)
    ride = jnp.pad(jnp.eye(128, dtype=BF), ((chans, 0), (width, 0)))
    w_ride = ride + jnp.pad(w_out, ((0, 128), (0, 128)))
    mix_part = jnp.dot(raw, w_ride, preferred_element_type=F32).astype(BF)
    mix_raw, part_in, *cots = tied(scatter(mix_part, PLANE), part_in, *cots)
    cot_all = ring_gather(in_order(cots, "z"), "c").swapaxes(0, 1)
    cot_all = cot_all.reshape(planes * pairs * rows, width)
    w_in = quad_whole(quad_parts(part_in.reshape(planes * pairs * own, 2 * inner), 0))

    order, gain_glu = (planes, quads), full_gains[2].reshape(1, width)
    after_mix, n2_home, mid_factor, home_factor = run_enter(mix_raw, tokens, gain_glu, order)
    n2 = gather(n2_home, LINE)
    gate_up = jnp.dot(n2, w_in, preferred_element_type=F32)
    gate, up_value = gate_up[:, :inner], gate_up[:, inner:]
    silu_gate = silu(gate)
    hidden = (silu_gate * up_value).astype(BF)

    grad_down = lax.dot_general(hidden, cot_all, (((0,), (0,)), ((), ())), preferred_element_type=F32)
    grad_down = grad_down.astype(BF)
    d_hidden = lax.dot_general(cot_all, w_down, (((1,), (1,)), ((), ())), preferred_element_type=F32)
    d_gate = d_hidden * up_value * silu_grad(gate)
    d_up = d_hidden * silu_gate
    d_gate_up = jnp.concatenate([d_gate.astype(BF), d_up.astype(BF)], axis=1)
    d_n2 = lax.dot_general(d_gate_up, w_in, (((1,), (1,)), ((), ())), preferred_element_type=F32)
    d_n2 = scatter(d_n2.astype(BF), LINE)
    grad_in = lax.dot_general(n2, d_gate_up, (((0,), (0,)), ((), ())), preferred_element_type=F32)
    grad_in = grad_in.astype(BF)
    down = jnp.dot(hidden, w_down, preferred_element_type=F32).astype(BF)
    sums_in = quad_sums(grad_in)
    downs = core_terms(down)
    d_n2, grad_down, *held_terms = tied(d_n2, grad_down, *downs, *sums_in)
    downs, sums_in = held_terms[: len(downs)], held_terms[len(downs) :]
    d_mid, d_mix_home = run_leave(
        d_n2, cot_low, after_mix, mid_factor, mix_raw, home_factor, gain_glu, order
    )
    *downs, d_mix_home = tied(*downs, d_mix_home)
    down = direct_scatter(added(downs).astype(BF), "z")
    shard_in = quad_rest(*sums_in).astype(BF)
    d_mix = gather(d_mix_home, PLANE)
    d_mix, shard_in, grad_down, down = tied(d_mix, shard_in, grad_down, down)
    block_out = (after_mix + down).astype(BF)
    riders = d_mix[:, width : width + 6].astype(F32)
    mean = jnp.sum(riders[:, :3], axis=1, keepdims=True)
    factor = jnp.sum(riders[:, 3:], axis=1, keepdims=True)
    shard_down = scatter(grad_down, QUAD).astype(F32)
    got_in = exchange(shard_in.reshape(planes * pairs, own, 2 * inner), LINE)

    d_mixed = lax.dot_general(
        d_mix, w_ride[:chans], (((1,), (1,)), ((), ())), preferred_element_type=F32
    )
    state_normed = state * factor
    mixed_in = (state_normed * gain_mid * gate_act).astype(BF)
    grad_out = lax.dot_general(mixed_in, d_mix, (((0,), (0,)), ((), ())), preferred_element_type=F32)
    d_gate_proj = d_mixed * state_normed * gain_mid * silu_grad(gate_proj)
    d_state = factor * (d_mixed * gain_mid * gate_act - state_normed * mean)
    d_gate_proj = d_gate_proj.astype(BF)
    d_in_proj, d_forget_proj = run_backward(proj[:, : 2 * chans], state, d_state, started, gap)
    d_proj = jnp.concatenate(
        [d_in_proj.astype(BF), d_forget_proj.astype(BF), d_gate_proj], axis=1
    )
    grad_proj = lax.dot_general(n1, d_proj, (((0,), (0,)), ((), ())), preferred_element_type=F32)
    grad_out = grad_out[:, :width].astype(BF).reshape(planes, spots * own, chans)
    grad_all = jnp.concatenate(
        [grad_proj.astype(BF).reshape(planes, spots * own, 3 * chans), grad_out], axis=2
    )
    grad_all, got_in, held_proj = tied(grad_all, got_in, d_proj)
    shard_all = scatter(grad_all.reshape(planes * spots * own, 4 * chans), "z")
    shard_in = got_in.reshape(planes, pairs, own, 2, quads, down_rows).transpose(2, 3, 0, 4, 1, 5)
    shard_in = as_stored(shard_in.reshape(own, 2, hidden_width).astype(F32))
    gain_in = jnp.sum(shard_in * low_in.astype(F32), axis=(1, 2))
    total_early = jnp.sum(shard_in * shard_in) + jnp.sum(shard_down * shard_down)
    d_n1 = lax.dot_general(held_proj, w_proj, (((1,), (1,)), ((), ())), preferred_element_type=F32)
    d_n1 = plane_scatter(d_n1.astype(BF))
    input_grad = d_mid + norm_back(d_n1 * full_gains[0], x_normed, x_factor)
    shard_all, shard_in, shard_down, gain_in, total_early, input_grad = tied(
        shard_all, shard_in, shard_down, gain_in, total_early, input_grad
    )
    got_proj = exchange(shard_all[:, : 3 * chans].reshape(spots, own, 3 * chans), PLANE)
    shard_out = shard_all[:, 3 * chans :].reshape(own, width)

    shard_mixer, gain_first, gain_inner, total_mixer = run_settle(got_proj, shard_out, low_mixer)
    shard_mixer = as_stored(shard_mixer)
    shard_gains = jnp.stack([gain_first, gain_inner, gain_in]) / gains
    local_total = jnp.sum(total_mixer) + total_early + jnp.sum(shard_gains * shard_gains)
    grad_norm = jnp.sqrt(total_of(local_total.reshape(1, 1))[0, 0])
    clip = jnp.minimum(1.0, CLIP_NORM / (grad_norm + 1e-06))
    new_mixer, new_mixer_m, new_mixer_v = adam_step(
        mixer_w, mixer_m, mixer_v, clip * shard_mixer, RATE_MATRIX, DECAY_WEIGHT
    )
    new_in, new_in_m, new_in_v = adam_step(
        mlp_in, in_m, in_v, clip * shard_in, RATE_MATRIX, DECAY_WEIGHT
    )
    new_down, new_down_m, new_down_v = adam_step(
        mlp_down, down_m, down_v, clip * shard_down, RATE_MATRIX, DECAY_WEIGHT
    )
    new_gains, new_gain_m, new_gain_v = adam_step(
        gains, gain_m, gain_v, clip * shard_gains, RATE_GAIN, 0.0
    )
    return (
        block_out,
        input_grad,
        grad_norm,
        new_mixer,
        new_mixer_m,
        new_mixer_v,
        new_in,
        new_in_m,
        new_in_v,
        new_down,
        new_down_m,
        new_down_v,
        new_gains,
        new_gain_m,
        new_gain_v,
    )


def solution(mesh):
    planes, spots = mesh.shape["dp"], mesh.shape["seq"]
    side = math.isqrt(spots // 2)
    split = Mesh(mesh.devices.reshape(planes, spots // (2 * side), side, 2), ALL)
    rows2, rows3, cols = P(ALL, None), P(ALL, None, None), P(None, ALL)
    return jax.shard_map(
        shards,
        mesh=split,
        in_specs=(rows2, rows2, P("z"), P(), rows3, rows3, rows2, cols)
        + (rows3,) * 4
        + (rows2,) * 2
        + (cols,) * 2,
        out_specs=(rows2, rows2, P()) + (rows3,) * 6 + (rows2,) * 3 + (cols,) * 3,
        check_vma=False,
    )
```

```python
import functools
import math

import jax
import jax.numpy as jnp
from jax import lax
from jax.experimental import pallas as pl
from jax.experimental.pallas import tpu as pltpu
from jax.sharding import Mesh, PartitionSpec as P

STEP = 10


EPS_NORM = 1e-06
BETA_ONE = 0.9
BETA_TWO = 0.999
ADAM_EPS = 1e-08
RATE_MATRIX = 0.03
RATE_GAIN = 0.5
DECAY_WEIGHT = 0.1
CLIP_NORM = 1.0

ALL = ("z", "y", "x", "c")
PLANE = ("y", "x", "c")
LINE = ("z", "c")
QUAD = ("y", "x")
TILE = 8
BF = jnp.bfloat16
F32 = jnp.float32


def gather(value, axes):
    return lax.all_gather(value, axes, axis=0, tiled=True)


def scatter(value, axes):
    return lax.psum_scatter(value, axes, scatter_dimension=0, tiled=True)


def exchange(value, axes):
    return lax.all_to_all(value, axes, 0, 0, tiled=True)


def ring_gather(value, axis):
    count, mine = lax.axis_size(axis), lax.axis_index(axis)
    if count == 2:
        other = lax.ppermute(value, axis, [(0, 1), (1, 0)])
        return jnp.stack([jnp.where(mine == 0, value, other), jnp.where(mine == 0, other, value)])
    up, down, ups, downs = value, value, [], []
    for hop in range(1, count):
        up = lax.ppermute(up, axis, [(i, i + 1) for i in range(hop - 1, count - 1)])
        down = lax.ppermute(down, axis, [(i, i - 1) for i in range(1, count - hop + 1)])
        ups.append(up)
        downs.append(down)
    places = []
    for place in range(count):
        found = value
        for back in range(1, count):
            if place + back < count:
                found = jnp.where(mine == place + back, ups[back - 1], found)
            if place >= back:
                found = jnp.where(mine == place - back, downs[back - 1], found)
        places.append(found)
    return jnp.stack(places)


def added(terms):
    return sum(term.astype(F32) for term in terms)


def ring_scatter(value, axis, dim=0):
    return added(ring_terms(value, axis, dim))


def ring_terms(value, axis, dim=0):
    count, mine = lax.axis_size(axis), lax.axis_index(axis)

    def block(back):
        return lax.dynamic_index_in_dim(value, (mine - back) % count, dim, False)

    if count == 2:
        return [block(0), lax.ppermute(block(1), axis, [(0, 1), (1, 0)])]
    up = down = None
    for hop in range(1, count):
        up_sum, down_sum = block(hop), block(count - hop)
        if up is not None:
            up_sum = (up_sum.astype(F32) + up.astype(F32)).astype(BF)
            down_sum = (down_sum.astype(F32) + down.astype(F32)).astype(BF)
        up = lax.ppermute(up_sum, axis, [(i, i + 1) for i in range(hop)])
        down = lax.ppermute(down_sum, axis, [(i, i - 1) for i in range(count - hop, count)])
    return [block(0), up, down]


def double_gather(value):
    value = value[None]
    for axis in ("c", "x", "y", "z"):
        count, mine = lax.axis_size(axis), lax.axis_index(axis)
        hop = 1
        while hop < count:
            other = lax.ppermute(value, axis, [(i, i ^ hop) for i in range(count)])
            low = (mine // hop) % 2 == 0
            value = jnp.concatenate([jnp.where(low, value, other), jnp.where(low, other, value)])
            hop *= 2
    return value


def tied(*values):
    return lax.optimization_barrier(values)


def in_parts_of(value):
    upper = value.astype(BF)
    rest = value - upper.astype(F32)
    middle = rest.astype(BF)
    lower = (rest - middle.astype(F32)).astype(BF)
    return [upper, middle, lower]


def direct_scatter(value, axis):
    count, mine = lax.axis_size(axis), lax.axis_index(axis)
    total = lax.dynamic_index_in_dim(value, mine, 0, False).astype(F32)
    for back in range(1, count):
        block = lax.dynamic_index_in_dim(value, (mine - back) % count, 0, False)
        total += lax.ppermute(block, axis, [(i, (i - back) % count) for i in range(count)])
    return total


def quad_halves(value, axis):
    half = value.shape[axis] // 2
    first = ring_gather(lax.slice_in_dim(value, 0, half, axis=axis), "x")
    return [first, ring_gather(lax.slice_in_dim(value, half, 2 * half, axis=axis), "y")]


def quad_others(first, second):
    return [ring_gather(first, "y"), ring_gather(second, "x").swapaxes(0, 1)]


def quad_parts(value, axis):
    return quad_others(*quad_halves(value, axis))


def quad_whole(parts):
    return jnp.concatenate(parts, axis=2).reshape(-1, parts[0].shape[-1])


def quad_sums(value):
    value = value.reshape(lax.axis_size("y"), lax.axis_size("x"), -1, value.shape[1])
    half = value.shape[2] // 2
    first = ring_terms(value[:, :, :half], "y")
    return first + ring_terms(value[:, :, half:].swapaxes(0, 1), "x")


def quad_rest(*terms):
    half = len(terms) // 2
    first, second = added(terms[:half]).astype(BF), added(terms[half:]).astype(BF)
    return jnp.concatenate([ring_scatter(first, "x"), ring_scatter(second, "y")], axis=0)


def core_gather(parts):
    both = ring_gather(jnp.concatenate(parts, axis=3), "c")
    return jnp.moveaxis(both, 0, 2).reshape(-1, both.shape[-1])


def line_gather(value):
    both = ring_gather(ring_gather(value, "z"), "c")
    return both.swapaxes(0, 1).reshape(-1, value.shape[1])


def plane_scatter(value):
    value = value.reshape(lax.axis_size("y"), lax.axis_size("x"), 2, -1, value.shape[1])
    value = ring_scatter(value, "c", 2).astype(BF)
    half = value.shape[3] // 2
    first = ring_scatter(ring_scatter(value[..., :half], "y").astype(BF), "x")
    second = ring_scatter(ring_scatter(value[..., half:], "x", 1).astype(BF), "y")
    return jnp.concatenate([first, second], axis=1)


def direct_gather(value, axis):
    count = lax.axis_size(axis)
    hops = [[(i, (i + back) % count) for i in range(count)] for back in range(1, count)]
    return [value] + [lax.ppermute(value, axis, hop) for hop in hops]


def in_order(values, axis):
    count, mine = lax.axis_size(axis), lax.axis_index(axis)
    places = []
    for place in range(count):
        found = values[0]
        for back in range(1, count):
            found = jnp.where((mine - back) % count == place, values[back], found)
        places.append(found)
    return jnp.stack(places)


def core_exchange(value):
    count, core = lax.axis_size("z"), lax.axis_index("c")
    value = value.reshape((count, 2) + value.shape[1:])
    kept = lax.dynamic_index_in_dim(value, core, 1, False)
    other = lax.dynamic_index_in_dim(value, 1 - core, 1, False)
    other = lax.ppermute(other, "c", [(0, 1), (1, 0)])
    first, second = jnp.where(core == 0, kept, other), jnp.where(core == 0, other, kept)
    return jnp.stack([first, second], axis=1)


def line_exchange(value):
    count, mine = lax.axis_size("z"), lax.axis_index("z")
    blocks = [lax.dynamic_index_in_dim(value, (mine - back) % count, 0, False) for back in range(count)]
    got = [blocks[0]]
    for back in range(1, count):
        got.append(lax.ppermute(blocks[back], "z", [(i, (i - back) % count) for i in range(count)]))
    places = []
    for place in range(count):
        found = got[0]
        for back in range(1, count):
            found = jnp.where((mine + back) % count == place, got[back], found)
        places.append(found)
    return jnp.concatenate(places)


def core_terms(value):
    value = value.reshape(lax.axis_size("z"), 2, -1, value.shape[1]).swapaxes(0, 1)
    return ring_terms(value, "c")


def total_of(value):
    for axis in ("c", "x", "y", "z"):
        count = lax.axis_size(axis)
        hop = 1
        while hop < count:
            value = value + lax.ppermute(value, axis, [(i, i ^ hop) for i in range(count)])
            hop *= 2
    return value


def normalize(value):
    factor = lax.rsqrt(jnp.mean(value * value, axis=-1, keepdims=True) + EPS_NORM)
    return (value * factor, factor)


def norm_back(grad_normed, normed, factor):
    return factor * (grad_normed - normed * jnp.mean(grad_normed * normed, axis=-1, keepdims=True))


def silu(value):
    return value * jax.nn.sigmoid(value)


def silu_grad(value):
    sig = jax.nn.sigmoid(value)
    return sig * (1.0 + value * (1.0 - sig))


def adam_step(weight, first, second, grad, rate, decay_w):
    first_new = BETA_ONE * first + (1.0 - BETA_ONE) * grad
    second_new = BETA_TWO * second + (1.0 - BETA_TWO) * grad * grad
    scale_one, scale_two = 1.0 / (1.0 - BETA_ONE**STEP), 1.0 / (1.0 - BETA_TWO**STEP)
    step_size = (first_new * scale_one) / (jnp.sqrt(second_new * scale_two) + ADAM_EPS)
    return (weight - rate * (step_size + decay_w * weight), first_new, second_new)


def shifted(value, hop, fill, row, later):
    size = value.shape[0]
    moved = pltpu.roll(value, size - hop if later else hop, 0)
    inside = row < size - hop if later else row >= hop
    return jnp.where(inside, moved, fill)


def tile_scan(coeff, value, row, later):
    hop = 1
    while hop < value.shape[0]:
        value = coeff * shifted(value, hop, 0.0, row, later) + value
        coeff = coeff * shifted(coeff, hop, 1.0, row, later)
        hop *= 2
    return coeff, value


def gates(forget_proj, gap, started):
    sig_neg = jax.nn.sigmoid(-forget_proj)
    keep = gap * sig_neg
    return sig_neg, keep, jnp.where(started > 0.0, 0.0, 1.0 - keep)


def scan_forward(proj_ref, started_ref, gap_ref, state_ref, squares_ref):
    rows, width = state_ref.shape
    row = lax.broadcasted_iota(jnp.int32, (TILE, width), 0)
    gap = gap_ref[...]

    def step(index, carry):
        place = pl.ds(pl.multiple_of(index * TILE, TILE), TILE)
        in_proj = proj_ref[place, pl.ds(0, width)]
        forget_proj = proj_ref[place, pl.ds(width, width)]
        _, keep, decay = gates(forget_proj, gap, started_ref[place, :])
        coeff, value = tile_scan(decay, silu(in_proj) * keep, row, False)
        state = value + coeff * carry
        state_ref[place, :] = state
        squares_ref[place, :] = jnp.sum(state * state, axis=-1, keepdims=True)
        return state[TILE - 1 :, :]

    lax.fori_loop(0, rows // TILE, step, jnp.zeros((1, width), F32), unroll=4)


def scan_backward(
    proj_ref, state_ref, d_mixed_ref, riders_ref, started_ref, gap_ref, gain_ref, d_proj_ref, mixed_ref
):
    rows, width = state_ref.shape
    row = lax.broadcasted_iota(jnp.int32, (TILE, width), 0)
    lane = lax.broadcasted_iota(jnp.int32, (2 * TILE, 128), 1)
    gap, gain = gap_ref[...], gain_ref[...]

    def located(index):
        return pl.ds(pl.multiple_of(index * TILE, TILE), TILE)

    def one(index, mean, factor, carry):
        place = located(index)
        before = located(jnp.maximum(index - 1, 0))
        in_proj = proj_ref[place, pl.ds(0, width)]
        forget_proj = proj_ref[place, pl.ds(width, width)]
        gate_proj = proj_ref[place, pl.ds(2 * width, width)]
        started = started_ref[place, :]
        sig_neg, keep, decay = gates(forget_proj, gap, started)
        state, d_mixed = state_ref[place, :], d_mixed_ref[place, :]
        normed = state * factor
        sig_gate = jax.nn.sigmoid(gate_proj)
        gain_act = gain * (gate_proj * sig_gate)
        d_gate = d_mixed * normed * gain * (sig_gate * (1.0 + gate_proj * (1.0 - sig_gate)))
        d_state = factor * (d_mixed * gain_act - normed * mean)
        coeff, value = tile_scan(decay, decay * d_state, row, True)
        passed = value + coeff * carry
        moved = jnp.where(row < TILE - 1, pltpu.roll(passed, TILE - 1, 0), carry)
        d_total = d_state + moved
        last = state_ref[before, :][TILE - 1 :, :]
        previous = jnp.where(row >= 1, pltpu.roll(state, 1, 0), last)
        previous = jnp.where(started > 0.0, 0.0, previous)
        sig = jax.nn.sigmoid(in_proj)
        d_in = d_total * keep * (sig * (1.0 + in_proj * (1.0 - sig)))
        d_keep = d_total * (in_proj * sig) - d_total * previous
        d_forget = -d_keep * gap * sig_neg * (1.0 - sig_neg)
        return [d_in, d_forget, d_gate, normed * gain_act], passed[:1, :]

    def step(count, carry):
        pair = rows // (2 * TILE) - 1 - count
        place = pl.ds(pl.multiple_of(pair * 2 * TILE, 2 * TILE), 2 * TILE)
        riders = riders_ref[place, :].astype(F32)
        mean = jnp.sum(jnp.where(lane < 3, riders, 0.0), axis=1, keepdims=True)
        factor = jnp.sum(jnp.where(lane < 3, 0.0, riders), axis=1, keepdims=True)
        late, carry = one(2 * pair + 1, mean[TILE:], factor[TILE:], carry)
        early, carry = one(2 * pair, mean[:TILE], factor[:TILE], carry)
        both = [jnp.concatenate(parts, axis=0).astype(BF) for parts in zip(early, late)]
        for kind in range(3):
            d_proj_ref[place, pl.ds(kind * width, width)] = both[kind]
        mixed_ref[place, :] = both[3]
        return carry

    lax.fori_loop(0, rows // (2 * TILE), step, jnp.zeros((1, width), F32), unroll=2)


def run_forward(proj, started, gap):
    rows, width = proj.shape[0], gap.shape[1]
    return pl.pallas_call(
        scan_forward,
        out_shape=[
            jax.ShapeDtypeStruct((rows, width), F32),
            jax.ShapeDtypeStruct((rows, 1), F32),
        ],
        compiler_params=pltpu.CompilerParams(vmem_limit_bytes=48 * 2**20),
    )(proj, started, gap)


def run_backward(proj, state, d_mixed, riders, started, gap, gain):
    rows, width = state.shape
    return pl.pallas_call(
        scan_backward,
        out_shape=[
            jax.ShapeDtypeStruct((rows, 3 * width), BF),
            jax.ShapeDtypeStruct((rows, width), BF),
        ],
        compiler_params=pltpu.CompilerParams(vmem_limit_bytes=48 * 2**20),
    )(proj, state, d_mixed, riders, started, gap, gain)


def adam_rows(clip_ref, weight_ref, first_ref, second_ref, grad_ref, *new_refs):
    clip = clip_ref[0, 0]
    for kind in range(weight_ref.shape[1]):
        moved = adam_step(
            weight_ref[:, kind, :],
            first_ref[:, kind, :],
            second_ref[:, kind, :],
            clip * grad_ref[kind].astype(F32),
            RATE_MATRIX,
            DECAY_WEIGHT,
        )
        for new_ref, value in zip(new_refs, moved):
            new_ref[:, kind, :] = value


def run_adam(weight, first, second, grad, clip):
    own, kinds, width = weight.shape
    rows = min(own, 16)
    rest = pl.BlockSpec((rows, kinds, width), lambda i: (i, 0, 0))
    return pl.pallas_call(
        adam_rows,
        grid=(own // rows,),
        in_specs=[pl.BlockSpec(memory_space=pltpu.SMEM), rest, rest, rest]
        + [pl.BlockSpec((kinds, rows, width), lambda i: (0, i, 0))],
        out_specs=[rest] * 3,
        out_shape=[jax.ShapeDtypeStruct(weight.shape, F32)] * 3,
        compiler_params=pltpu.CompilerParams(vmem_limit_bytes=48 * 2**20),
    )(clip.reshape(1, 1), weight, first, second, grad)


def pack(weight_ref, sent_ref, low_ref):
    spots, own, packed = sent_ref.shape
    planes = packed // (3 * own)
    low_half = lax.broadcasted_iota(jnp.int32, (own, 2 * own), 1) < own
    for kind in range(3):
        for pair in range(0, spots, 2):
            for plane in range(0, planes, 2):
                places = [pl.ds(((plane + i) * spots + pair) * own, 2 * own) for i in range(2)]
                near, far = [weight_ref[:, kind, place] for place in places]
                low_ref[kind, :, places[0]] = near.astype(BF)
                low_ref[kind, :, places[1]] = far.astype(BF)
                at = pl.ds((kind * planes + plane) * own, 2 * own)
                even = jnp.where(low_half, near, pltpu.roll(far, own, 1))
                odd = jnp.where(low_half, pltpu.roll(near, own, 1), far)
                sent_ref[pair, :, at] = even.astype(BF)
                sent_ref[pair + 1, :, at] = odd.astype(BF)
    low_ref[3, :, :] = weight_ref[:, 3, :].astype(BF)


def run_pack(weight, planes, spots):
    own, _, width = weight.shape
    if 2 * own != 128 or planes % 2 != 0:
        low = weight.astype(BF)
        sent = low[:, :3, :].reshape(own, 3, planes, spots, own).transpose(3, 0, 1, 2, 4)
        return sent.reshape(spots, own, 3 * planes * own), low.swapaxes(0, 1)
    return pl.pallas_call(
        pack,
        out_shape=[
            jax.ShapeDtypeStruct((spots, own, 3 * planes * own), BF),
            jax.ShapeDtypeStruct((4, own, width), BF),
        ],
        compiler_params=pltpu.CompilerParams(vmem_limit_bytes=48 * 2**20),
    )(weight)


def settle(got_ref, out_ref, low_ref, grad_ref, first_ref, inner_ref, total_ref):
    spots, own, packed = got_ref.shape
    width = out_ref.shape[1]
    planes = packed // (3 * own)
    low_half = lax.broadcasted_iota(jnp.int32, (own, 2 * own), 1) < own
    total = jnp.zeros((own, 2 * own), F32)
    first, inner = total, total
    for pair in range(0, spots, 2):
        for kind in range(3):
            for plane in range(0, planes, 2):
                at = pl.ds((kind * planes + plane) * own, 2 * own)
                even = got_ref[pair, :, at].astype(F32)
                odd = got_ref[pair + 1, :, at].astype(F32)
                near = jnp.where(low_half, even, pltpu.roll(odd, own, 1))
                far = jnp.where(low_half, pltpu.roll(even, own, 1), odd)
                for step, grad in enumerate((near, far)):
                    place = pl.ds(((plane + step) * spots + pair) * own, 2 * own)
                    grad_ref[kind, :, place] = grad
                    total += grad * grad
                    first += grad * low_ref[kind, :, place].astype(F32)
    for start in range(0, width, 2 * own):
        place = pl.ds(start, 2 * own)
        grad = out_ref[:, place].astype(F32)
        grad_ref[3, :, place] = grad
        total += grad * grad
        inner += grad * low_ref[3, :, place].astype(F32)
    first_ref[...] = jnp.sum(first, axis=1, keepdims=True)
    inner_ref[...] = jnp.sum(inner, axis=1, keepdims=True)
    total_ref[...] = jnp.sum(total, axis=1, keepdims=True)


def run_settle(got, shard_out, low_mixer):
    spots, own, packed = got.shape
    width = shard_out.shape[1]
    planes = packed // (3 * own)
    if 2 * own != 128 or planes % 2 != 0:
        grad = got.reshape(spots, own, 3, planes, own).transpose(1, 2, 3, 0, 4)
        grad = jnp.concatenate([grad.reshape(own, 3, width), shard_out[:, None, :]], axis=1)
        grad = grad.astype(F32)
        product = jnp.sum(grad * low_mixer.swapaxes(0, 1).astype(F32), axis=2)
        squares = jnp.sum(grad * grad, axis=(1, 2))
        return grad.swapaxes(0, 1), jnp.sum(product[:, :3], axis=1), product[:, 3], squares
    column = jax.ShapeDtypeStruct((own, 1), F32)
    grad, *sums = pl.pallas_call(
        settle,
        out_shape=[jax.ShapeDtypeStruct((4, own, width), F32)] + [column] * 3,
        compiler_params=pltpu.CompilerParams(vmem_limit_bytes=48 * 2**20),
    )(got, shard_out, low_mixer)
    return [grad] + [column[:, 0] for column in sums]


def column_blocks(width, first, second):
    size = width // (first * second)
    for i in range(first):
        for j in range(second):
            yield pl.ds((i * second + j) * size, size), pl.ds((j * first + i) * size, size)


def enter_glu(order, mix_ref, x_ref, gain_ref, after_ref, n2_ref, mid_ref, home_ref):
    width = x_ref.shape[1]
    squares = jnp.sum(mix_ref[:, width:].astype(F32), axis=1, keepdims=True)
    home = lax.rsqrt(squares / width + EPS_NORM)
    after = x_ref[...].astype(F32) + mix_ref[:, :width].astype(F32) * home
    mid = lax.rsqrt(jnp.mean(after * after, axis=1, keepdims=True) + EPS_NORM)
    after_ref[...] = after
    mid_ref[...] = mid
    home_ref[...] = home
    n2 = (after * mid * gain_ref[...]).astype(BF)
    for source, target in column_blocks(width, *order):
        n2_ref[:, target] = n2[:, source.start : source.start + source.size]


def leave_glu(
    order, d_n2_ref, cot_ref, after_ref, mid_ref, mix_ref, home_ref, gain_ref, d_mid_ref, out_ref, held_ref
):
    width = cot_ref.shape[1]
    mid, home = mid_ref[...], home_ref[...]
    for target, source in column_blocks(width, *order):
        held_ref[:, target] = d_n2_ref[:, source].astype(F32) * gain_ref[:, target]
    normed = after_ref[...] * mid
    grad = held_ref[...]
    inner = jnp.mean(grad * normed, axis=1, keepdims=True)
    d_mid = cot_ref[...].astype(F32) + mid * (grad - normed * inner)
    d_mid_ref[...] = d_mid
    low = d_mid.astype(BF)
    out_ref[:, :width] = low
    mean = jnp.sum(low.astype(F32) * (mix_ref[:, :width].astype(F32) * home), axis=1, keepdims=True) / width
    lane = lax.broadcasted_iota(jnp.int32, (mid.shape[0], 128), 1)
    riders = jnp.zeros((mid.shape[0], 128), F32)
    for at, value in ((0, mean), (3, home)):
        for part in range(3):
            upper = value.astype(BF).astype(F32)
            riders = jnp.where(lane == at + part, upper, riders)
            value = value - upper
    out_ref[:, width:] = riders.astype(BF)


def run_enter(mix_raw, tokens, gain, order):
    rows, width = tokens.shape
    if width // (order[0] * order[1]) % 128 != 0:
        squares = jnp.sum(mix_raw[:, width:].astype(F32), axis=1, keepdims=True)
        home = lax.rsqrt(squares / width + EPS_NORM)
        after = tokens.astype(F32) + mix_raw[:, :width].astype(F32) * home
        normed, mid = normalize(after)
        n2 = (normed * gain).astype(BF).reshape(rows, *order, -1).swapaxes(1, 2)
        return after, n2.reshape(rows, width), mid, home
    column = jax.ShapeDtypeStruct((rows, 1), F32)
    return pl.pallas_call(
        functools.partial(enter_glu, order),
        out_shape=[
            jax.ShapeDtypeStruct((rows, width), F32),
            jax.ShapeDtypeStruct((rows, width), BF),
            column,
            column,
        ],
        compiler_params=pltpu.CompilerParams(vmem_limit_bytes=48 * 2**20),
    )(mix_raw, tokens, gain)


def run_leave(d_n2, cot, after, mid, mix_raw, home, gain, order):
    rows, width = cot.shape
    if width // (order[0] * order[1]) % 128 != 0:
        grad = d_n2.reshape(rows, order[1], order[0], -1).swapaxes(1, 2).reshape(rows, width)
        d_mid = cot.astype(F32) + norm_back(grad.astype(F32) * gain, after * mid, mid)
        low = d_mid.astype(BF)
        mix = mix_raw[:, :width].astype(F32) * home
        mean = jnp.sum(low.astype(F32) * mix, axis=1, keepdims=True) / width
        riders = jnp.concatenate(in_parts_of(mean) + in_parts_of(home), axis=1)
        riders = jnp.pad(riders, ((0, 0), (0, 128 - riders.shape[1])))
        return d_mid, jnp.concatenate([low, riders], axis=1)
    return pl.pallas_call(
        functools.partial(leave_glu, order),
        out_shape=[
            jax.ShapeDtypeStruct((rows, width), F32),
            jax.ShapeDtypeStruct((rows, width + 128), BF),
        ],
        scratch_shapes=[pltpu.VMEM((rows, width), F32)],
        compiler_params=pltpu.CompilerParams(vmem_limit_bytes=48 * 2**20),
    )(d_n2, cot, after, mid, mix_raw, home, gain)


def shards(
    tokens,
    cotangent,
    lengths,
    lower_bound,
    mixer_w,
    mlp_in,
    mlp_down,
    gains,
    mixer_m,
    mixer_v,
    in_m,
    in_v,
    down_m,
    down_v,
    gain_m,
    gain_v,
):
    rows, width = tokens.shape
    own, _, hidden_width = mlp_in.shape
    down_rows = mlp_down.shape[0]
    planes = lax.axis_size("z")
    spots = lax.axis_size(PLANE)
    quads = lax.axis_size(QUAD)
    pairs = lax.axis_size("c")
    group = spots * rows
    spot = lax.axis_index(PLANE)
    chans = planes * own

    ends = jnp.cumsum(lengths)
    starts = ends - lengths
    places = jnp.arange(group, dtype=jnp.int32)
    started = jnp.any(places[:, None] == starts[None, :], axis=-1, keepdims=True).astype(F32)
    home = spot * rows + jnp.arange(rows, dtype=jnp.int32)
    valid = (home < ends[-1]).astype(F32)

    cot_low = (cotangent.astype(F32) * valid[:, None]).astype(BF)

    w_out = gather(mixer_w[:, 3, :].astype(BF), "z")
    sent, low_mixer = run_pack(mixer_w, planes, spots)
    part = exchange(sent, PLANE).reshape(spots * own, 3 * chans)
    low_in = mlp_in.astype(BF)
    inner = quads * down_rows
    sent_in = low_in.reshape(own, 2, planes, quads, pairs, down_rows).transpose(2, 4, 0, 1, 3, 5)
    sent_in = sent_in.reshape(planes * pairs, own, 2 * inner)
    part, w_out, x_low, low_gains, low_down, sent_in = tied(
        part, w_out, tokens, gains, mlp_down, sent_in
    )
    x_parts = quad_parts(x_low, 1)
    full_gains = double_gather(low_gains).swapaxes(0, 1).reshape(3, width)
    w_down = quad_whole(quad_parts(low_down.astype(BF), 0))
    w_proj = gather(part, "z")
    x_all = core_gather(x_parts)

    bound = lower_bound.reshape(planes, spots, own)
    gap = (1.0 - lax.dynamic_index_in_dim(bound, spot, 1, False)).reshape(1, chans)
    gain_mid = full_gains[1].reshape(planes, spots, own)
    gain_mid = lax.dynamic_index_in_dim(gain_mid, spot, 1, False).reshape(1, chans)

    x = tokens.astype(F32)
    x_normed, x_factor = normalize(x)
    n1 = (normalize(x_all.astype(F32))[0] * full_gains[0]).astype(BF)
    blocks_in = core_exchange(sent_in)
    w_proj, w_down, n1, blocks_in, held_cot = tied(w_proj, w_down, n1, blocks_in, cot_low)
    cots = direct_gather(held_cot, "z")
    proj = jnp.dot(n1, w_proj, preferred_element_type=F32)
    proj, blocks_in = tied(proj, blocks_in)
    part_in = line_exchange(blocks_in)
    state, squares = run_forward(proj, started, gap)
    gate_proj = proj[:, 2 * chans :]
    gate_act = silu(gate_proj)
    raw = (state * gain_mid * gate_act).astype(BF)
    lane = jnp.arange(128, dtype=jnp.int32)[None, :]
    upper = squares.astype(BF).astype(F32)
    riders = jnp.where(lane == spot, upper, jnp.where(lane == spots + spot, squares - upper, 0.0))
    raw = jnp.concatenate([raw, riders.astype(BF)], axis=1)
    ride = jnp.pad(jnp.eye(128, dtype=BF), ((chans, 0), (width, 0)))
    w_ride = ride + jnp.pad(w_out, ((0, 128), (0, 128)))
    mix_part = jnp.dot(raw, w_ride, preferred_element_type=F32).astype(BF)
    mix_part, cots[1], cots[-1] = tied(mix_part, cots[1], cots[-1])
    mix_raw, part_in, *cots = tied(scatter(mix_part, PLANE), part_in, *cots)
    cot_all = ring_gather(in_order(cots, "z"), "c").swapaxes(0, 1)
    cot_all = cot_all.reshape(planes * pairs * rows, width)
    w_in = quad_whole(quad_parts(part_in.reshape(planes * pairs * own, 2 * inner), 0))

    order, gain_glu = (planes, quads), full_gains[2].reshape(1, width)
    after_mix, n2_home, mid_factor, home_factor = run_enter(mix_raw, tokens, gain_glu, order)
    n2 = gather(n2_home, LINE)
    gate_up = jnp.dot(n2, w_in, preferred_element_type=F32)
    gate, up_value = gate_up[:, :inner], gate_up[:, inner:]
    silu_gate = silu(gate)
    hidden = (silu_gate * up_value).astype(BF)

    grad_down = lax.dot_general(hidden, cot_all, (((0,), (0,)), ((), ())), preferred_element_type=F32)
    grad_down = grad_down.astype(BF)
    d_hidden = lax.dot_general(cot_all, w_down, (((1,), (1,)), ((), ())), preferred_element_type=F32)
    d_gate = d_hidden * up_value * silu_grad(gate)
    d_up = d_hidden * silu_gate
    d_gate_up = jnp.concatenate([d_gate.astype(BF), d_up.astype(BF)], axis=1)
    d_n2 = lax.dot_general(d_gate_up, w_in, (((1,), (1,)), ((), ())), preferred_element_type=F32)
    d_n2 = scatter(d_n2.astype(BF), LINE)
    grad_in = lax.dot_general(n2, d_gate_up, (((0,), (0,)), ((), ())), preferred_element_type=F32)
    grad_in = grad_in.astype(BF)
    down = jnp.dot(hidden, w_down, preferred_element_type=F32).astype(BF)
    sums_in = quad_sums(grad_in)
    downs = core_terms(down)
    d_n2, grad_down, *held_terms = tied(d_n2, grad_down, *downs, *sums_in)
    downs, sums_in = held_terms[: len(downs)], held_terms[len(downs) :]
    d_mid, d_mix_home = run_leave(
        d_n2, cot_low, after_mix, mid_factor, mix_raw, home_factor, gain_glu, order
    )
    *downs, d_mix_home = tied(*downs, d_mix_home)
    down = direct_scatter(added(downs).astype(BF), "z")
    shard_in = quad_rest(*sums_in).astype(BF)
    d_mix = gather(d_mix_home, PLANE)
    d_mix, shard_in, grad_down, down = tied(d_mix, shard_in, grad_down, down)
    block_out = (after_mix + down).astype(BF)
    shard_down = scatter(grad_down, QUAD).astype(F32)
    got_in = exchange(shard_in.reshape(planes * pairs, own, 2 * inner), LINE)

    d_mixed = lax.dot_general(
        d_mix, w_ride[:chans], (((1,), (1,)), ((), ())), preferred_element_type=F32
    )
    d_proj, mixed_in = run_backward(proj, state, d_mixed, d_mix[:, width:], started, gap, gain_mid)
    grad_out = lax.dot_general(mixed_in, d_mix, (((0,), (0,)), ((), ())), preferred_element_type=F32)
    grad_proj = lax.dot_general(n1, d_proj, (((0,), (0,)), ((), ())), preferred_element_type=F32)
    grad_out = grad_out[:, :width].astype(BF).reshape(planes, spots * own, chans)
    grad_all = jnp.concatenate(
        [grad_proj.astype(BF).reshape(planes, spots * own, 3 * chans), grad_out], axis=2
    )
    grad_all, got_in, held_proj = tied(grad_all, got_in, d_proj)
    shard_all = scatter(grad_all.reshape(planes * spots * own, 4 * chans), "z")
    shard_in = got_in.reshape(planes, pairs, own, 2, quads, down_rows).transpose(3, 2, 0, 4, 1, 5)
    shard_in = shard_in.reshape(2, own, hidden_width)
    wide_in = shard_in.astype(F32)
    gain_in = jnp.sum(wide_in * low_in.swapaxes(0, 1).astype(F32), axis=(0, 2))
    total_early = jnp.sum(wide_in * wide_in) + jnp.sum(shard_down * shard_down)
    d_n1 = lax.dot_general(held_proj, w_proj, (((1,), (1,)), ((), ())), preferred_element_type=F32)
    d_n1 = plane_scatter(d_n1.astype(BF))
    input_grad = d_mid + norm_back(d_n1 * full_gains[0], x_normed, x_factor)
    shard_all, shard_in, shard_down, gain_in, total_early, input_grad = tied(
        shard_all, shard_in, shard_down, gain_in, total_early, input_grad
    )
    got_proj = exchange(shard_all[:, : 3 * chans].reshape(spots, own, 3 * chans), PLANE)
    shard_out = shard_all[:, 3 * chans :].reshape(own, width)

    shard_mixer, gain_first, gain_inner, total_mixer = run_settle(got_proj, shard_out, low_mixer)
    shard_gains = jnp.stack([gain_first, gain_inner, gain_in]) / gains
    local_total = jnp.sum(total_mixer) + total_early + jnp.sum(shard_gains * shard_gains)
    grad_norm = jnp.sqrt(total_of(local_total.reshape(1, 1))[0, 0])
    clip = jnp.minimum(1.0, CLIP_NORM / (grad_norm + 1e-06))
    new_mixer, new_mixer_m, new_mixer_v = run_adam(mixer_w, mixer_m, mixer_v, shard_mixer, clip)
    new_in, new_in_m, new_in_v = run_adam(mlp_in, in_m, in_v, shard_in, clip)
    new_down, new_down_m, new_down_v = adam_step(
        mlp_down, down_m, down_v, clip * shard_down, RATE_MATRIX, DECAY_WEIGHT
    )
    new_gains, new_gain_m, new_gain_v = adam_step(
        gains, gain_m, gain_v, clip * shard_gains, RATE_GAIN, 0.0
    )
    return (
        block_out,
        input_grad,
        grad_norm,
        new_mixer,
        new_mixer_m,
        new_mixer_v,
        new_in,
        new_in_m,
        new_in_v,
        new_down,
        new_down_m,
        new_down_v,
        new_gains,
        new_gain_m,
        new_gain_v,
    )


def solution(mesh):
    planes, spots = mesh.shape["dp"], mesh.shape["seq"]
    side = math.isqrt(spots // 2)
    split = Mesh(mesh.devices.reshape(planes, spots // (2 * side), side, 2), ALL)
    rows2, rows3, cols = P(ALL, None), P(ALL, None, None), P(None, ALL)
    return jax.shard_map(
        shards,
        mesh=split,
        in_specs=(rows2, rows2, P("z"), P(), rows3, rows3, rows2, cols)
        + (rows3,) * 4
        + (rows2,) * 2
        + (cols,) * 2,
        out_specs=(rows2, rows2, P()) + (rows3,) * 6 + (rows2,) * 3 + (cols,) * 3,
        check_vma=False,
    )
```

```python
import functools
import math

import jax
import jax.numpy as jnp
from jax import lax
from jax.experimental import pallas as pl
from jax.experimental.pallas import tpu as pltpu
from jax.sharding import Mesh, PartitionSpec as P

STEP = 10


EPS_NORM = 1e-06
BETA_ONE = 0.9
BETA_TWO = 0.999
ADAM_EPS = 1e-08
RATE_MATRIX = 0.03
RATE_GAIN = 0.5
DECAY_WEIGHT = 0.1
CLIP_NORM = 1.0

ALL = ("z", "y", "x", "c")
PLANE = ("y", "x", "c")
LINE = ("z", "c")
QUAD = ("y", "x")
TILE = 8
BF = jnp.bfloat16
F32 = jnp.float32


def gather(value, axes):
    return lax.all_gather(value, axes, axis=0, tiled=True)


def scatter(value, axes):
    return lax.psum_scatter(value, axes, scatter_dimension=0, tiled=True)


def exchange(value, axes):
    return lax.all_to_all(value, axes, 0, 0, tiled=True)


def ring_gather(value, axis):
    count, mine = lax.axis_size(axis), lax.axis_index(axis)
    if count == 2:
        other = lax.ppermute(value, axis, [(0, 1), (1, 0)])
        return jnp.stack([jnp.where(mine == 0, value, other), jnp.where(mine == 0, other, value)])
    up, down, ups, downs = value, value, [], []
    for hop in range(1, count):
        up = lax.ppermute(up, axis, [(i, i + 1) for i in range(hop - 1, count - 1)])
        down = lax.ppermute(down, axis, [(i, i - 1) for i in range(1, count - hop + 1)])
        ups.append(up)
        downs.append(down)
    places = []
    for place in range(count):
        found = value
        for back in range(1, count):
            if place + back < count:
                found = jnp.where(mine == place + back, ups[back - 1], found)
            if place >= back:
                found = jnp.where(mine == place - back, downs[back - 1], found)
        places.append(found)
    return jnp.stack(places)


def added(terms):
    return sum(term.astype(F32) for term in terms)


def ring_scatter(value, axis, dim=0):
    return added(ring_terms(value, axis, dim))


def ring_terms(value, axis, dim=0):
    count, mine = lax.axis_size(axis), lax.axis_index(axis)

    def block(back):
        return lax.dynamic_index_in_dim(value, (mine - back) % count, dim, False)

    if count == 2:
        return [block(0), lax.ppermute(block(1), axis, [(0, 1), (1, 0)])]
    up = down = None
    for hop in range(1, count):
        up_sum, down_sum = block(hop), block(count - hop)
        if up is not None:
            up_sum = (up_sum.astype(F32) + up.astype(F32)).astype(BF)
            down_sum = (down_sum.astype(F32) + down.astype(F32)).astype(BF)
        up = lax.ppermute(up_sum, axis, [(i, i + 1) for i in range(hop)])
        down = lax.ppermute(down_sum, axis, [(i, i - 1) for i in range(count - hop, count)])
    return [block(0), up, down]


def double_gather(value):
    value = value[None]
    for axis in ("c", "x", "y", "z"):
        count, mine = lax.axis_size(axis), lax.axis_index(axis)
        hop = 1
        while hop < count:
            other = lax.ppermute(value, axis, [(i, i ^ hop) for i in range(count)])
            low = (mine // hop) % 2 == 0
            value = jnp.concatenate([jnp.where(low, value, other), jnp.where(low, other, value)])
            hop *= 2
    return value


def tied(*values):
    return lax.optimization_barrier(values)


def in_parts_of(value):
    upper = value.astype(BF)
    rest = value - upper.astype(F32)
    middle = rest.astype(BF)
    lower = (rest - middle.astype(F32)).astype(BF)
    return [upper, middle, lower]


def direct_scatter(value, axis):
    count, mine = lax.axis_size(axis), lax.axis_index(axis)
    total = lax.dynamic_index_in_dim(value, mine, 0, False).astype(F32)
    for back in range(1, count):
        block = lax.dynamic_index_in_dim(value, (mine - back) % count, 0, False)
        total += lax.ppermute(block, axis, [(i, (i - back) % count) for i in range(count)])
    return total


def quad_halves(value, axis):
    half = value.shape[axis] // 2
    first = ring_gather(lax.slice_in_dim(value, 0, half, axis=axis), "x")
    return [first, ring_gather(lax.slice_in_dim(value, half, 2 * half, axis=axis), "y")]


def quad_others(first, second):
    return [ring_gather(first, "y"), ring_gather(second, "x").swapaxes(0, 1)]


def quad_parts(value, axis):
    return quad_others(*quad_halves(value, axis))


def quad_whole(parts):
    return jnp.concatenate(parts, axis=2).reshape(-1, parts[0].shape[-1])


def quad_sums(value):
    value = value.reshape(lax.axis_size("y"), lax.axis_size("x"), -1, value.shape[1])
    half = value.shape[2] // 2
    first = ring_terms(value[:, :, :half], "y")
    return first + ring_terms(value[:, :, half:].swapaxes(0, 1), "x")


def quad_rest(*terms):
    half = len(terms) // 2
    first, second = added(terms[:half]).astype(BF), added(terms[half:]).astype(BF)
    return jnp.concatenate([ring_scatter(first, "x"), ring_scatter(second, "y")], axis=0)


def core_gather(parts):
    both = ring_gather(jnp.concatenate(parts, axis=3), "c")
    return jnp.moveaxis(both, 0, 2).reshape(-1, both.shape[-1])


def line_gather(value):
    both = ring_gather(ring_gather(value, "z"), "c")
    return both.swapaxes(0, 1).reshape(-1, value.shape[1])


def plane_scatter(value):
    value = value.reshape(lax.axis_size("y"), lax.axis_size("x"), 2, -1, value.shape[1])
    value = ring_scatter(value, "c", 2).astype(BF)
    half = value.shape[3] // 2
    first = ring_scatter(ring_scatter(value[..., :half], "y").astype(BF), "x")
    second = ring_scatter(ring_scatter(value[..., half:], "x", 1).astype(BF), "y")
    return jnp.concatenate([first, second], axis=1)


def direct_gather(value, axis):
    count = lax.axis_size(axis)
    hops = [[(i, (i + back) % count) for i in range(count)] for back in range(1, count)]
    return [value] + [lax.ppermute(value, axis, hop) for hop in hops]


def in_order(values, axis):
    count, mine = lax.axis_size(axis), lax.axis_index(axis)
    places = []
    for place in range(count):
        found = values[0]
        for back in range(1, count):
            found = jnp.where((mine - back) % count == place, values[back], found)
        places.append(found)
    return jnp.stack(places)


def core_exchange(value):
    count, core = lax.axis_size("z"), lax.axis_index("c")
    value = value.reshape((count, 2) + value.shape[1:])
    kept = lax.dynamic_index_in_dim(value, core, 1, False)
    other = lax.dynamic_index_in_dim(value, 1 - core, 1, False)
    other = lax.ppermute(other, "c", [(0, 1), (1, 0)])
    first, second = jnp.where(core == 0, kept, other), jnp.where(core == 0, other, kept)
    return jnp.stack([first, second], axis=1)


def line_exchange(value):
    count, mine = lax.axis_size("z"), lax.axis_index("z")
    blocks = [lax.dynamic_index_in_dim(value, (mine - back) % count, 0, False) for back in range(count)]
    got = [blocks[0]]
    for back in range(1, count):
        got.append(lax.ppermute(blocks[back], "z", [(i, (i - back) % count) for i in range(count)]))
    places = []
    for place in range(count):
        found = got[0]
        for back in range(1, count):
            found = jnp.where((mine + back) % count == place, got[back], found)
        places.append(found)
    return jnp.concatenate(places)


def core_terms(value):
    value = value.reshape(lax.axis_size("z"), 2, -1, value.shape[1]).swapaxes(0, 1)
    return ring_terms(value, "c")


def total_of(value, axes):
    for axis in axes:
        count = lax.axis_size(axis)
        hop = 1
        while hop < count:
            value = value + lax.ppermute(value, axis, [(i, i ^ hop) for i in range(count)])
            hop *= 2
    return value


def normalize(value):
    factor = lax.rsqrt(jnp.mean(value * value, axis=-1, keepdims=True) + EPS_NORM)
    return (value * factor, factor)


def norm_back(grad_normed, normed, factor):
    return factor * (grad_normed - normed * jnp.mean(grad_normed * normed, axis=-1, keepdims=True))


def silu(value):
    return value * jax.nn.sigmoid(value)


def silu_grad(value):
    sig = jax.nn.sigmoid(value)
    return sig * (1.0 + value * (1.0 - sig))


def adam_step(weight, first, second, grad, rate, decay_w):
    first_new = BETA_ONE * first + (1.0 - BETA_ONE) * grad
    second_new = BETA_TWO * second + (1.0 - BETA_TWO) * grad * grad
    scale_one, scale_two = 1.0 / (1.0 - BETA_ONE**STEP), 1.0 / (1.0 - BETA_TWO**STEP)
    step_size = (first_new * scale_one) / (jnp.sqrt(second_new * scale_two) + ADAM_EPS)
    return (weight - rate * (step_size + decay_w * weight), first_new, second_new)


def shifted(value, hop, fill, row, later):
    size = value.shape[0]
    moved = pltpu.roll(value, size - hop if later else hop, 0)
    inside = row < size - hop if later else row >= hop
    return jnp.where(inside, moved, fill)


def tile_scan(coeff, value, row, later):
    hop = 1
    while hop < value.shape[0]:
        value = coeff * shifted(value, hop, 0.0, row, later) + value
        coeff = coeff * shifted(coeff, hop, 1.0, row, later)
        hop *= 2
    return coeff, value


def gates(forget_proj, gap, started):
    sig_neg = jax.nn.sigmoid(-forget_proj)
    keep = gap * sig_neg
    return sig_neg, keep, jnp.where(started > 0.0, 0.0, 1.0 - keep)


def scan_forward(proj_ref, started_ref, gap_ref, state_ref, squares_ref):
    rows, width = state_ref.shape
    row = lax.broadcasted_iota(jnp.int32, (TILE, width), 0)
    gap = gap_ref[...]

    def step(index, carry):
        place = pl.ds(pl.multiple_of(index * TILE, TILE), TILE)
        in_proj = proj_ref[place, pl.ds(0, width)]
        forget_proj = proj_ref[place, pl.ds(width, width)]
        _, keep, decay = gates(forget_proj, gap, started_ref[place, :])
        coeff, value = tile_scan(decay, silu(in_proj) * keep, row, False)
        state = value + coeff * carry
        state_ref[place, :] = state
        squares_ref[place, :] = jnp.sum(state * state, axis=-1, keepdims=True)
        return state[TILE - 1 :, :]

    lax.fori_loop(0, rows // TILE, step, jnp.zeros((1, width), F32), unroll=4)


def scan_backward(
    proj_ref, state_ref, d_mixed_ref, riders_ref, started_ref, gap_ref, gain_ref, d_proj_ref, mixed_ref
):
    rows, width = state_ref.shape
    row = lax.broadcasted_iota(jnp.int32, (TILE, width), 0)
    lane = lax.broadcasted_iota(jnp.int32, (2 * TILE, 128), 1)
    gap, gain = gap_ref[...], gain_ref[...]

    def located(index):
        return pl.ds(pl.multiple_of(index * TILE, TILE), TILE)

    def one(index, mean, factor, carry):
        place = located(index)
        before = located(jnp.maximum(index - 1, 0))
        in_proj = proj_ref[place, pl.ds(0, width)]
        forget_proj = proj_ref[place, pl.ds(width, width)]
        gate_proj = proj_ref[place, pl.ds(2 * width, width)]
        started = started_ref[place, :]
        sig_neg, keep, decay = gates(forget_proj, gap, started)
        state, d_mixed = state_ref[place, :], d_mixed_ref[place, :]
        normed = state * factor
        sig_gate = jax.nn.sigmoid(gate_proj)
        gain_act = gain * (gate_proj * sig_gate)
        d_gate = d_mixed * normed * gain * (sig_gate * (1.0 + gate_proj * (1.0 - sig_gate)))
        d_state = factor * (d_mixed * gain_act - normed * mean)
        coeff, value = tile_scan(decay, decay * d_state, row, True)
        passed = value + coeff * carry
        moved = jnp.where(row < TILE - 1, pltpu.roll(passed, TILE - 1, 0), carry)
        d_total = d_state + moved
        last = state_ref[before, :][TILE - 1 :, :]
        previous = jnp.where(row >= 1, pltpu.roll(state, 1, 0), last)
        previous = jnp.where(started > 0.0, 0.0, previous)
        sig = jax.nn.sigmoid(in_proj)
        d_in = d_total * keep * (sig * (1.0 + in_proj * (1.0 - sig)))
        d_keep = d_total * (in_proj * sig) - d_total * previous
        d_forget = -d_keep * gap * sig_neg * (1.0 - sig_neg)
        return [d_in, d_forget, d_gate, normed * gain_act], passed[:1, :]

    def step(count, carry):
        pair = rows // (2 * TILE) - 1 - count
        place = pl.ds(pl.multiple_of(pair * 2 * TILE, 2 * TILE), 2 * TILE)
        riders = riders_ref[place, :].astype(F32)
        mean = jnp.sum(jnp.where(lane < 3, riders, 0.0), axis=1, keepdims=True)
        factor = jnp.sum(jnp.where(lane < 3, 0.0, riders), axis=1, keepdims=True)
        late, carry = one(2 * pair + 1, mean[TILE:], factor[TILE:], carry)
        early, carry = one(2 * pair, mean[:TILE], factor[:TILE], carry)
        both = [jnp.concatenate(parts, axis=0).astype(BF) for parts in zip(early, late)]
        for kind in range(3):
            d_proj_ref[place, pl.ds(kind * width, width)] = both[kind]
        mixed_ref[place, :] = both[3]
        return carry

    lax.fori_loop(0, rows // (2 * TILE), step, jnp.zeros((1, width), F32), unroll=2)


def run_forward(proj, started, gap):
    rows, width = proj.shape[0], gap.shape[1]
    return pl.pallas_call(
        scan_forward,
        out_shape=[
            jax.ShapeDtypeStruct((rows, width), F32),
            jax.ShapeDtypeStruct((rows, 1), F32),
        ],
        compiler_params=pltpu.CompilerParams(vmem_limit_bytes=48 * 2**20),
    )(proj, started, gap)


def run_backward(proj, state, d_mixed, riders, started, gap, gain):
    rows, width = state.shape
    return pl.pallas_call(
        scan_backward,
        out_shape=[
            jax.ShapeDtypeStruct((rows, 3 * width), BF),
            jax.ShapeDtypeStruct((rows, width), BF),
        ],
        compiler_params=pltpu.CompilerParams(vmem_limit_bytes=48 * 2**20),
    )(proj, state, d_mixed, riders, started, gap, gain)


def adam_rows(clip_ref, weight_ref, first_ref, second_ref, grad_ref, *new_refs):
    clip = clip_ref[0, 0]
    for kind in range(weight_ref.shape[1]):
        moved = adam_step(
            weight_ref[:, kind, :],
            first_ref[:, kind, :],
            second_ref[:, kind, :],
            clip * grad_ref[kind].astype(F32),
            RATE_MATRIX,
            DECAY_WEIGHT,
        )
        for new_ref, value in zip(new_refs, moved):
            new_ref[:, kind, :] = value


def run_adam(weight, first, second, grad, clip):
    own, kinds, width = weight.shape
    rows = min(own, 16)
    rest = pl.BlockSpec((rows, kinds, width), lambda i: (i, 0, 0))
    return pl.pallas_call(
        adam_rows,
        grid=(own // rows,),
        in_specs=[pl.BlockSpec(memory_space=pltpu.SMEM), rest, rest, rest]
        + [pl.BlockSpec((kinds, rows, width), lambda i: (0, i, 0))],
        out_specs=[rest] * 3,
        out_shape=[jax.ShapeDtypeStruct(weight.shape, F32)] * 3,
        compiler_params=pltpu.CompilerParams(vmem_limit_bytes=48 * 2**20),
    )(clip.reshape(1, 1), weight, first, second, grad)


def pack(weight_ref, sent_ref, low_ref):
    spots, own, packed = sent_ref.shape
    planes = packed // (3 * own)
    low_half = lax.broadcasted_iota(jnp.int32, (own, 2 * own), 1) < own
    for kind in range(3):
        for pair in range(0, spots, 2):
            for plane in range(0, planes, 2):
                places = [pl.ds(((plane + i) * spots + pair) * own, 2 * own) for i in range(2)]
                near, far = [weight_ref[:, kind, place] for place in places]
                low_ref[kind, :, places[0]] = near.astype(BF)
                low_ref[kind, :, places[1]] = far.astype(BF)
                at = pl.ds((kind * planes + plane) * own, 2 * own)
                even = jnp.where(low_half, near, pltpu.roll(far, own, 1))
                odd = jnp.where(low_half, pltpu.roll(near, own, 1), far)
                sent_ref[pair, :, at] = even.astype(BF)
                sent_ref[pair + 1, :, at] = odd.astype(BF)
    low_ref[3, :, :] = weight_ref[:, 3, :].astype(BF)


def run_pack(weight, planes, spots):
    own, _, width = weight.shape
    if 2 * own != 128 or planes % 2 != 0:
        low = weight.astype(BF)
        sent = low[:, :3, :].reshape(own, 3, planes, spots, own).transpose(3, 0, 1, 2, 4)
        return sent.reshape(spots, own, 3 * planes * own), low.swapaxes(0, 1)
    return pl.pallas_call(
        pack,
        out_shape=[
            jax.ShapeDtypeStruct((spots, own, 3 * planes * own), BF),
            jax.ShapeDtypeStruct((4, own, width), BF),
        ],
        compiler_params=pltpu.CompilerParams(vmem_limit_bytes=48 * 2**20),
    )(weight)


def row_sums(shard_ref, first_ref, inner_ref, sums_ref):
    split = first_ref.shape[1]
    grad = shard_ref[...].astype(F32)
    first = jnp.sum(grad[:, :split] * first_ref[...].astype(F32), axis=1, keepdims=True)
    inner = jnp.sum(grad[:, split:] * inner_ref[...].astype(F32), axis=1, keepdims=True)
    squares = jnp.sum(grad * grad, axis=1, keepdims=True)
    lane = lax.broadcasted_iota(jnp.int32, sums_ref.shape, 1)
    sums_ref[...] = jnp.where(lane == 0, first, jnp.where(lane == 1, inner, squares))


def run_row_sums(shard, first, inner):
    if first.shape[1] % 128 != 0 or inner.shape[1] % 128 != 0:
        grad = shard.astype(F32)
        split = first.shape[1]
        parts = [grad[:, :split] * first.astype(F32), grad[:, split:] * inner.astype(F32), grad * grad]
        return [jnp.sum(part, axis=1) for part in parts]
    sums = pl.pallas_call(
        row_sums,
        out_shape=jax.ShapeDtypeStruct((shard.shape[0], 128), F32),
        compiler_params=pltpu.CompilerParams(vmem_limit_bytes=48 * 2**20),
    )(shard, first, inner)
    return [sums[:, column] for column in range(3)]


def settle(got_ref, out_ref, grad_ref):
    spots, own, packed = got_ref.shape
    planes = packed // (3 * own)
    low_half = lax.broadcasted_iota(jnp.int32, (own, 2 * own), 1) < own
    for pair in range(0, spots, 2):
        for kind in range(3):
            for plane in range(0, planes, 2):
                at = pl.ds((kind * planes + plane) * own, 2 * own)
                even = got_ref[pair, :, at].astype(F32)
                odd = got_ref[pair + 1, :, at].astype(F32)
                near = jnp.where(low_half, even, pltpu.roll(odd, own, 1))
                far = jnp.where(low_half, pltpu.roll(even, own, 1), odd)
                for step, grad in enumerate((near, far)):
                    grad_ref[kind, :, pl.ds(((plane + step) * spots + pair) * own, 2 * own)] = grad
    grad_ref[3, :, :] = out_ref[...].astype(F32)


def run_settle(got, shard_out):
    spots, own, packed = got.shape
    width = shard_out.shape[1]
    planes = packed // (3 * own)
    if 2 * own != 128 or planes % 2 != 0:
        grad = got.reshape(spots, own, 3, planes, own).transpose(2, 1, 3, 0, 4).reshape(3, own, width)
        return jnp.concatenate([grad, shard_out[None]], axis=0).astype(F32)
    return pl.pallas_call(
        settle,
        out_shape=jax.ShapeDtypeStruct((4, own, width), F32),
        compiler_params=pltpu.CompilerParams(vmem_limit_bytes=48 * 2**20),
    )(got, shard_out)


def column_blocks(width, first, second):
    size = width // (first * second)
    for i in range(first):
        for j in range(second):
            yield pl.ds((i * second + j) * size, size), pl.ds((j * first + i) * size, size)


def enter_glu(order, mix_ref, x_ref, gain_ref, after_ref, n2_ref, mid_ref, home_ref):
    width = x_ref.shape[1]
    squares = jnp.sum(mix_ref[:, width:].astype(F32), axis=1, keepdims=True)
    home = lax.rsqrt(squares / width + EPS_NORM)
    after = x_ref[...].astype(F32) + mix_ref[:, :width].astype(F32) * home
    mid = lax.rsqrt(jnp.mean(after * after, axis=1, keepdims=True) + EPS_NORM)
    after_ref[...] = after
    mid_ref[...] = mid
    home_ref[...] = home
    n2 = (after * mid * gain_ref[...]).astype(BF)
    for source, target in column_blocks(width, *order):
        n2_ref[:, target] = n2[:, source.start : source.start + source.size]


def leave_glu(
    order, d_n2_ref, cot_ref, after_ref, mid_ref, mix_ref, home_ref, gain_ref, d_mid_ref, out_ref, held_ref
):
    width = cot_ref.shape[1]
    mid, home = mid_ref[...], home_ref[...]
    for target, source in column_blocks(width, *order):
        held_ref[:, target] = d_n2_ref[:, source].astype(F32) * gain_ref[:, target]
    normed = after_ref[...] * mid
    grad = held_ref[...]
    inner = jnp.mean(grad * normed, axis=1, keepdims=True)
    d_mid = cot_ref[...].astype(F32) + mid * (grad - normed * inner)
    d_mid_ref[...] = d_mid
    low = d_mid.astype(BF)
    out_ref[:, :width] = low
    mean = jnp.sum(low.astype(F32) * (mix_ref[:, :width].astype(F32) * home), axis=1, keepdims=True) / width
    lane = lax.broadcasted_iota(jnp.int32, (mid.shape[0], 128), 1)
    riders = jnp.zeros((mid.shape[0], 128), F32)
    for at, value in ((0, mean), (3, home)):
        for part in range(3):
            upper = value.astype(BF).astype(F32)
            riders = jnp.where(lane == at + part, upper, riders)
            value = value - upper
    out_ref[:, width:] = riders.astype(BF)


def run_enter(mix_raw, tokens, gain, order):
    rows, width = tokens.shape
    if width // (order[0] * order[1]) % 128 != 0:
        squares = jnp.sum(mix_raw[:, width:].astype(F32), axis=1, keepdims=True)
        home = lax.rsqrt(squares / width + EPS_NORM)
        after = tokens.astype(F32) + mix_raw[:, :width].astype(F32) * home
        normed, mid = normalize(after)
        n2 = (normed * gain).astype(BF).reshape(rows, *order, -1).swapaxes(1, 2)
        return after, n2.reshape(rows, width), mid, home
    column = jax.ShapeDtypeStruct((rows, 1), F32)
    return pl.pallas_call(
        functools.partial(enter_glu, order),
        out_shape=[
            jax.ShapeDtypeStruct((rows, width), F32),
            jax.ShapeDtypeStruct((rows, width), BF),
            column,
            column,
        ],
        compiler_params=pltpu.CompilerParams(vmem_limit_bytes=48 * 2**20),
    )(mix_raw, tokens, gain)


def run_leave(d_n2, cot, after, mid, mix_raw, home, gain, order):
    rows, width = cot.shape
    if width // (order[0] * order[1]) % 128 != 0:
        grad = d_n2.reshape(rows, order[1], order[0], -1).swapaxes(1, 2).reshape(rows, width)
        d_mid = cot.astype(F32) + norm_back(grad.astype(F32) * gain, after * mid, mid)
        low = d_mid.astype(BF)
        mix = mix_raw[:, :width].astype(F32) * home
        mean = jnp.sum(low.astype(F32) * mix, axis=1, keepdims=True) / width
        riders = jnp.concatenate(in_parts_of(mean) + in_parts_of(home), axis=1)
        riders = jnp.pad(riders, ((0, 0), (0, 128 - riders.shape[1])))
        return d_mid, jnp.concatenate([low, riders], axis=1)
    return pl.pallas_call(
        functools.partial(leave_glu, order),
        out_shape=[
            jax.ShapeDtypeStruct((rows, width), F32),
            jax.ShapeDtypeStruct((rows, width + 128), BF),
        ],
        scratch_shapes=[pltpu.VMEM((rows, width), F32)],
        compiler_params=pltpu.CompilerParams(vmem_limit_bytes=48 * 2**20),
    )(d_n2, cot, after, mid, mix_raw, home, gain)


def shards(
    tokens,
    cotangent,
    lengths,
    lower_bound,
    mixer_w,
    mlp_in,
    mlp_down,
    gains,
    mixer_m,
    mixer_v,
    in_m,
    in_v,
    down_m,
    down_v,
    gain_m,
    gain_v,
):
    rows, width = tokens.shape
    own, _, hidden_width = mlp_in.shape
    down_rows = mlp_down.shape[0]
    planes = lax.axis_size("z")
    spots = lax.axis_size(PLANE)
    quads = lax.axis_size(QUAD)
    pairs = lax.axis_size("c")
    group = spots * rows
    spot = lax.axis_index(PLANE)
    chans = planes * own

    ends = jnp.cumsum(lengths)
    starts = ends - lengths
    places = jnp.arange(group, dtype=jnp.int32)
    started = jnp.any(places[:, None] == starts[None, :], axis=-1, keepdims=True).astype(F32)
    home = spot * rows + jnp.arange(rows, dtype=jnp.int32)
    valid = (home < ends[-1]).astype(F32)

    cot_low = (cotangent.astype(F32) * valid[:, None]).astype(BF)

    w_out = gather(mixer_w[:, 3, :].astype(BF), "z")
    sent, low_mixer = run_pack(mixer_w, planes, spots)
    part = exchange(sent, PLANE).reshape(spots * own, 3 * chans)
    low_in = mlp_in.astype(BF)
    inner = quads * down_rows
    sent_in = low_in.reshape(own, 2, planes, quads, pairs, down_rows).transpose(2, 4, 0, 1, 3, 5)
    sent_in = sent_in.reshape(planes * pairs, own, 2 * inner)
    part, w_out, x_low, low_gains, low_down, sent_in = tied(
        part, w_out, tokens, gains, mlp_down, sent_in
    )
    x_parts = quad_parts(x_low, 1)
    full_gains = double_gather(low_gains).swapaxes(0, 1).reshape(3, width)
    w_down = quad_whole(quad_parts(low_down.astype(BF), 0))
    w_proj = gather(part, "z")
    x_all = core_gather(x_parts)

    bound = lower_bound.reshape(planes, spots, own)
    gap = (1.0 - lax.dynamic_index_in_dim(bound, spot, 1, False)).reshape(1, chans)
    gain_mid = full_gains[1].reshape(planes, spots, own)
    gain_mid = lax.dynamic_index_in_dim(gain_mid, spot, 1, False).reshape(1, chans)

    x = tokens.astype(F32)
    x_normed, x_factor = normalize(x)
    n1 = (normalize(x_all.astype(F32))[0] * full_gains[0]).astype(BF)
    blocks_in = core_exchange(sent_in)
    w_proj, w_down, n1, blocks_in, held_cot = tied(w_proj, w_down, n1, blocks_in, cot_low)
    cots = direct_gather(held_cot, "z")
    proj = jnp.dot(n1, w_proj, preferred_element_type=F32)
    proj, blocks_in = tied(proj, blocks_in)
    part_in = line_exchange(blocks_in)
    state, squares = run_forward(proj, started, gap)
    gate_proj = proj[:, 2 * chans :]
    gate_act = silu(gate_proj)
    raw = (state * gain_mid * gate_act).astype(BF)
    lane = jnp.arange(128, dtype=jnp.int32)[None, :]
    upper = squares.astype(BF).astype(F32)
    riders = jnp.where(lane == spot, upper, jnp.where(lane == spots + spot, squares - upper, 0.0))
    raw = jnp.concatenate([raw, riders.astype(BF)], axis=1)
    ride = jnp.pad(jnp.eye(128, dtype=BF), ((chans, 0), (width, 0)))
    w_ride = ride + jnp.pad(w_out, ((0, 128), (0, 128)))
    mix_part = jnp.dot(raw, w_ride, preferred_element_type=F32).astype(BF)
    mix_part, cots[1], cots[-1] = tied(mix_part, cots[1], cots[-1])
    mix_raw, part_in, *cots = tied(scatter(mix_part, PLANE), part_in, *cots)
    cot_all = ring_gather(in_order(cots, "z"), "c").swapaxes(0, 1)
    cot_all = cot_all.reshape(planes * pairs * rows, width)
    w_in = quad_whole(quad_parts(part_in.reshape(planes * pairs * own, 2 * inner), 0))

    order, gain_glu = (planes, quads), full_gains[2].reshape(1, width)
    after_mix, n2_home, mid_factor, home_factor = run_enter(mix_raw, tokens, gain_glu, order)
    n2 = gather(n2_home, LINE)
    gate_up = jnp.dot(n2, w_in, preferred_element_type=F32)
    gate, up_value = gate_up[:, :inner], gate_up[:, inner:]
    silu_gate = silu(gate)
    hidden = (silu_gate * up_value).astype(BF)

    d_hidden = lax.dot_general(cot_all, w_down, (((1,), (1,)), ((), ())), preferred_element_type=F32)
    d_gate = d_hidden * up_value * silu_grad(gate)
    d_up = d_hidden * silu_gate
    d_gate_up = jnp.concatenate([d_gate.astype(BF), d_up.astype(BF)], axis=1)
    d_n2 = lax.dot_general(d_gate_up, w_in, (((1,), (1,)), ((), ())), preferred_element_type=F32)
    d_n2 = scatter(d_n2.astype(BF), LINE)
    grad_in = lax.dot_general(n2, d_gate_up, (((0,), (0,)), ((), ())), preferred_element_type=F32)
    grad_in = grad_in.astype(BF)
    down = jnp.dot(hidden, w_down, preferred_element_type=F32).astype(BF)
    sums_in = quad_sums(grad_in)
    down, held_hidden = tied(added(core_terms(down)).astype(BF), hidden)
    grad_down = lax.dot_general(
        held_hidden, cot_all, (((0,), (0,)), ((), ())), preferred_element_type=F32
    ).astype(BF)
    d_n2, grad_down, down, *sums_in = tied(d_n2, grad_down, down, *sums_in)
    d_mid, d_mix_home = run_leave(
        d_n2, cot_low, after_mix, mid_factor, mix_raw, home_factor, gain_glu, order
    )
    down = direct_scatter(down, "z")
    shard_in = quad_rest(*sums_in).astype(BF)
    d_mix = gather(d_mix_home, PLANE)
    d_mix, shard_in, grad_down, down = tied(d_mix, shard_in, grad_down, down)
    block_out = (after_mix + down).astype(BF)
    shard_down = scatter(grad_down, QUAD).astype(F32)
    got_in = exchange(shard_in.reshape(planes * pairs, own, 2 * inner), LINE)

    d_mixed = lax.dot_general(
        d_mix, w_ride[:chans], (((1,), (1,)), ((), ())), preferred_element_type=F32
    )
    d_proj, mixed_in = run_backward(proj, state, d_mixed, d_mix[:, width:], started, gap, gain_mid)
    grad_out = lax.dot_general(mixed_in, d_mix, (((0,), (0,)), ((), ())), preferred_element_type=F32)
    grad_proj = lax.dot_general(n1, d_proj, (((0,), (0,)), ((), ())), preferred_element_type=F32)
    grad_out = grad_out[:, :width].astype(BF).reshape(planes, spots * own, chans)
    grad_all = jnp.concatenate(
        [grad_proj.astype(BF).reshape(planes, spots * own, 3 * chans), grad_out], axis=2
    )
    grad_all, got_in, held_proj = tied(grad_all, got_in, d_proj)
    shard_all = scatter(grad_all.reshape(planes * spots * own, 4 * chans), "z")
    shard_in = got_in.reshape(planes, pairs, own, 2, quads, down_rows).transpose(3, 2, 0, 4, 1, 5)
    shard_in = shard_in.reshape(2, own, hidden_width)
    wide_in = shard_in.astype(F32)
    gain_in = jnp.sum(wide_in * low_in.swapaxes(0, 1).astype(F32), axis=(0, 2))
    total_early = jnp.sum(wide_in * wide_in) + jnp.sum(shard_down * shard_down)
    d_n1 = lax.dot_general(held_proj, w_proj, (((1,), (1,)), ((), ())), preferred_element_type=F32)
    d_n1 = plane_scatter(d_n1.astype(BF))
    input_grad = d_mid + norm_back(d_n1 * full_gains[0], x_normed, x_factor)
    plane_rows = spots * own
    first_row = lax.axis_index("z") * plane_rows
    rows_first = lax.dynamic_slice_in_dim(w_proj, first_row, plane_rows)
    rows_inner = low_mixer[3].reshape(plane_rows, chans)
    shard_all, shard_in, shard_down, gain_in, total_early, input_grad, rows_first, rows_inner = tied(
        shard_all, shard_in, shard_down, gain_in, total_early, input_grad, rows_first, rows_inner
    )
    shard_proj = shard_all[:, : 3 * chans]
    got_proj = exchange(shard_proj.reshape(spots, own, 3 * chans), PLANE)
    shard_out = shard_all[:, 3 * chans :].reshape(own, width)

    row_first, row_inner, row_squares = run_row_sums(shard_all, rows_first, rows_inner)
    gain_inner = jnp.sum(row_inner.reshape(own, spots), axis=1) / gains[1]
    gain_in = gain_in / gains[2]
    local_total = jnp.sum(row_squares) + total_early
    local_total += jnp.sum(gain_inner * gain_inner) + jnp.sum(gain_in * gain_in)
    sums = jnp.concatenate(
        [row_first.reshape(spots, own), jnp.full((1, own), local_total)], axis=0
    )
    sums = total_of(sums, ("c", "x", "y"))
    gain_rows = lax.dynamic_slice_in_dim(full_gains[0], first_row, plane_rows).reshape(spots, own)
    gain_first = sums[:spots] / gain_rows
    total = sums[spots:, :1] + jnp.sum(gain_first * gain_first)
    grad_norm = jnp.sqrt(total_of(total, ("z",))[0, 0])
    gain_first = lax.dynamic_index_in_dim(gain_first, spot, 0, False)
    shard_gains = jnp.stack([gain_first, gain_inner, gain_in])
    clip = jnp.minimum(1.0, CLIP_NORM / (grad_norm + 1e-06))
    shard_mixer = run_settle(got_proj, shard_out)
    new_mixer, new_mixer_m, new_mixer_v = run_adam(mixer_w, mixer_m, mixer_v, shard_mixer, clip)
    new_in, new_in_m, new_in_v = run_adam(mlp_in, in_m, in_v, shard_in, clip)
    new_down, new_down_m, new_down_v = adam_step(
        mlp_down, down_m, down_v, clip * shard_down, RATE_MATRIX, DECAY_WEIGHT
    )
    new_gains, new_gain_m, new_gain_v = adam_step(
        gains, gain_m, gain_v, clip * shard_gains, RATE_GAIN, 0.0
    )
    return (
        block_out,
        input_grad,
        grad_norm,
        new_mixer,
        new_mixer_m,
        new_mixer_v,
        new_in,
        new_in_m,
        new_in_v,
        new_down,
        new_down_m,
        new_down_v,
        new_gains,
        new_gain_m,
        new_gain_v,
    )


def solution(mesh):
    planes, spots = mesh.shape["dp"], mesh.shape["seq"]
    side = math.isqrt(spots // 2)
    split = Mesh(mesh.devices.reshape(planes, spots // (2 * side), side, 2), ALL)
    rows2, rows3, cols = P(ALL, None), P(ALL, None, None), P(None, ALL)
    return jax.shard_map(
        shards,
        mesh=split,
        in_specs=(rows2, rows2, P("z"), P(), rows3, rows3, rows2, cols)
        + (rows3,) * 4
        + (rows2,) * 2
        + (cols,) * 2,
        out_specs=(rows2, rows2, P()) + (rows3,) * 6 + (rows2,) * 3 + (cols,) * 3,
        check_vma=False,
    )
```

```python
import functools
import math

import jax
import jax.numpy as jnp
from jax import lax
from jax.experimental import pallas as pl
from jax.experimental.pallas import tpu as pltpu
from jax.sharding import Mesh, PartitionSpec as P

STEP = 10


EPS_NORM = 1e-06
BETA_ONE = 0.9
BETA_TWO = 0.999
ADAM_EPS = 1e-08
RATE_MATRIX = 0.03
RATE_GAIN = 0.5
DECAY_WEIGHT = 0.1
CLIP_NORM = 1.0

ALL = ("z", "y", "x", "c")
PLANE = ("y", "x", "c")
LINE = ("z", "c")
QUAD = ("y", "x")
TILE = 8
BF = jnp.bfloat16
F32 = jnp.float32


def gather(value, axes):
    return lax.all_gather(value, axes, axis=0, tiled=True)


def scatter(value, axes):
    return lax.psum_scatter(value, axes, scatter_dimension=0, tiled=True)


def exchange(value, axes):
    return lax.all_to_all(value, axes, 0, 0, tiled=True)


def ring_gather(value, axis):
    count, mine = lax.axis_size(axis), lax.axis_index(axis)
    if count == 2:
        other = lax.ppermute(value, axis, [(0, 1), (1, 0)])
        return jnp.stack([jnp.where(mine == 0, value, other), jnp.where(mine == 0, other, value)])
    up, down, ups, downs = value, value, [], []
    for hop in range(1, count):
        up = lax.ppermute(up, axis, [(i, i + 1) for i in range(hop - 1, count - 1)])
        down = lax.ppermute(down, axis, [(i, i - 1) for i in range(1, count - hop + 1)])
        ups.append(up)
        downs.append(down)
    places = []
    for place in range(count):
        found = value
        for back in range(1, count):
            if place + back < count:
                found = jnp.where(mine == place + back, ups[back - 1], found)
            if place >= back:
                found = jnp.where(mine == place - back, downs[back - 1], found)
        places.append(found)
    return jnp.stack(places)


def added(terms):
    return sum(term.astype(F32) for term in terms)


def ring_scatter(value, axis, dim=0):
    return added(ring_terms(value, axis, dim))


def ring_terms(value, axis, dim=0):
    count, mine = lax.axis_size(axis), lax.axis_index(axis)

    def block(back):
        return lax.dynamic_index_in_dim(value, (mine - back) % count, dim, False)

    if count == 2:
        return [block(0), lax.ppermute(block(1), axis, [(0, 1), (1, 0)])]
    up = down = None
    for hop in range(1, count):
        up_sum, down_sum = block(hop), block(count - hop)
        if up is not None:
            up_sum = (up_sum.astype(F32) + up.astype(F32)).astype(BF)
            down_sum = (down_sum.astype(F32) + down.astype(F32)).astype(BF)
        up = lax.ppermute(up_sum, axis, [(i, i + 1) for i in range(hop)])
        down = lax.ppermute(down_sum, axis, [(i, i - 1) for i in range(count - hop, count)])
    return [block(0), up, down]


def double_gather(value):
    value = value[None]
    for axis in ("c", "x", "y", "z"):
        count, mine = lax.axis_size(axis), lax.axis_index(axis)
        hop = 1
        while hop < count:
            other = lax.ppermute(value, axis, [(i, i ^ hop) for i in range(count)])
            low = (mine // hop) % 2 == 0
            value = jnp.concatenate([jnp.where(low, value, other), jnp.where(low, other, value)])
            hop *= 2
    return value


def tied(*values):
    return lax.optimization_barrier(values)


def in_parts_of(value):
    upper = value.astype(BF)
    rest = value - upper.astype(F32)
    middle = rest.astype(BF)
    lower = (rest - middle.astype(F32)).astype(BF)
    return [upper, middle, lower]


def direct_scatter(value, axis):
    count, mine = lax.axis_size(axis), lax.axis_index(axis)
    total = lax.dynamic_index_in_dim(value, mine, 0, False).astype(F32)
    for back in range(1, count):
        block = lax.dynamic_index_in_dim(value, (mine - back) % count, 0, False)
        total += lax.ppermute(block, axis, [(i, (i - back) % count) for i in range(count)])
    return total


def quad_halves(value, axis):
    half = value.shape[axis] // 2
    first = ring_gather(lax.slice_in_dim(value, 0, half, axis=axis), "x")
    return [first, ring_gather(lax.slice_in_dim(value, half, 2 * half, axis=axis), "y")]


def quad_others(first, second):
    return [ring_gather(first, "y"), ring_gather(second, "x").swapaxes(0, 1)]


def quad_parts(value, axis):
    return quad_others(*quad_halves(value, axis))


def quad_whole(parts):
    return jnp.concatenate(parts, axis=2).reshape(-1, parts[0].shape[-1])


def quad_sums(value):
    value = value.reshape(lax.axis_size("y"), lax.axis_size("x"), -1, value.shape[1])
    half = value.shape[2] // 2
    first = ring_terms(value[:, :, :half], "y")
    return first + ring_terms(value[:, :, half:].swapaxes(0, 1), "x")


def quad_rest(*terms):
    half = len(terms) // 2
    first, second = added(terms[:half]).astype(BF), added(terms[half:]).astype(BF)
    return jnp.concatenate([ring_scatter(first, "x"), ring_scatter(second, "y")], axis=0)


def core_gather(parts):
    both = ring_gather(jnp.concatenate(parts, axis=3), "c")
    return jnp.moveaxis(both, 0, 2).reshape(-1, both.shape[-1])


def line_gather(value):
    both = ring_gather(ring_gather(value, "z"), "c")
    return both.swapaxes(0, 1).reshape(-1, value.shape[1])


def plane_scatter(value):
    value = value.reshape(lax.axis_size("y"), lax.axis_size("x"), 2, -1, value.shape[1])
    value = ring_scatter(value, "c", 2).astype(BF)
    half = value.shape[3] // 2
    first = ring_scatter(ring_scatter(value[..., :half], "y").astype(BF), "x")
    second = ring_scatter(ring_scatter(value[..., half:], "x", 1).astype(BF), "y")
    return jnp.concatenate([first, second], axis=1)


def direct_gather(value, axis):
    count = lax.axis_size(axis)
    hops = [[(i, (i + back) % count) for i in range(count)] for back in range(1, count)]
    return [value] + [lax.ppermute(value, axis, hop) for hop in hops]


def in_order(values, axis):
    count, mine = lax.axis_size(axis), lax.axis_index(axis)
    places = []
    for place in range(count):
        found = values[0]
        for back in range(1, count):
            found = jnp.where((mine - back) % count == place, values[back], found)
        places.append(found)
    return jnp.stack(places)


def core_exchange(value):
    count, core = lax.axis_size("z"), lax.axis_index("c")
    value = value.reshape((count, 2) + value.shape[1:])
    kept = lax.dynamic_index_in_dim(value, core, 1, False)
    other = lax.dynamic_index_in_dim(value, 1 - core, 1, False)
    other = lax.ppermute(other, "c", [(0, 1), (1, 0)])
    first, second = jnp.where(core == 0, kept, other), jnp.where(core == 0, other, kept)
    return jnp.stack([first, second], axis=1)


def line_exchange(value):
    count, mine = lax.axis_size("z"), lax.axis_index("z")
    blocks = [lax.dynamic_index_in_dim(value, (mine - back) % count, 0, False) for back in range(count)]
    got = [blocks[0]]
    for back in range(1, count):
        got.append(lax.ppermute(blocks[back], "z", [(i, (i - back) % count) for i in range(count)]))
    places = []
    for place in range(count):
        found = got[0]
        for back in range(1, count):
            found = jnp.where((mine + back) % count == place, got[back], found)
        places.append(found)
    return jnp.concatenate(places)


def core_terms(value):
    value = value.reshape(lax.axis_size("z"), 2, -1, value.shape[1]).swapaxes(0, 1)
    return ring_terms(value, "c")


def total_of(value, axes):
    for axis in axes:
        count = lax.axis_size(axis)
        hop = 1
        while hop < count:
            value = value + lax.ppermute(value, axis, [(i, i ^ hop) for i in range(count)])
            hop *= 2
    return value


def normalize(value):
    factor = lax.rsqrt(jnp.mean(value * value, axis=-1, keepdims=True) + EPS_NORM)
    return (value * factor, factor)


def norm_back(grad_normed, normed, factor):
    return factor * (grad_normed - normed * jnp.mean(grad_normed * normed, axis=-1, keepdims=True))


def silu(value):
    return value * jax.nn.sigmoid(value)


def silu_grad(value):
    sig = jax.nn.sigmoid(value)
    return sig * (1.0 + value * (1.0 - sig))


def adam_step(weight, first, second, grad, rate, decay_w):
    first_new = BETA_ONE * first + (1.0 - BETA_ONE) * grad
    second_new = BETA_TWO * second + (1.0 - BETA_TWO) * grad * grad
    scale_one, scale_two = 1.0 / (1.0 - BETA_ONE**STEP), 1.0 / (1.0 - BETA_TWO**STEP)
    step_size = (first_new * scale_one) / (jnp.sqrt(second_new * scale_two) + ADAM_EPS)
    return (weight - rate * (step_size + decay_w * weight), first_new, second_new)


def shifted(value, hop, fill, row, later):
    size = value.shape[0]
    moved = pltpu.roll(value, size - hop if later else hop, 0)
    inside = row < size - hop if later else row >= hop
    return jnp.where(inside, moved, fill)


def tile_scan(coeff, value, row, later):
    hop = 1
    while hop < value.shape[0]:
        value = coeff * shifted(value, hop, 0.0, row, later) + value
        coeff = coeff * shifted(coeff, hop, 1.0, row, later)
        hop *= 2
    return coeff, value


def gates(forget_proj, gap, started):
    sig_neg = jax.nn.sigmoid(-forget_proj)
    keep = gap * sig_neg
    return sig_neg, keep, jnp.where(started > 0.0, 0.0, 1.0 - keep)


def scan_forward(proj_ref, started_ref, gap_ref, state_ref, squares_ref):
    rows, width = state_ref.shape
    row = lax.broadcasted_iota(jnp.int32, (TILE, width), 0)
    gap = gap_ref[...]

    def step(index, carry):
        place = pl.ds(pl.multiple_of(index * TILE, TILE), TILE)
        in_proj = proj_ref[place, pl.ds(0, width)]
        forget_proj = proj_ref[place, pl.ds(width, width)]
        _, keep, decay = gates(forget_proj, gap, started_ref[place, :])
        coeff, value = tile_scan(decay, silu(in_proj) * keep, row, False)
        state = value + coeff * carry
        state_ref[place, :] = state
        squares_ref[place, :] = jnp.sum(state * state, axis=-1, keepdims=True)
        return state[TILE - 1 :, :]

    lax.fori_loop(0, rows // TILE, step, jnp.zeros((1, width), F32), unroll=8)


def scan_backward(
    proj_ref, state_ref, d_mixed_ref, riders_ref, started_ref, gap_ref, gain_ref, d_proj_ref, mixed_ref
):
    rows, width = state_ref.shape
    row = lax.broadcasted_iota(jnp.int32, (TILE, width), 0)
    lane = lax.broadcasted_iota(jnp.int32, (2 * TILE, 128), 1)
    gap, gain = gap_ref[...], gain_ref[...]

    def located(index):
        return pl.ds(pl.multiple_of(index * TILE, TILE), TILE)

    def one(index, mean, factor, carry):
        place = located(index)
        before = located(jnp.maximum(index - 1, 0))
        in_proj = proj_ref[place, pl.ds(0, width)]
        forget_proj = proj_ref[place, pl.ds(width, width)]
        gate_proj = proj_ref[place, pl.ds(2 * width, width)]
        started = started_ref[place, :]
        sig_neg, keep, decay = gates(forget_proj, gap, started)
        state, d_mixed = state_ref[place, :], d_mixed_ref[place, :]
        normed = state * factor
        sig_gate = jax.nn.sigmoid(gate_proj)
        gain_act = gain * (gate_proj * sig_gate)
        d_gate = d_mixed * normed * gain * (sig_gate * (1.0 + gate_proj * (1.0 - sig_gate)))
        d_state = factor * (d_mixed * gain_act - normed * mean)
        coeff, value = tile_scan(decay, decay * d_state, row, True)
        passed = value + coeff * carry
        moved = jnp.where(row < TILE - 1, pltpu.roll(passed, TILE - 1, 0), carry)
        d_total = d_state + moved
        last = state_ref[before, :][TILE - 1 :, :]
        previous = jnp.where(row >= 1, pltpu.roll(state, 1, 0), last)
        previous = jnp.where(started > 0.0, 0.0, previous)
        sig = jax.nn.sigmoid(in_proj)
        d_in = d_total * keep * (sig * (1.0 + in_proj * (1.0 - sig)))
        d_keep = d_total * (in_proj * sig) - d_total * previous
        d_forget = -d_keep * gap * sig_neg * (1.0 - sig_neg)
        return [d_in, d_forget, d_gate, normed * gain_act], passed[:1, :]

    def step(count, carry):
        pair = rows // (2 * TILE) - 1 - count
        place = pl.ds(pl.multiple_of(pair * 2 * TILE, 2 * TILE), 2 * TILE)
        riders = riders_ref[place, :].astype(F32)
        mean = jnp.sum(jnp.where(lane < 3, riders, 0.0), axis=1, keepdims=True)
        factor = jnp.sum(jnp.where(lane < 3, 0.0, riders), axis=1, keepdims=True)
        late, carry = one(2 * pair + 1, mean[TILE:], factor[TILE:], carry)
        early, carry = one(2 * pair, mean[:TILE], factor[:TILE], carry)
        both = [jnp.concatenate(parts, axis=0).astype(BF) for parts in zip(early, late)]
        for kind in range(3):
            d_proj_ref[place, pl.ds(kind * width, width)] = both[kind]
        mixed_ref[place, :] = both[3]
        return carry

    lax.fori_loop(0, rows // (2 * TILE), step, jnp.zeros((1, width), F32), unroll=4)


def run_forward(proj, started, gap):
    rows, width = proj.shape[0], gap.shape[1]
    return pl.pallas_call(
        scan_forward,
        out_shape=[
            jax.ShapeDtypeStruct((rows, width), F32),
            jax.ShapeDtypeStruct((rows, 1), F32),
        ],
        compiler_params=pltpu.CompilerParams(vmem_limit_bytes=48 * 2**20),
    )(proj, started, gap)


def run_backward(proj, state, d_mixed, riders, started, gap, gain):
    rows, width = state.shape
    return pl.pallas_call(
        scan_backward,
        out_shape=[
            jax.ShapeDtypeStruct((rows, 3 * width), BF),
            jax.ShapeDtypeStruct((rows, width), BF),
        ],
        compiler_params=pltpu.CompilerParams(vmem_limit_bytes=48 * 2**20),
    )(proj, state, d_mixed, riders, started, gap, gain)


def adam_rows(clip_ref, weight_ref, first_ref, second_ref, grad_ref, *new_refs):
    clip = clip_ref[0, 0]
    for kind in range(weight_ref.shape[1]):
        moved = adam_step(
            weight_ref[:, kind, :],
            first_ref[:, kind, :],
            second_ref[:, kind, :],
            clip * grad_ref[kind].astype(F32),
            RATE_MATRIX,
            DECAY_WEIGHT,
        )
        for new_ref, value in zip(new_refs, moved):
            new_ref[:, kind, :] = value


def run_adam(weight, first, second, grad, clip):
    own, kinds, width = weight.shape
    rows = min(own, 16)
    rest = pl.BlockSpec((rows, kinds, width), lambda i: (i, 0, 0))
    return pl.pallas_call(
        adam_rows,
        grid=(own // rows,),
        in_specs=[pl.BlockSpec(memory_space=pltpu.SMEM), rest, rest, rest]
        + [pl.BlockSpec((kinds, rows, width), lambda i: (0, i, 0))],
        out_specs=[rest] * 3,
        out_shape=[jax.ShapeDtypeStruct(weight.shape, F32)] * 3,
        compiler_params=pltpu.CompilerParams(vmem_limit_bytes=48 * 2**20),
    )(clip.reshape(1, 1), weight, first, second, grad)


def pack(weight_ref, sent_ref, low_ref):
    spots, own, packed = sent_ref.shape
    planes = packed // (3 * own)
    low_half = lax.broadcasted_iota(jnp.int32, (own, 2 * own), 1) < own
    for kind in range(3):
        for pair in range(0, spots, 2):
            for plane in range(0, planes, 2):
                places = [pl.ds(((plane + i) * spots + pair) * own, 2 * own) for i in range(2)]
                near, far = [weight_ref[:, kind, place] for place in places]
                low_ref[kind, :, places[0]] = near.astype(BF)
                low_ref[kind, :, places[1]] = far.astype(BF)
                at = pl.ds((kind * planes + plane) * own, 2 * own)
                even = jnp.where(low_half, near, pltpu.roll(far, own, 1))
                odd = jnp.where(low_half, pltpu.roll(near, own, 1), far)
                sent_ref[pair, :, at] = even.astype(BF)
                sent_ref[pair + 1, :, at] = odd.astype(BF)
    low_ref[3, :, :] = weight_ref[:, 3, :].astype(BF)


def run_pack(weight, planes, spots):
    own, _, width = weight.shape
    if 2 * own != 128 or planes % 2 != 0:
        low = weight.astype(BF)
        sent = low[:, :3, :].reshape(own, 3, planes, spots, own).transpose(3, 0, 1, 2, 4)
        return sent.reshape(spots, own, 3 * planes * own), low.swapaxes(0, 1)
    return pl.pallas_call(
        pack,
        out_shape=[
            jax.ShapeDtypeStruct((spots, own, 3 * planes * own), BF),
            jax.ShapeDtypeStruct((4, own, width), BF),
        ],
        compiler_params=pltpu.CompilerParams(vmem_limit_bytes=48 * 2**20),
    )(weight)


def row_sums(shard_ref, first_ref, inner_ref, sums_ref):
    split = first_ref.shape[1]
    grad = shard_ref[...].astype(F32)
    first = jnp.sum(grad[:, :split] * first_ref[...].astype(F32), axis=1, keepdims=True)
    inner = jnp.sum(grad[:, split:] * inner_ref[...].astype(F32), axis=1, keepdims=True)
    squares = jnp.sum(grad * grad, axis=1, keepdims=True)
    lane = lax.broadcasted_iota(jnp.int32, sums_ref.shape, 1)
    sums_ref[...] = jnp.where(lane == 0, first, jnp.where(lane == 1, inner, squares))


def run_row_sums(shard, first, inner):
    if first.shape[1] % 128 != 0 or inner.shape[1] % 128 != 0:
        grad = shard.astype(F32)
        split = first.shape[1]
        parts = [grad[:, :split] * first.astype(F32), grad[:, split:] * inner.astype(F32), grad * grad]
        return [jnp.sum(part, axis=1) for part in parts]
    sums = pl.pallas_call(
        row_sums,
        out_shape=jax.ShapeDtypeStruct((shard.shape[0], 128), F32),
        compiler_params=pltpu.CompilerParams(vmem_limit_bytes=48 * 2**20),
    )(shard, first, inner)
    return [sums[:, column] for column in range(3)]


def settle(got_ref, out_ref, grad_ref):
    spots, own, packed = got_ref.shape
    planes = packed // (3 * own)
    low_half = lax.broadcasted_iota(jnp.int32, (own, 2 * own), 1) < own
    for pair in range(0, spots, 2):
        for kind in range(3):
            for plane in range(0, planes, 2):
                at = pl.ds((kind * planes + plane) * own, 2 * own)
                even = got_ref[pair, :, at].astype(F32)
                odd = got_ref[pair + 1, :, at].astype(F32)
                near = jnp.where(low_half, even, pltpu.roll(odd, own, 1))
                far = jnp.where(low_half, pltpu.roll(even, own, 1), odd)
                for step, grad in enumerate((near, far)):
                    grad_ref[kind, :, pl.ds(((plane + step) * spots + pair) * own, 2 * own)] = grad.astype(BF)
    grad_ref[3, :, :] = out_ref[...]


def run_settle(got, shard_out):
    spots, own, packed = got.shape
    width = shard_out.shape[1]
    planes = packed // (3 * own)
    if 2 * own != 128 or planes % 2 != 0:
        grad = got.reshape(spots, own, 3, planes, own).transpose(2, 1, 3, 0, 4).reshape(3, own, width)
        return jnp.concatenate([grad, shard_out[None]], axis=0)
    return pl.pallas_call(
        settle,
        out_shape=jax.ShapeDtypeStruct((4, own, width), BF),
        compiler_params=pltpu.CompilerParams(vmem_limit_bytes=48 * 2**20),
    )(got, shard_out)


def column_blocks(width, first, second):
    size = width // (first * second)
    for i in range(first):
        for j in range(second):
            yield pl.ds((i * second + j) * size, size), pl.ds((j * first + i) * size, size)


def enter_glu(order, mix_ref, x_ref, gain_ref, after_ref, n2_ref, mid_ref, home_ref):
    width = x_ref.shape[1]
    squares = jnp.sum(mix_ref[:, width:].astype(F32), axis=1, keepdims=True)
    home = lax.rsqrt(squares / width + EPS_NORM)
    after = x_ref[...].astype(F32) + mix_ref[:, :width].astype(F32) * home
    mid = lax.rsqrt(jnp.mean(after * after, axis=1, keepdims=True) + EPS_NORM)
    after_ref[...] = after
    mid_ref[...] = mid
    home_ref[...] = home
    n2 = (after * mid * gain_ref[...]).astype(BF)
    for source, target in column_blocks(width, *order):
        n2_ref[:, target] = n2[:, source.start : source.start + source.size]


def leave_glu(
    order, d_n2_ref, cot_ref, after_ref, mid_ref, mix_ref, home_ref, gain_ref, d_mid_ref, out_ref, held_ref
):
    width = cot_ref.shape[1]
    mid, home = mid_ref[...], home_ref[...]
    for target, source in column_blocks(width, *order):
        held_ref[:, target] = d_n2_ref[:, source].astype(F32) * gain_ref[:, target]
    normed = after_ref[...] * mid
    grad = held_ref[...]
    inner = jnp.mean(grad * normed, axis=1, keepdims=True)
    d_mid = cot_ref[...].astype(F32) + mid * (grad - normed * inner)
    d_mid_ref[...] = d_mid
    low = d_mid.astype(BF)
    out_ref[:, :width] = low
    mean = jnp.sum(low.astype(F32) * (mix_ref[:, :width].astype(F32) * home), axis=1, keepdims=True) / width
    lane = lax.broadcasted_iota(jnp.int32, (mid.shape[0], 128), 1)
    riders = jnp.zeros((mid.shape[0], 128), F32)
    for at, value in ((0, mean), (3, home)):
        for part in range(3):
            upper = value.astype(BF).astype(F32)
            riders = jnp.where(lane == at + part, upper, riders)
            value = value - upper
    out_ref[:, width:] = riders.astype(BF)


def run_enter(mix_raw, tokens, gain, order):
    rows, width = tokens.shape
    if width // (order[0] * order[1]) % 128 != 0:
        squares = jnp.sum(mix_raw[:, width:].astype(F32), axis=1, keepdims=True)
        home = lax.rsqrt(squares / width + EPS_NORM)
        after = tokens.astype(F32) + mix_raw[:, :width].astype(F32) * home
        normed, mid = normalize(after)
        n2 = (normed * gain).astype(BF).reshape(rows, *order, -1).swapaxes(1, 2)
        return after, n2.reshape(rows, width), mid, home
    column = jax.ShapeDtypeStruct((rows, 1), F32)
    return pl.pallas_call(
        functools.partial(enter_glu, order),
        out_shape=[
            jax.ShapeDtypeStruct((rows, width), F32),
            jax.ShapeDtypeStruct((rows, width), BF),
            column,
            column,
        ],
        compiler_params=pltpu.CompilerParams(vmem_limit_bytes=48 * 2**20),
    )(mix_raw, tokens, gain)


def run_leave(d_n2, cot, after, mid, mix_raw, home, gain, order):
    rows, width = cot.shape
    if width // (order[0] * order[1]) % 128 != 0:
        grad = d_n2.reshape(rows, order[1], order[0], -1).swapaxes(1, 2).reshape(rows, width)
        d_mid = cot.astype(F32) + norm_back(grad.astype(F32) * gain, after * mid, mid)
        low = d_mid.astype(BF)
        mix = mix_raw[:, :width].astype(F32) * home
        mean = jnp.sum(low.astype(F32) * mix, axis=1, keepdims=True) / width
        riders = jnp.concatenate(in_parts_of(mean) + in_parts_of(home), axis=1)
        riders = jnp.pad(riders, ((0, 0), (0, 128 - riders.shape[1])))
        return d_mid, jnp.concatenate([low, riders], axis=1)
    return pl.pallas_call(
        functools.partial(leave_glu, order),
        out_shape=[
            jax.ShapeDtypeStruct((rows, width), F32),
            jax.ShapeDtypeStruct((rows, width + 128), BF),
        ],
        scratch_shapes=[pltpu.VMEM((rows, width), F32)],
        compiler_params=pltpu.CompilerParams(vmem_limit_bytes=48 * 2**20),
    )(d_n2, cot, after, mid, mix_raw, home, gain)


def shards(
    tokens,
    cotangent,
    lengths,
    lower_bound,
    mixer_w,
    mlp_in,
    mlp_down,
    gains,
    mixer_m,
    mixer_v,
    in_m,
    in_v,
    down_m,
    down_v,
    gain_m,
    gain_v,
):
    rows, width = tokens.shape
    own, _, hidden_width = mlp_in.shape
    down_rows = mlp_down.shape[0]
    planes = lax.axis_size("z")
    spots = lax.axis_size(PLANE)
    quads = lax.axis_size(QUAD)
    pairs = lax.axis_size("c")
    group = spots * rows
    spot = lax.axis_index(PLANE)
    chans = planes * own

    ends = jnp.cumsum(lengths)
    starts = ends - lengths
    places = jnp.arange(group, dtype=jnp.int32)
    started = jnp.any(places[:, None] == starts[None, :], axis=-1, keepdims=True).astype(F32)
    home = spot * rows + jnp.arange(rows, dtype=jnp.int32)
    valid = (home < ends[-1]).astype(F32)

    cot_low = (cotangent.astype(F32) * valid[:, None]).astype(BF)

    w_out = gather(mixer_w[:, 3, :].astype(BF), "z")
    sent, low_mixer = run_pack(mixer_w, planes, spots)
    part = exchange(sent, PLANE).reshape(spots * own, 3 * chans)
    low_in = mlp_in.astype(BF)
    inner = quads * down_rows
    sent_in = low_in.reshape(own, 2, planes, quads, pairs, down_rows).transpose(2, 4, 0, 1, 3, 5)
    sent_in = sent_in.reshape(planes * pairs, own, 2 * inner)
    part, w_out, x_low, low_gains, low_down, sent_in = tied(
        part, w_out, tokens, gains, mlp_down, sent_in
    )
    x_parts = quad_parts(x_low, 1)
    full_gains = double_gather(low_gains).swapaxes(0, 1).reshape(3, width)
    w_down = quad_whole(quad_parts(low_down.astype(BF), 0))
    w_proj = gather(part, "z")
    x_all = core_gather(x_parts)

    bound = lower_bound.reshape(planes, spots, own)
    gap = (1.0 - lax.dynamic_index_in_dim(bound, spot, 1, False)).reshape(1, chans)
    gain_mid = full_gains[1].reshape(planes, spots, own)
    gain_mid = lax.dynamic_index_in_dim(gain_mid, spot, 1, False).reshape(1, chans)

    x = tokens.astype(F32)
    x_normed, x_factor = normalize(x)
    n1 = (normalize(x_all.astype(F32))[0] * full_gains[0]).astype(BF)
    blocks_in = core_exchange(sent_in)
    w_proj, w_down, n1, blocks_in, held_cot = tied(w_proj, w_down, n1, blocks_in, cot_low)
    cots = direct_gather(held_cot, "z")
    proj = jnp.dot(n1, w_proj, preferred_element_type=F32)
    proj, blocks_in = tied(proj, blocks_in)
    part_in = line_exchange(blocks_in)
    state, squares = run_forward(proj, started, gap)
    gate_proj = proj[:, 2 * chans :]
    gate_act = silu(gate_proj)
    raw = (state * gain_mid * gate_act).astype(BF)
    lane = jnp.arange(128, dtype=jnp.int32)[None, :]
    upper = squares.astype(BF).astype(F32)
    riders = jnp.where(lane == spot, upper, jnp.where(lane == spots + spot, squares - upper, 0.0))
    raw = jnp.concatenate([raw, riders.astype(BF)], axis=1)
    ride = jnp.pad(jnp.eye(128, dtype=BF), ((chans, 0), (width, 0)))
    w_ride = ride + jnp.pad(w_out, ((0, 128), (0, 128)))
    mix_part = jnp.dot(raw, w_ride, preferred_element_type=F32).astype(BF)
    mix_part, cots[1], cots[-1] = tied(mix_part, cots[1], cots[-1])
    in_halves = quad_halves(part_in.reshape(planes * pairs * own, 2 * inner), 0)
    mix_raw, *cots = tied(scatter(mix_part, PLANE), *cots)
    cot_all = ring_gather(in_order(cots, "z"), "c").swapaxes(0, 1)
    cot_all = cot_all.reshape(planes * pairs * rows, width)

    order, gain_glu = (planes, quads), full_gains[2].reshape(1, width)
    after_mix, n2_home, mid_factor, home_factor = run_enter(mix_raw, tokens, gain_glu, order)
    n2_home, *in_halves = tied(n2_home, *in_halves)
    n2 = gather(n2_home, LINE)
    w_in = quad_whole(quad_others(*in_halves))
    gate_up = jnp.dot(n2, w_in, preferred_element_type=F32)
    gate, up_value = gate_up[:, :inner], gate_up[:, inner:]
    silu_gate = silu(gate)
    hidden = (silu_gate * up_value).astype(BF)

    d_hidden = lax.dot_general(cot_all, w_down, (((1,), (1,)), ((), ())), preferred_element_type=F32)
    d_gate = d_hidden * up_value * silu_grad(gate)
    d_up = d_hidden * silu_gate
    d_gate_up = jnp.concatenate([d_gate.astype(BF), d_up.astype(BF)], axis=1)
    d_n2 = lax.dot_general(d_gate_up, w_in, (((1,), (1,)), ((), ())), preferred_element_type=F32)
    d_n2 = scatter(d_n2.astype(BF), LINE)
    grad_in = lax.dot_general(n2, d_gate_up, (((0,), (0,)), ((), ())), preferred_element_type=F32)
    grad_in = grad_in.astype(BF)
    down = jnp.dot(hidden, w_down, preferred_element_type=F32).astype(BF)
    sums_in = quad_sums(grad_in)
    down, held_hidden = tied(added(core_terms(down)).astype(BF), hidden)
    grad_down = lax.dot_general(
        held_hidden, cot_all, (((0,), (0,)), ((), ())), preferred_element_type=F32
    ).astype(BF)
    d_n2, grad_down, down, *sums_in = tied(d_n2, grad_down, down, *sums_in)
    d_mid, d_mix_home = run_leave(
        d_n2, cot_low, after_mix, mid_factor, mix_raw, home_factor, gain_glu, order
    )
    down = direct_scatter(down, "z")
    shard_in = quad_rest(*sums_in).astype(BF)
    d_mix = gather(d_mix_home, PLANE)
    d_mix, shard_in, grad_down, down = tied(d_mix, shard_in, grad_down, down)
    block_out = (after_mix + down).astype(BF)
    shard_down = scatter(grad_down, QUAD).astype(F32)
    got_in = exchange(shard_in.reshape(planes * pairs, own, 2 * inner), LINE)

    d_mixed = lax.dot_general(
        d_mix, w_ride[:chans], (((1,), (1,)), ((), ())), preferred_element_type=F32
    )
    d_proj, mixed_in = run_backward(proj, state, d_mixed, d_mix[:, width:], started, gap, gain_mid)
    grad_out = lax.dot_general(mixed_in, d_mix, (((0,), (0,)), ((), ())), preferred_element_type=F32)
    grad_proj = lax.dot_general(n1, d_proj, (((0,), (0,)), ((), ())), preferred_element_type=F32)
    grad_out = grad_out[:, :width].astype(BF).reshape(planes, spots * own, chans)
    grad_all = jnp.concatenate(
        [grad_proj.astype(BF).reshape(planes, spots * own, 3 * chans), grad_out], axis=2
    )
    grad_all, got_in, held_proj = tied(grad_all, got_in, d_proj)
    shard_all = scatter(grad_all.reshape(planes * spots * own, 4 * chans), "z")
    shard_in = got_in.reshape(planes, pairs, own, 2, quads, down_rows).transpose(3, 2, 0, 4, 1, 5)
    shard_in = shard_in.reshape(2, own, hidden_width)
    wide_in = shard_in.astype(F32)
    gain_in = jnp.sum(wide_in * low_in.swapaxes(0, 1).astype(F32), axis=(0, 2))
    total_early = jnp.sum(wide_in * wide_in) + jnp.sum(shard_down * shard_down)
    d_n1 = lax.dot_general(held_proj, w_proj, (((1,), (1,)), ((), ())), preferred_element_type=F32)
    d_n1 = plane_scatter(d_n1.astype(BF))
    input_grad = d_mid + norm_back(d_n1 * full_gains[0], x_normed, x_factor)
    plane_rows = spots * own
    first_row = lax.axis_index("z") * plane_rows
    rows_first = lax.dynamic_slice_in_dim(w_proj, first_row, plane_rows)
    rows_inner = low_mixer[3].reshape(plane_rows, chans)
    shard_all, shard_in, shard_down, gain_in, total_early, input_grad, rows_first, rows_inner = tied(
        shard_all, shard_in, shard_down, gain_in, total_early, input_grad, rows_first, rows_inner
    )
    shard_proj = shard_all[:, : 3 * chans]
    got_proj = exchange(shard_proj.reshape(spots, own, 3 * chans), PLANE)
    shard_out = shard_all[:, 3 * chans :].reshape(own, width)

    row_first, row_inner, row_squares = run_row_sums(shard_all, rows_first, rows_inner)
    gain_inner = jnp.sum(row_inner.reshape(own, spots), axis=1) / gains[1]
    gain_in = gain_in / gains[2]
    local_total = jnp.sum(row_squares) + total_early
    local_total += jnp.sum(gain_inner * gain_inner) + jnp.sum(gain_in * gain_in)
    sums = jnp.concatenate(
        [row_first.reshape(spots, own), jnp.full((1, own), local_total)], axis=0
    )
    sums = total_of(sums, ("c", "x", "y"))
    gain_rows = lax.dynamic_slice_in_dim(full_gains[0], first_row, plane_rows).reshape(spots, own)
    gain_first = sums[:spots] / gain_rows
    total = sums[spots:, :1] + jnp.sum(gain_first * gain_first)
    grad_norm = jnp.sqrt(total_of(total, ("z",))[0, 0])
    gain_first = lax.dynamic_index_in_dim(gain_first, spot, 0, False)
    shard_gains = jnp.stack([gain_first, gain_inner, gain_in])
    clip = jnp.minimum(1.0, CLIP_NORM / (grad_norm + 1e-06))
    shard_mixer = run_settle(got_proj, shard_out)
    new_mixer, new_mixer_m, new_mixer_v = run_adam(mixer_w, mixer_m, mixer_v, shard_mixer, clip)
    new_in, new_in_m, new_in_v = run_adam(mlp_in, in_m, in_v, shard_in, clip)
    new_down, new_down_m, new_down_v = adam_step(
        mlp_down, down_m, down_v, clip * shard_down, RATE_MATRIX, DECAY_WEIGHT
    )
    new_gains, new_gain_m, new_gain_v = adam_step(
        gains, gain_m, gain_v, clip * shard_gains, RATE_GAIN, 0.0
    )
    return (
        block_out,
        input_grad,
        grad_norm,
        new_mixer,
        new_mixer_m,
        new_mixer_v,
        new_in,
        new_in_m,
        new_in_v,
        new_down,
        new_down_m,
        new_down_v,
        new_gains,
        new_gain_m,
        new_gain_v,
    )


def solution(mesh):
    planes, spots = mesh.shape["dp"], mesh.shape["seq"]
    side = math.isqrt(spots // 2)
    split = Mesh(mesh.devices.reshape(planes, spots // (2 * side), side, 2), ALL)
    rows2, rows3, cols = P(ALL, None), P(ALL, None, None), P(None, ALL)
    return jax.shard_map(
        shards,
        mesh=split,
        in_specs=(rows2, rows2, P("z"), P(), rows3, rows3, rows2, cols)
        + (rows3,) * 4
        + (rows2,) * 2
        + (cols,) * 2,
        out_specs=(rows2, rows2, P()) + (rows3,) * 6 + (rows2,) * 3 + (cols,) * 3,
        check_vma=False,
    )
```

```python
import functools
import math

import jax
import jax.numpy as jnp
from jax import lax
from jax.experimental import pallas as pl
from jax.experimental.pallas import tpu as pltpu
from jax.sharding import Mesh, PartitionSpec as P

STEP = 10


EPS_NORM = 1e-06
BETA_ONE = 0.9
BETA_TWO = 0.999
ADAM_EPS = 1e-08
RATE_MATRIX = 0.03
RATE_GAIN = 0.5
DECAY_WEIGHT = 0.1
CLIP_NORM = 1.0

ALL = ("z", "y", "x", "c")
PLANE = ("y", "x", "c")
LINE = ("z", "c")
QUAD = ("y", "x")
TILE = 8
BF = jnp.bfloat16
F32 = jnp.float32


def gather(value, axes):
    return lax.all_gather(value, axes, axis=0, tiled=True)


def scatter(value, axes):
    return lax.psum_scatter(value, axes, scatter_dimension=0, tiled=True)


def exchange(value, axes):
    return lax.all_to_all(value, axes, 0, 0, tiled=True)


def ring_gather(value, axis):
    count, mine = lax.axis_size(axis), lax.axis_index(axis)
    if count == 2:
        other = lax.ppermute(value, axis, [(0, 1), (1, 0)])
        return jnp.stack([jnp.where(mine == 0, value, other), jnp.where(mine == 0, other, value)])
    up, down, ups, downs = value, value, [], []
    for hop in range(1, count):
        up = lax.ppermute(up, axis, [(i, i + 1) for i in range(hop - 1, count - 1)])
        down = lax.ppermute(down, axis, [(i, i - 1) for i in range(1, count - hop + 1)])
        ups.append(up)
        downs.append(down)
    places = []
    for place in range(count):
        found = value
        for back in range(1, count):
            if place + back < count:
                found = jnp.where(mine == place + back, ups[back - 1], found)
            if place >= back:
                found = jnp.where(mine == place - back, downs[back - 1], found)
        places.append(found)
    return jnp.stack(places)


def added(terms):
    return sum(term.astype(F32) for term in terms)


def ring_scatter(value, axis, dim=0):
    return added(ring_terms(value, axis, dim))


def ring_terms(value, axis, dim=0):
    count, mine = lax.axis_size(axis), lax.axis_index(axis)

    def block(back):
        return lax.dynamic_index_in_dim(value, (mine - back) % count, dim, False)

    if count == 2:
        return [block(0), lax.ppermute(block(1), axis, [(0, 1), (1, 0)])]
    up = down = None
    for hop in range(1, count):
        up_sum, down_sum = block(hop), block(count - hop)
        if up is not None:
            up_sum = (up_sum.astype(F32) + up.astype(F32)).astype(BF)
            down_sum = (down_sum.astype(F32) + down.astype(F32)).astype(BF)
        up = lax.ppermute(up_sum, axis, [(i, i + 1) for i in range(hop)])
        down = lax.ppermute(down_sum, axis, [(i, i - 1) for i in range(count - hop, count)])
    return [block(0), up, down]


def double_gather(value):
    value = value[None]
    for axis in ("c", "x", "y", "z"):
        count, mine = lax.axis_size(axis), lax.axis_index(axis)
        hop = 1
        while hop < count:
            other = lax.ppermute(value, axis, [(i, i ^ hop) for i in range(count)])
            low = (mine // hop) % 2 == 0
            value = jnp.concatenate([jnp.where(low, value, other), jnp.where(low, other, value)])
            hop *= 2
    return value


def tied(*values):
    return lax.optimization_barrier(values)


def in_parts_of(value):
    upper = value.astype(BF)
    rest = value - upper.astype(F32)
    middle = rest.astype(BF)
    lower = (rest - middle.astype(F32)).astype(BF)
    return [upper, middle, lower]


def direct_scatter(value, axis):
    count, mine = lax.axis_size(axis), lax.axis_index(axis)
    total = lax.dynamic_index_in_dim(value, mine, 0, False).astype(F32)
    for back in range(1, count):
        block = lax.dynamic_index_in_dim(value, (mine - back) % count, 0, False)
        total += lax.ppermute(block, axis, [(i, (i - back) % count) for i in range(count)])
    return total


def quad_halves(value, axis):
    half = value.shape[axis] // 2
    first = ring_gather(lax.slice_in_dim(value, 0, half, axis=axis), "x")
    return [first, ring_gather(lax.slice_in_dim(value, half, 2 * half, axis=axis), "y")]


def quad_others(first, second):
    return [ring_gather(first, "y"), ring_gather(second, "x").swapaxes(0, 1)]


def quad_parts(value, axis):
    return quad_others(*quad_halves(value, axis))


def quad_whole(parts):
    return jnp.concatenate(parts, axis=2).reshape(-1, parts[0].shape[-1])


def quad_sums(value):
    value = value.reshape(lax.axis_size("y"), lax.axis_size("x"), -1, value.shape[1])
    half = value.shape[2] // 2
    first = ring_terms(value[:, :, :half], "y")
    return first + ring_terms(value[:, :, half:].swapaxes(0, 1), "x")


def quad_rest(*terms):
    half = len(terms) // 2
    first, second = added(terms[:half]).astype(BF), added(terms[half:]).astype(BF)
    return jnp.concatenate([ring_scatter(first, "x"), ring_scatter(second, "y")], axis=0)


def core_gather(parts):
    both = ring_gather(jnp.concatenate(parts, axis=3), "c")
    return jnp.moveaxis(both, 0, 2).reshape(-1, both.shape[-1])


def line_gather(value):
    both = ring_gather(ring_gather(value, "z"), "c")
    return both.swapaxes(0, 1).reshape(-1, value.shape[1])


def plane_scatter(value):
    value = value.reshape(lax.axis_size("y"), lax.axis_size("x"), 2, -1, value.shape[1])
    value = ring_scatter(value, "c", 2).astype(BF)
    half = value.shape[3] // 2
    first = ring_scatter(ring_scatter(value[..., :half], "y").astype(BF), "x")
    second = ring_scatter(ring_scatter(value[..., half:], "x", 1).astype(BF), "y")
    return jnp.concatenate([first, second], axis=1)


def direct_gather(value, axis):
    count = lax.axis_size(axis)
    hops = [[(i, (i + back) % count) for i in range(count)] for back in range(1, count)]
    return [value] + [lax.ppermute(value, axis, hop) for hop in hops]


def in_order(values, axis):
    count, mine = lax.axis_size(axis), lax.axis_index(axis)
    places = []
    for place in range(count):
        found = values[0]
        for back in range(1, count):
            found = jnp.where((mine - back) % count == place, values[back], found)
        places.append(found)
    return jnp.stack(places)


def core_exchange(value):
    count, core = lax.axis_size("z"), lax.axis_index("c")
    value = value.reshape((count, 2) + value.shape[1:])
    kept = lax.dynamic_index_in_dim(value, core, 1, False)
    other = lax.dynamic_index_in_dim(value, 1 - core, 1, False)
    other = lax.ppermute(other, "c", [(0, 1), (1, 0)])
    first, second = jnp.where(core == 0, kept, other), jnp.where(core == 0, other, kept)
    return jnp.stack([first, second], axis=1)


def line_exchange(value):
    count, mine = lax.axis_size("z"), lax.axis_index("z")
    blocks = [lax.dynamic_index_in_dim(value, (mine - back) % count, 0, False) for back in range(count)]
    got = [blocks[0]]
    for back in range(1, count):
        got.append(lax.ppermute(blocks[back], "z", [(i, (i - back) % count) for i in range(count)]))
    places = []
    for place in range(count):
        found = got[0]
        for back in range(1, count):
            found = jnp.where((mine + back) % count == place, got[back], found)
        places.append(found)
    return jnp.concatenate(places)


def core_terms(value):
    value = value.reshape(lax.axis_size("z"), 2, -1, value.shape[1]).swapaxes(0, 1)
    return ring_terms(value, "c")


def total_of(value, axes):
    for axis in axes:
        count = lax.axis_size(axis)
        hop = 1
        while hop < count:
            value = value + lax.ppermute(value, axis, [(i, i ^ hop) for i in range(count)])
            hop *= 2
    return value


def normalize(value):
    factor = lax.rsqrt(jnp.mean(value * value, axis=-1, keepdims=True) + EPS_NORM)
    return (value * factor, factor)


def norm_back(grad_normed, normed, factor):
    return factor * (grad_normed - normed * jnp.mean(grad_normed * normed, axis=-1, keepdims=True))


def silu(value):
    return value * jax.nn.sigmoid(value)


def silu_grad(value):
    sig = jax.nn.sigmoid(value)
    return sig * (1.0 + value * (1.0 - sig))


def adam_step(weight, first, second, grad, rate, decay_w):
    first_new = BETA_ONE * first + (1.0 - BETA_ONE) * grad
    second_new = BETA_TWO * second + (1.0 - BETA_TWO) * grad * grad
    scale_one, scale_two = 1.0 / (1.0 - BETA_ONE**STEP), 1.0 / (1.0 - BETA_TWO**STEP)
    step_size = (first_new * scale_one) / (jnp.sqrt(second_new * scale_two) + ADAM_EPS)
    return (weight - rate * (step_size + decay_w * weight), first_new, second_new)


def shifted(value, hop, fill, row, later):
    size = value.shape[0]
    moved = pltpu.roll(value, size - hop if later else hop, 0)
    inside = row < size - hop if later else row >= hop
    return jnp.where(inside, moved, fill)


def tile_scan(coeff, value, row, later):
    hop = 1
    while hop < value.shape[0]:
        value = coeff * shifted(value, hop, 0.0, row, later) + value
        coeff = coeff * shifted(coeff, hop, 1.0, row, later)
        hop *= 2
    return coeff, value


def gates(forget_proj, gap, started):
    sig_neg = jax.nn.sigmoid(-forget_proj)
    keep = gap * sig_neg
    return sig_neg, keep, jnp.where(started > 0.0, 0.0, 1.0 - keep)


def scan_forward(proj_ref, started_ref, gap_ref, state_ref, squares_ref):
    rows, width = state_ref.shape
    row = lax.broadcasted_iota(jnp.int32, (TILE, width), 0)
    gap = gap_ref[...]

    def step(index, carry):
        place = pl.ds(pl.multiple_of(index * TILE, TILE), TILE)
        in_proj = proj_ref[place, pl.ds(0, width)]
        forget_proj = proj_ref[place, pl.ds(width, width)]
        _, keep, decay = gates(forget_proj, gap, started_ref[place, :])
        coeff, value = tile_scan(decay, silu(in_proj) * keep, row, False)
        state = value + coeff * carry
        state_ref[place, :] = state
        squares_ref[place, :] = jnp.sum(state * state, axis=-1, keepdims=True)
        return state[TILE - 1 :, :]

    lax.fori_loop(0, rows // TILE, step, jnp.zeros((1, width), F32), unroll=8)


def scan_backward(
    proj_ref, state_ref, d_mixed_ref, riders_ref, started_ref, gap_ref, gain_ref, d_proj_ref, mixed_ref
):
    rows, width = state_ref.shape
    row = lax.broadcasted_iota(jnp.int32, (TILE, width), 0)
    lane = lax.broadcasted_iota(jnp.int32, (2 * TILE, 128), 1)
    gap, gain = gap_ref[...], gain_ref[...]

    def located(index):
        return pl.ds(pl.multiple_of(index * TILE, TILE), TILE)

    def one(index, mean, factor, carry):
        place = located(index)
        before = located(jnp.maximum(index - 1, 0))
        in_proj = proj_ref[place, pl.ds(0, width)]
        forget_proj = proj_ref[place, pl.ds(width, width)]
        gate_proj = proj_ref[place, pl.ds(2 * width, width)]
        started = started_ref[place, :]
        sig_neg, keep, decay = gates(forget_proj, gap, started)
        state, d_mixed = state_ref[place, :], d_mixed_ref[place, :]
        normed = state * factor
        sig_gate = jax.nn.sigmoid(gate_proj)
        gain_act = gain * (gate_proj * sig_gate)
        d_gate = d_mixed * normed * gain * (sig_gate * (1.0 + gate_proj * (1.0 - sig_gate)))
        d_state = factor * (d_mixed * gain_act - normed * mean)
        coeff, value = tile_scan(decay, decay * d_state, row, True)
        passed = value + coeff * carry
        moved = jnp.where(row < TILE - 1, pltpu.roll(passed, TILE - 1, 0), carry)
        d_total = d_state + moved
        last = state_ref[before, :][TILE - 1 :, :]
        previous = jnp.where(row >= 1, pltpu.roll(state, 1, 0), last)
        previous = jnp.where(started > 0.0, 0.0, previous)
        sig = jax.nn.sigmoid(in_proj)
        d_in = d_total * keep * (sig * (1.0 + in_proj * (1.0 - sig)))
        d_keep = d_total * (in_proj * sig) - d_total * previous
        d_forget = -d_keep * gap * sig_neg * (1.0 - sig_neg)
        return [d_in, d_forget, d_gate, normed * gain_act], passed[:1, :]

    def step(count, carry):
        pair = rows // (2 * TILE) - 1 - count
        place = pl.ds(pl.multiple_of(pair * 2 * TILE, 2 * TILE), 2 * TILE)
        riders = riders_ref[place, :].astype(F32)
        mean = jnp.sum(jnp.where(lane < 3, riders, 0.0), axis=1, keepdims=True)
        factor = jnp.sum(jnp.where(lane < 3, 0.0, riders), axis=1, keepdims=True)
        late, carry = one(2 * pair + 1, mean[TILE:], factor[TILE:], carry)
        early, carry = one(2 * pair, mean[:TILE], factor[:TILE], carry)
        both = [jnp.concatenate(parts, axis=0).astype(BF) for parts in zip(early, late)]
        for kind in range(3):
            d_proj_ref[place, pl.ds(kind * width, width)] = both[kind]
        mixed_ref[place, :] = both[3]
        return carry

    lax.fori_loop(0, rows // (2 * TILE), step, jnp.zeros((1, width), F32), unroll=4)


def run_forward(proj, started, gap):
    rows, width = proj.shape[0], gap.shape[1]
    return pl.pallas_call(
        scan_forward,
        out_shape=[
            jax.ShapeDtypeStruct((rows, width), F32),
            jax.ShapeDtypeStruct((rows, 1), F32),
        ],
        compiler_params=pltpu.CompilerParams(vmem_limit_bytes=48 * 2**20),
    )(proj, started, gap)


def run_backward(proj, state, d_mixed, riders, started, gap, gain):
    rows, width = state.shape
    return pl.pallas_call(
        scan_backward,
        out_shape=[
            jax.ShapeDtypeStruct((rows, 3 * width), BF),
            jax.ShapeDtypeStruct((rows, width), BF),
        ],
        compiler_params=pltpu.CompilerParams(vmem_limit_bytes=48 * 2**20),
    )(proj, state, d_mixed, riders, started, gap, gain)


def adam_rows(clip_ref, weight_ref, first_ref, second_ref, grad_ref, *new_refs):
    clip = clip_ref[0, 0]
    for kind in range(weight_ref.shape[1]):
        moved = adam_step(
            weight_ref[:, kind, :],
            first_ref[:, kind, :],
            second_ref[:, kind, :],
            clip * grad_ref[kind].astype(F32),
            RATE_MATRIX,
            DECAY_WEIGHT,
        )
        for new_ref, value in zip(new_refs, moved):
            new_ref[:, kind, :] = value


def run_adam(weight, first, second, grad, clip):
    own, kinds, width = weight.shape
    rows = min(own, 16)
    rest = pl.BlockSpec((rows, kinds, width), lambda i: (i, 0, 0))
    return pl.pallas_call(
        adam_rows,
        grid=(own // rows,),
        in_specs=[pl.BlockSpec(memory_space=pltpu.SMEM), rest, rest, rest]
        + [pl.BlockSpec((kinds, rows, width), lambda i: (0, i, 0))],
        out_specs=[rest] * 3,
        out_shape=[jax.ShapeDtypeStruct(weight.shape, F32)] * 3,
        compiler_params=pltpu.CompilerParams(vmem_limit_bytes=48 * 2**20),
    )(clip.reshape(1, 1), weight, first, second, grad)


def pack(weight_ref, sent_ref, low_ref):
    spots, own, packed = sent_ref.shape
    planes = packed // (3 * own)
    low_half = lax.broadcasted_iota(jnp.int32, (own, 2 * own), 1) < own
    for kind in range(3):
        for pair in range(0, spots, 2):
            for plane in range(0, planes, 2):
                places = [pl.ds(((plane + i) * spots + pair) * own, 2 * own) for i in range(2)]
                near, far = [weight_ref[:, kind, place] for place in places]
                low_ref[kind, :, places[0]] = near.astype(BF)
                low_ref[kind, :, places[1]] = far.astype(BF)
                at = pl.ds((kind * planes + plane) * own, 2 * own)
                even = jnp.where(low_half, near, pltpu.roll(far, own, 1))
                odd = jnp.where(low_half, pltpu.roll(near, own, 1), far)
                sent_ref[pair, :, at] = even.astype(BF)
                sent_ref[pair + 1, :, at] = odd.astype(BF)
    low_ref[3, :, :] = weight_ref[:, 3, :].astype(BF)


def run_pack(weight, planes, spots):
    own, _, width = weight.shape
    if 2 * own != 128 or planes % 2 != 0:
        low = weight.astype(BF)
        sent = low[:, :3, :].reshape(own, 3, planes, spots, own).transpose(3, 0, 1, 2, 4)
        return sent.reshape(spots, own, 3 * planes * own), low.swapaxes(0, 1)
    return pl.pallas_call(
        pack,
        out_shape=[
            jax.ShapeDtypeStruct((spots, own, 3 * planes * own), BF),
            jax.ShapeDtypeStruct((4, own, width), BF),
        ],
        compiler_params=pltpu.CompilerParams(vmem_limit_bytes=48 * 2**20),
    )(weight)


def row_sums(shard_ref, first_ref, inner_ref, sums_ref):
    split = first_ref.shape[1]
    grad = shard_ref[...].astype(F32)
    first = jnp.sum(grad[:, :split] * first_ref[...].astype(F32), axis=1, keepdims=True)
    inner = jnp.sum(grad[:, split:] * inner_ref[...].astype(F32), axis=1, keepdims=True)
    squares = jnp.sum(grad * grad, axis=1, keepdims=True)
    lane = lax.broadcasted_iota(jnp.int32, sums_ref.shape, 1)
    sums_ref[...] = jnp.where(lane == 0, first, jnp.where(lane == 1, inner, squares))


def run_row_sums(shard, first, inner):
    if first.shape[1] % 128 != 0 or inner.shape[1] % 128 != 0:
        grad = shard.astype(F32)
        split = first.shape[1]
        parts = [grad[:, :split] * first.astype(F32), grad[:, split:] * inner.astype(F32), grad * grad]
        return [jnp.sum(part, axis=1) for part in parts]
    sums = pl.pallas_call(
        row_sums,
        out_shape=jax.ShapeDtypeStruct((shard.shape[0], 128), F32),
        compiler_params=pltpu.CompilerParams(vmem_limit_bytes=48 * 2**20),
    )(shard, first, inner)
    return [sums[:, column] for column in range(3)]


def settle(got_ref, out_ref, grad_ref):
    spots, own, packed = got_ref.shape
    planes = packed // (3 * own)
    low_half = lax.broadcasted_iota(jnp.int32, (own, 2 * own), 1) < own
    for pair in range(0, spots, 2):
        for kind in range(3):
            for plane in range(0, planes, 2):
                at = pl.ds((kind * planes + plane) * own, 2 * own)
                even = got_ref[pair, :, at].astype(F32)
                odd = got_ref[pair + 1, :, at].astype(F32)
                near = jnp.where(low_half, even, pltpu.roll(odd, own, 1))
                far = jnp.where(low_half, pltpu.roll(even, own, 1), odd)
                for step, grad in enumerate((near, far)):
                    grad_ref[kind, :, pl.ds(((plane + step) * spots + pair) * own, 2 * own)] = grad.astype(BF)
    grad_ref[3, :, :] = out_ref[...]


def run_settle(got, shard_out):
    spots, own, packed = got.shape
    width = shard_out.shape[1]
    planes = packed // (3 * own)
    if 2 * own != 128 or planes % 2 != 0:
        grad = got.reshape(spots, own, 3, planes, own).transpose(2, 1, 3, 0, 4).reshape(3, own, width)
        return jnp.concatenate([grad, shard_out[None]], axis=0)
    return pl.pallas_call(
        settle,
        out_shape=jax.ShapeDtypeStruct((4, own, width), BF),
        compiler_params=pltpu.CompilerParams(vmem_limit_bytes=48 * 2**20),
    )(got, shard_out)


def column_blocks(width, first, second):
    size = width // (first * second)
    for i in range(first):
        for j in range(second):
            yield pl.ds((i * second + j) * size, size), pl.ds((j * first + i) * size, size)


def enter_glu(order, mix_ref, x_ref, gain_ref, after_ref, n2_ref, mid_ref, home_ref):
    width = x_ref.shape[1]
    squares = jnp.sum(mix_ref[:, width:].astype(F32), axis=1, keepdims=True)
    home = lax.rsqrt(squares / width + EPS_NORM)
    after = x_ref[...].astype(F32) + mix_ref[:, :width].astype(F32) * home
    mid = lax.rsqrt(jnp.mean(after * after, axis=1, keepdims=True) + EPS_NORM)
    after_ref[...] = after
    mid_ref[...] = mid
    home_ref[...] = home
    n2 = (after * mid * gain_ref[...]).astype(BF)
    for source, target in column_blocks(width, *order):
        n2_ref[:, target] = n2[:, source.start : source.start + source.size]


def leave_glu(
    order, d_n2_ref, cot_ref, after_ref, mid_ref, mix_ref, home_ref, gain_ref, d_mid_ref, out_ref, held_ref
):
    width = cot_ref.shape[1]
    mid, home = mid_ref[...], home_ref[...]
    for target, source in column_blocks(width, *order):
        held_ref[:, target] = d_n2_ref[:, source].astype(F32) * gain_ref[:, target]
    normed = after_ref[...] * mid
    grad = held_ref[...]
    inner = jnp.mean(grad * normed, axis=1, keepdims=True)
    d_mid = cot_ref[...].astype(F32) + mid * (grad - normed * inner)
    d_mid_ref[...] = d_mid
    low = d_mid.astype(BF)
    out_ref[:, :width] = low
    mean = jnp.sum(low.astype(F32) * (mix_ref[:, :width].astype(F32) * home), axis=1, keepdims=True) / width
    lane = lax.broadcasted_iota(jnp.int32, (mid.shape[0], 128), 1)
    riders = jnp.zeros((mid.shape[0], 128), F32)
    for at, value in ((0, mean), (3, home)):
        for part in range(3):
            upper = value.astype(BF).astype(F32)
            riders = jnp.where(lane == at + part, upper, riders)
            value = value - upper
    out_ref[:, width:] = riders.astype(BF)


def run_enter(mix_raw, tokens, gain, order):
    rows, width = tokens.shape
    if width // (order[0] * order[1]) % 128 != 0:
        squares = jnp.sum(mix_raw[:, width:].astype(F32), axis=1, keepdims=True)
        home = lax.rsqrt(squares / width + EPS_NORM)
        after = tokens.astype(F32) + mix_raw[:, :width].astype(F32) * home
        normed, mid = normalize(after)
        n2 = (normed * gain).astype(BF).reshape(rows, *order, -1).swapaxes(1, 2)
        return after, n2.reshape(rows, width), mid, home
    column = jax.ShapeDtypeStruct((rows, 1), F32)
    return pl.pallas_call(
        functools.partial(enter_glu, order),
        out_shape=[
            jax.ShapeDtypeStruct((rows, width), F32),
            jax.ShapeDtypeStruct((rows, width), BF),
            column,
            column,
        ],
        compiler_params=pltpu.CompilerParams(vmem_limit_bytes=48 * 2**20),
    )(mix_raw, tokens, gain)


def run_leave(d_n2, cot, after, mid, mix_raw, home, gain, order):
    rows, width = cot.shape
    if width // (order[0] * order[1]) % 128 != 0:
        grad = d_n2.reshape(rows, order[1], order[0], -1).swapaxes(1, 2).reshape(rows, width)
        d_mid = cot.astype(F32) + norm_back(grad.astype(F32) * gain, after * mid, mid)
        low = d_mid.astype(BF)
        mix = mix_raw[:, :width].astype(F32) * home
        mean = jnp.sum(low.astype(F32) * mix, axis=1, keepdims=True) / width
        riders = jnp.concatenate(in_parts_of(mean) + in_parts_of(home), axis=1)
        riders = jnp.pad(riders, ((0, 0), (0, 128 - riders.shape[1])))
        return d_mid, jnp.concatenate([low, riders], axis=1)
    return pl.pallas_call(
        functools.partial(leave_glu, order),
        out_shape=[
            jax.ShapeDtypeStruct((rows, width), F32),
            jax.ShapeDtypeStruct((rows, width + 128), BF),
        ],
        scratch_shapes=[pltpu.VMEM((rows, width), F32)],
        compiler_params=pltpu.CompilerParams(vmem_limit_bytes=48 * 2**20),
    )(d_n2, cot, after, mid, mix_raw, home, gain)


def shards(
    tokens,
    cotangent,
    lengths,
    lower_bound,
    mixer_w,
    mlp_in,
    mlp_down,
    gains,
    mixer_m,
    mixer_v,
    in_m,
    in_v,
    down_m,
    down_v,
    gain_m,
    gain_v,
):
    rows, width = tokens.shape
    own, _, hidden_width = mlp_in.shape
    down_rows = mlp_down.shape[0]
    planes = lax.axis_size("z")
    spots = lax.axis_size(PLANE)
    quads = lax.axis_size(QUAD)
    pairs = lax.axis_size("c")
    group = spots * rows
    spot = lax.axis_index(PLANE)
    chans = planes * own

    ends = jnp.cumsum(lengths)
    starts = ends - lengths
    places = jnp.arange(group, dtype=jnp.int32)
    started = jnp.any(places[:, None] == starts[None, :], axis=-1, keepdims=True).astype(F32)
    home = spot * rows + jnp.arange(rows, dtype=jnp.int32)
    valid = (home < ends[-1]).astype(F32)

    cot_low = (cotangent.astype(F32) * valid[:, None]).astype(BF)

    w_out = gather(mixer_w[:, 3, :].astype(BF), "z")
    sent, low_mixer = run_pack(mixer_w, planes, spots)
    part = exchange(sent, PLANE).reshape(spots * own, 3 * chans)
    low_in = mlp_in.astype(BF)
    inner = quads * down_rows
    sent_in = low_in.reshape(own, 2, planes, quads, pairs, down_rows).transpose(2, 4, 0, 1, 3, 5)
    sent_in = sent_in.reshape(planes * pairs, own, 2 * inner)
    part, w_out, x_low, low_gains, low_down, sent_in = tied(
        part, w_out, tokens, gains, mlp_down, sent_in
    )
    x_parts = quad_parts(x_low, 1)
    full_gains = double_gather(low_gains).swapaxes(0, 1).reshape(3, width)
    w_down = quad_whole(quad_parts(low_down.astype(BF), 0))
    w_proj = gather(part, "z")
    x_all = core_gather(x_parts)

    bound = lower_bound.reshape(planes, spots, own)
    gap = (1.0 - lax.dynamic_index_in_dim(bound, spot, 1, False)).reshape(1, chans)
    gain_mid = full_gains[1].reshape(planes, spots, own)
    gain_mid = lax.dynamic_index_in_dim(gain_mid, spot, 1, False).reshape(1, chans)

    x = tokens.astype(F32)
    x_normed, x_factor = normalize(x)
    n1 = (normalize(x_all.astype(F32))[0] * full_gains[0]).astype(BF)
    blocks_in = core_exchange(sent_in)
    w_proj, w_down, n1, blocks_in, held_cot = tied(w_proj, w_down, n1, blocks_in, cot_low)
    cots = direct_gather(held_cot, "z")
    proj = jnp.dot(n1, w_proj, preferred_element_type=F32)
    proj, blocks_in = tied(proj, blocks_in)
    part_in = line_exchange(blocks_in)
    state, squares = run_forward(proj, started, gap)
    gate_proj = proj[:, 2 * chans :]
    gate_act = silu(gate_proj)
    raw = (state * gain_mid * gate_act).astype(BF)
    lane = jnp.arange(128, dtype=jnp.int32)[None, :]
    upper = squares.astype(BF).astype(F32)
    riders = jnp.where(lane == spot, upper, jnp.where(lane == spots + spot, squares - upper, 0.0))
    raw = jnp.concatenate([raw, riders.astype(BF)], axis=1)
    ride = jnp.pad(jnp.eye(128, dtype=BF), ((chans, 0), (width, 0)))
    w_ride = ride + jnp.pad(w_out, ((0, 128), (0, 128)))
    mix_part = jnp.dot(raw, w_ride, preferred_element_type=F32).astype(BF)
    mix_part, cots[1], cots[-1] = tied(mix_part, cots[1], cots[-1])
    in_halves = quad_halves(part_in.reshape(planes * pairs * own, 2 * inner), 0)
    mix_raw, *cots = tied(scatter(mix_part, PLANE), *cots)
    cot_all = ring_gather(in_order(cots, "z"), "c").swapaxes(0, 1)
    cot_all = cot_all.reshape(planes * pairs * rows, width)

    order, gain_glu = (planes, quads), full_gains[2].reshape(1, width)
    after_mix, n2_home, mid_factor, home_factor = run_enter(mix_raw, tokens, gain_glu, order)
    n2_home, *in_halves = tied(n2_home, *in_halves)
    n2 = gather(n2_home, LINE)
    w_in = quad_whole(quad_others(*in_halves))
    gate_up = jnp.dot(n2, w_in, preferred_element_type=F32)
    gate, up_value = gate_up[:, :inner], gate_up[:, inner:]
    silu_gate = silu(gate)
    hidden = (silu_gate * up_value).astype(BF)

    d_hidden = lax.dot_general(cot_all, w_down, (((1,), (1,)), ((), ())), preferred_element_type=F32)
    d_gate = d_hidden * up_value * silu_grad(gate)
    d_up = d_hidden * silu_gate
    d_gate_up = jnp.concatenate([d_gate.astype(BF), d_up.astype(BF)], axis=1)
    d_n2 = lax.dot_general(d_gate_up, w_in, (((1,), (1,)), ((), ())), preferred_element_type=F32)
    d_n2 = scatter(d_n2.astype(BF), LINE)
    grad_in = lax.dot_general(n2, d_gate_up, (((0,), (0,)), ((), ())), preferred_element_type=F32)
    grad_in = grad_in.astype(BF)
    down = jnp.dot(hidden, w_down, preferred_element_type=F32).astype(BF)
    sums_in = quad_sums(grad_in)
    down, held_hidden = tied(added(core_terms(down)).astype(BF), hidden)
    grad_down = lax.dot_general(
        held_hidden, cot_all, (((0,), (0,)), ((), ())), preferred_element_type=F32
    ).astype(BF)
    d_n2, grad_down, down, *sums_in = tied(d_n2, grad_down, down, *sums_in)
    d_mid, d_mix_home = run_leave(
        d_n2, cot_low, after_mix, mid_factor, mix_raw, home_factor, gain_glu, order
    )
    down = direct_scatter(down, "z")
    shard_in = quad_rest(*sums_in).astype(BF)
    d_mix = gather(d_mix_home, PLANE)
    d_mix, shard_in, grad_down, down = tied(d_mix, shard_in, grad_down, down)
    block_out = (after_mix + down).astype(BF)
    shard_down = scatter(grad_down, QUAD).astype(F32)
    got_in = exchange(shard_in.reshape(planes * pairs, own, 2 * inner), LINE)

    d_mixed = lax.dot_general(
        d_mix, w_ride[:chans], (((1,), (1,)), ((), ())), preferred_element_type=F32
    )
    d_proj, mixed_in = run_backward(proj, state, d_mixed, d_mix[:, width:], started, gap, gain_mid)
    grad_out = lax.dot_general(mixed_in, d_mix, (((0,), (0,)), ((), ())), preferred_element_type=F32)
    grad_proj = lax.dot_general(n1, d_proj, (((0,), (0,)), ((), ())), preferred_element_type=F32)
    grad_out = grad_out[:, :width].astype(BF).reshape(planes, spots * own, chans)
    grad_all = jnp.concatenate(
        [grad_proj.astype(BF).reshape(planes, spots * own, 3 * chans), grad_out], axis=2
    )
    grad_all, got_in, held_proj = tied(grad_all, got_in, d_proj)
    shard_all = scatter(grad_all.reshape(planes * spots * own, 4 * chans), "z")
    shard_in = got_in.reshape(planes, pairs, own, 2, quads, down_rows).transpose(3, 2, 0, 4, 1, 5)
    shard_in = shard_in.reshape(2, own, hidden_width)
    wide_in = shard_in.astype(F32)
    gain_in = jnp.sum(wide_in * low_in.swapaxes(0, 1).astype(F32), axis=(0, 2))
    total_early = jnp.sum(wide_in * wide_in) + jnp.sum(shard_down * shard_down)
    d_n1 = lax.dot_general(held_proj, w_proj, (((1,), (1,)), ((), ())), preferred_element_type=F32)
    d_n1 = plane_scatter(d_n1.astype(BF))
    input_grad = d_mid + norm_back(d_n1 * full_gains[0], x_normed, x_factor)
    plane_rows = spots * own
    first_row = lax.axis_index("z") * plane_rows
    rows_first = lax.dynamic_slice_in_dim(w_proj, first_row, plane_rows)
    rows_inner = low_mixer[3].reshape(plane_rows, chans)
    shard_all, shard_in, shard_down, gain_in, total_early, input_grad, rows_first, rows_inner, block_out = tied(
        shard_all, shard_in, shard_down, gain_in, total_early, input_grad, rows_first, rows_inner, block_out
    )
    shard_proj = shard_all[:, : 3 * chans]
    got_proj = exchange(shard_proj.reshape(spots, own, 3 * chans), PLANE)
    shard_out = shard_all[:, 3 * chans :].reshape(own, width)

    row_first, row_inner, row_squares = run_row_sums(shard_all, rows_first, rows_inner)
    gain_inner = jnp.sum(row_inner.reshape(own, spots), axis=1) / gains[1]
    gain_in = gain_in / gains[2]
    local_total = jnp.sum(row_squares) + total_early
    local_total += jnp.sum(gain_inner * gain_inner) + jnp.sum(gain_in * gain_in)
    sums = jnp.concatenate(
        [row_first.reshape(spots, own), jnp.full((1, own), local_total)], axis=0
    )
    sums = total_of(sums, ("c", "x", "y"))
    gain_rows = lax.dynamic_slice_in_dim(full_gains[0], first_row, plane_rows).reshape(spots, own)
    gain_first = sums[:spots] / gain_rows
    total = sums[spots:, :1] + jnp.sum(gain_first * gain_first)
    grad_norm = jnp.sqrt(total_of(total, ("z",))[0, 0])
    gain_first = lax.dynamic_index_in_dim(gain_first, spot, 0, False)
    shard_gains = jnp.stack([gain_first, gain_inner, gain_in])
    clip = jnp.minimum(1.0, CLIP_NORM / (grad_norm + 1e-06))
    shard_mixer = run_settle(got_proj, shard_out)
    new_mixer, new_mixer_m, new_mixer_v = run_adam(mixer_w, mixer_m, mixer_v, shard_mixer, clip)
    new_in, new_in_m, new_in_v = run_adam(mlp_in, in_m, in_v, shard_in, clip)
    new_down, new_down_m, new_down_v = adam_step(
        mlp_down, down_m, down_v, clip * shard_down, RATE_MATRIX, DECAY_WEIGHT
    )
    new_gains, new_gain_m, new_gain_v = adam_step(
        gains, gain_m, gain_v, clip * shard_gains, RATE_GAIN, 0.0
    )
    return (
        block_out,
        input_grad,
        grad_norm,
        new_mixer,
        new_mixer_m,
        new_mixer_v,
        new_in,
        new_in_m,
        new_in_v,
        new_down,
        new_down_m,
        new_down_v,
        new_gains,
        new_gain_m,
        new_gain_v,
    )


def solution(mesh):
    planes, spots = mesh.shape["dp"], mesh.shape["seq"]
    side = math.isqrt(spots // 2)
    split = Mesh(mesh.devices.reshape(planes, spots // (2 * side), side, 2), ALL)
    rows2, rows3, cols = P(ALL, None), P(ALL, None, None), P(None, ALL)
    return jax.shard_map(
        shards,
        mesh=split,
        in_specs=(rows2, rows2, P("z"), P(), rows3, rows3, rows2, cols)
        + (rows3,) * 4
        + (rows2,) * 2
        + (cols,) * 2,
        out_specs=(rows2, rows2, P()) + (rows3,) * 6 + (rows2,) * 3 + (cols,) * 3,
        check_vma=False,
    )
```
